128 devices in a mesh: ta: 4 (over x), sa: 32 (over z, y, core).
Axes of the slice: x: 4, y: 4, z: 4, core: 2. Of those that a mesh axis runs over, the one named last changes fastest.
Arguments:
- start: float32 [8, 3, 32, 32, 32, 128], P('ta', None, 'sa'), parts along dimension 0, may hold values from -10 to 10
- links: float32 [12, 2, 3, 3, 32, 32, 32], P('ta', None, None, None, 'sa'), parts along dimension 0, may hold values from -1 to 1, as said below
- momenta: int32 [7, 3], replicated, may hold values from -2 to 2
- displace: int32 [3], replicated, may hold values from 0 to 2, each once
Outputs:
- basis: float32 [8, 3, 32, 32, 32, 128], P('ta', None, 'sa'), parts along dimension 0
- ritz: float32 [8, 128, 128], P('ta'), parts along dimension 0
- phi: float32 [128, 28, 3, 2, 128], P('sa', 'ta'), parts along dimension 1
The draws below stay inside these ranges and needn't reach their ends.
There are 4 independent parts, one for each index of `ta`. The reference program is written for one: setup_inputs(seed, part) draws one part's arguments, and reference() takes and returns one part's arrays. A program takes and returns all parts, laid end to end along the dimension named above; an argument that names none is the same for every part. Nothing has to cross between parts.
Inputs may be any that keep to these rules, and one draw needn't show every extreme that they name: `links`: each 3 x 3 complex matrix of one direction and site is special unitary. `displace`: names each of the three directions once.
All inputs are finite; a program needn't handle non-finite values.
Results may differ from the reference program's by a relative error of at most 0.0002.
Values sent between devices are 32-bit elements; how exact they have to be, the bound alone decides.
No kernel may reach another device: no remote copies, remote signals or barrier semaphores. Data moves between devices by JAX's collectives and lax.ppermute only.
A program may use at most 576 MiB of HBM per device.

```python
import math
import jax
import jax.numpy as jnp
from jax import lax

NX = 32
NY = 32
NEV = 128
NMOM = 7
NDISP = 3
DEG = 3
NS_ITERS = 3
NZ = 32


def rotation(angles, first, second):
    theta = angles[0]
    phase = angles[1]
    other = angles[2]
    ones = jnp.ones_like(theta)
    zeros = jnp.zeros_like(theta)
    real = [[ones if row == column else zeros for column in range(3)] for row in range(3)]
    imag = [[zeros for column in range(3)] for row in range(3)]
    cosine = jnp.cos(theta)
    sine = jnp.sin(theta)
    real[first][first] = cosine * jnp.cos(phase)
    imag[first][first] = cosine * jnp.sin(phase)
    real[first][second] = sine * jnp.cos(other)
    imag[first][second] = sine * jnp.sin(other)
    real[second][first] = -sine * jnp.cos(other)
    imag[second][first] = sine * jnp.sin(other)
    real[second][second] = cosine * jnp.cos(phase)
    imag[second][second] = -cosine * jnp.sin(phase)
    return jnp.stack([jnp.stack([jnp.stack(line) for line in real]), jnp.stack([jnp.stack(line) for line in imag])])


def multiply(left, right):
    real = jnp.sum(left[0][:, :, None] * right[0][None], axis=1) - jnp.sum(left[1][:, :, None] * right[1][None], axis=1)
    imag = jnp.sum(left[0][:, :, None] * right[1][None], axis=1) + jnp.sum(left[1][:, :, None] * right[0][None], axis=1)
    return jnp.stack([real, imag])


def draw_links(key, part):
    key = jax.random.fold_in(key, 11)
    first_key, second_key = jax.random.split(key)
    theta = jax.random.uniform(first_key, (3, 3, 1, NZ, NY, NX), jnp.float32, 0.0, 0.5 * math.pi)
    phases = jax.random.uniform(second_key, (3, 3, 2, NZ, NY, NX), jnp.float32, -math.pi, math.pi)
    angles = jnp.concatenate([theta, phases], axis=2)
    result = []
    for direction in range(3):
        matrix = rotation(angles[direction, 0], 0, 1)
        matrix = multiply(matrix, rotation(angles[direction, 1], 1, 2))
        matrix = multiply(matrix, rotation(angles[direction, 2], 0, 2))
        result.append(matrix)
    return jnp.stack(result).astype(jnp.float32)


def column_amplitude(key, lowest, highest):
    return jnp.exp(jax.random.uniform(key, (NEV,), jnp.float32, math.log(lowest), math.log(highest)))


def draw_start(key, part):
    key = jax.random.fold_in(key, 5)
    shape = (2, 3, NZ, NY, NX, NEV)
    position = jnp.arange(NZ, dtype=jnp.float32) / max(NZ - 1, 1)
    first_key = jax.random.fold_in(key, 0)
    third_key = jax.random.fold_in(key, 2)
    height = (0.3 + 1.5 * position).reshape(1, 1, NZ, 1, 1, 1)
    column_scale = column_amplitude(third_key, 1e-06, 0.01)
    return (jnp.clip(jax.random.normal(first_key, shape, jnp.float32), -4.0, 4.0) * column_scale * height).astype(jnp.float32)


def with_ends(values, rng, least, high):
    dims = values.shape
    spot = [jax.random.randint(jax.random.fold_in(rng, axis), (), 0, dims[axis]) for axis in range(len(dims))]
    values = values.at[tuple(spot)].set(least)
    longest = dims.index(max(dims))
    spot[longest] = (spot[longest] + 1) % dims[longest]
    return values.at[tuple(spot)].set(high)


def setup_inputs(seed: int = 0, part: int = 0) -> dict:
    seeds = jax.random.split(jax.random.key(seed), 5)
    own_keys = jax.random.split(jax.random.fold_in(seeds[4], part), 5)
    start = draw_start(jax.random.fold_in(jax.random.fold_in(seeds[4], part), 71), part)
    links = draw_links(jax.random.fold_in(jax.random.fold_in(seeds[4], part), 71), part)
    momenta = with_ends(jax.random.randint(seeds[2], (NMOM, 3), -2, 3), jax.random.fold_in(seeds[2], 1), -2, 2).astype(jnp.int32)
    displace = jax.random.permutation(seeds[3], NDISP).astype(jnp.int32)
    return {"start": start, "links": links, "momenta": momenta, "displace": displace}


highest = lax.Precision.HIGHEST
ALPHA = 2.0 / 11.0
BETA = 13.0 / 11.0
EPS = 1e-06
TWO_PI = 2.0 * math.pi

def product(matrix, vector):
    form = 'abzyx,bzyxn->azyxn'
    real_real = jnp.einsum(form, matrix[0], vector[0], precision=highest)
    imag_imag = jnp.einsum(form, matrix[1], vector[1], precision=highest)
    real_imag = jnp.einsum(form, matrix[0], vector[1], precision=highest)
    imag_real = jnp.einsum(form, matrix[1], vector[0], precision=highest)
    return jnp.stack([real_real - imag_imag, real_imag + imag_real])

def adjoint(matrix, vector):
    form = 'bazyx,bzyxn->azyxn'
    real_real = jnp.einsum(form, matrix[0], vector[0], precision=highest)
    imag_imag = jnp.einsum(form, matrix[1], vector[1], precision=highest)
    real_imag = jnp.einsum(form, matrix[0], vector[1], precision=highest)
    imag_real = jnp.einsum(form, matrix[1], vector[0], precision=highest)
    return jnp.stack([real_real + imag_imag, real_imag - imag_real])

def laplace(field, links, below_links, above, below):
    total = 6.0 * field
    total = total - product(links[0], jnp.roll(field, -1, 4)) - adjoint(jnp.roll(links[0], 1, 5), jnp.roll(field, 1, 4))
    total = total - product(links[1], jnp.roll(field, -1, 3)) - adjoint(jnp.roll(links[1], 1, 4), jnp.roll(field, 1, 3))
    total = total - product(links[2], above) - adjoint(below_links, below)
    return total

def complex_product(left, right):
    first = jnp.dot(left[0], right[0], precision=highest) - jnp.dot(left[1], right[1], precision=highest)
    second = jnp.dot(left[0], right[1], precision=highest) + jnp.dot(left[1], right[0], precision=highest)
    return (first, second)

def crossed(first, second):
    return lax.dot_general(first, second, (((0,), (0,)), ((), ())), precision=highest, preferred_element_type=jnp.float32)

def reference(start, links, momenta, displace):
    count = 6.0 * NX * NY * NZ
    below_links = jnp.roll(links[2], 1, 3)

    def apply(field):
        return laplace(field, links, below_links, jnp.roll(field, -1, 2), jnp.roll(field, 1, 2))
    current = start
    image = apply(current)
    previous = start
    for step in range(DEG):
        if step == 0:
            fresh = ALPHA * image - BETA * current
        else:
            fresh = 2.0 * (ALPHA * image - BETA * current) - previous
        scale = lax.rsqrt(lax.optimization_barrier(jnp.sum(fresh * fresh, axis=(0, 1, 2, 3, 4))) / count + EPS)
        previous = scale * current
        current = scale * fresh
        image = apply(current)
    flat = current.reshape(2, -1, NEV)
    flat_image = image.reshape(2, -1, NEV)
    gram_real = crossed(flat[0], flat[0]) + crossed(flat[1], flat[1])
    gram_imag = crossed(flat[0], flat[1]) - crossed(flat[1], flat[0])
    hmat_real = crossed(flat[0], flat_image[0]) + crossed(flat[1], flat_image[1])
    hmat_imag = crossed(flat[0], flat_image[1]) - crossed(flat[1], flat_image[0])
    identity = jnp.eye(NEV, dtype=jnp.float32)
    iterate = (gram_real / count, gram_imag / count)
    inverse = (identity, jnp.zeros((NEV, NEV), jnp.float32))
    for step in range(NS_ITERS):
        middle = complex_product(inverse, iterate)
        factor = (1.5 * identity - 0.5 * middle[0], -0.5 * middle[1])
        iterate = complex_product(iterate, factor)
        inverse = complex_product(factor, inverse)
    basis_pair = complex_product((flat[0], flat[1]), inverse)
    basis = jnp.stack(basis_pair).reshape(current.shape)
    halfway = complex_product((hmat_real, hmat_imag), inverse)
    ritz_pair = complex_product((inverse[0].T, -inverse[1].T), halfway)
    ritz = jnp.stack(ritz_pair) / count
    shifted = [jnp.roll(basis, -1, 4), jnp.roll(basis, -1, 3), jnp.roll(basis, -1, 2)]
    carried = [product(links[k], shifted[k]) for k in range(3)]
    chosen = []
    for slot in range(NDISP):
        total = jnp.zeros_like(basis)
        for k in range(3):
            total = total + (displace[slot] == k).astype(jnp.float32) * carried[k]
        chosen.append(total)
    right = jnp.stack(chosen).reshape(NDISP, 2, -1, NEV)
    xs = jnp.arange(NX, dtype=jnp.int32)[None, None, None, :]
    ys = jnp.arange(NY, dtype=jnp.int32)[None, None, :, None]
    zs = jnp.arange(NZ, dtype=jnp.int32)[None, :, None, None]
    along_x = momenta[:, 0][:, None, None, None]
    along_y = momenta[:, 1][:, None, None, None]
    along_z = momenta[:, 2][:, None, None, None]
    angles = TWO_PI * ((along_x * xs % NX).astype(jnp.float32) / NX + (along_y * ys % NY).astype(jnp.float32) / NY + (along_z * zs % NZ).astype(jnp.float32) / NZ)
    factor_norm = 1.0 / math.sqrt(NX * NY * NZ)

    def single(angle):
        cosine = jnp.cos(angle)[None, :, :, :, None]
        sine = jnp.sin(angle)[None, :, :, :, None]
        left_real = (basis[0] * cosine - basis[1] * sine).reshape(-1, NEV)
        left_imag = (-(basis[0] * sine + basis[1] * cosine)).reshape(-1, NEV)
        form = 'ki,dkj->dij'
        real = jnp.einsum(form, left_real, right[:, 0], precision=highest) - jnp.einsum(form, left_imag, right[:, 1], precision=highest)
        imag = jnp.einsum(form, left_real, right[:, 1], precision=highest) + jnp.einsum(form, left_imag, right[:, 0], precision=highest)
        return jnp.stack([real, imag], axis=1)
    every = lax.map(single, angles)
    phi = jnp.transpose(every, (3, 0, 1, 2, 4)) * factor_norm
    return (basis, ritz, phi)
```

```python
import math

import jax
import jax.numpy as jnp
from jax import lax
from jax.experimental import pallas as pl
from jax.experimental.pallas import tpu as pltpu
from jax.sharding import PartitionSpec as P

NMOM = 7
ALPHA = 2.0 / 11.0
BETA = 13.0 / 11.0
EPS = 1e-06
TWO_PI = 2.0 * math.pi
RANGE = 2.0**40
COUNT = 196608.0
HIGHEST = lax.Precision.HIGHEST
F32 = jnp.float32
BF16 = jnp.bfloat16
VMEM_LIMIT = 56 * 1024 * 1024


def params(**extra):
    return pltpu.CompilerParams(vmem_limit_bytes=VMEM_LIMIT, **extra)


def link_of(rows, direction):
    def entry(part, a, b):
        lane = ((direction * 2 + part) * 3 + a) * 3 + b
        return jnp.broadcast_to(rows[:, lane : lane + 1], rows.shape)

    real = [[entry(0, a, b) for b in range(3)] for a in range(2)]
    imag = [[entry(1, a, b) for b in range(3)] for a in range(2)]
    third_real, third_imag = [], []
    for b in range(3):
        p, q = (b + 1) % 3, (b + 2) % 3
        first = real[0][p] * real[1][q] - imag[0][p] * imag[1][q]
        second = real[0][q] * real[1][p] - imag[0][q] * imag[1][p]
        third_real.append(first - second)
        first = real[0][p] * imag[1][q] + imag[0][p] * real[1][q]
        second = real[0][q] * imag[1][p] + imag[0][q] * real[1][p]
        third_imag.append(second - first)
    return [real + [third_real], imag + [third_imag]]


def forward(link, v):
    real, imag = [], []
    for a in range(3):
        r = i = None
        for b in range(3):
            x = link[0][a][b] * v[b] - link[1][a][b] * v[3 + b]
            y = link[0][a][b] * v[3 + b] + link[1][a][b] * v[b]
            r = x if r is None else r + x
            i = y if i is None else i + y
        real.append(r)
        imag.append(i)
    return real + imag


def backward(link, v):
    real, imag = [], []
    for a in range(3):
        r = i = None
        for b in range(3):
            x = link[0][b][a] * v[b] + link[1][b][a] * v[3 + b]
            y = link[0][b][a] * v[3 + b] - link[1][b][a] * v[b]
            r = x if r is None else r + x
            i = y if i is None else i + y
        real.append(r)
        imag.append(i)
    return real + imag


def add(first, second):
    return [a + b for a, b in zip(first, second)]


def cell(ref, c, at, z=0):
    return ref[z, c * 128 + at.start : c * 128 + at.stop, :]


def cell_flat(ref, c, at):
    return ref[c * 128 + at.start : c * 128 + at.stop, :]


def interior(u, links, before, c0, c1, cp, name):
    first = links is None

    def kernel(*refs):
        if first:
            here, above, out, norm, link_ref, px, wx, py, pz = refs
            rows = jnp.concatenate([here[0, 768:840, :], jnp.zeros((56, 128), F32)], axis=0)
            link_ref[0] = rows.T
        else:
            here, above, link_ref, before_ref, out, norm, px, wx, py, pz = refs
        z = pl.program_id(0)
        inside = jnp.where(z < 7, 1.0, 0.0).astype(F32)

        @pl.when(z == 0)
        def _():
            norm[...] = jnp.zeros_like(norm)
            pz[...] = jnp.zeros_like(pz)

        total = jnp.zeros((8, 128), F32)
        for y in range(4):
            row = y * 32
            for c in range(6):
                px[c] = pltpu.roll(cell(here, c, slice(row, row + 32)), 31, 0)
            for g in range(4):
                at = slice(row + 8 * g, row + 8 * g + 8)
                own = slice(8 * g, 8 * g + 8)
                rows = link_ref[0, at, :]
                v = [cell(here, c, at) for c in range(6)]
                if not first:
                    for c in range(6):
                        total = total + v[c] * v[c]
                link = link_of(rows, 0)
                hop = forward(link, [px[c, own, :] for c in range(6)])
                side = backward(link, v)
                for c in range(6):
                    wx[c, own, :] = side[c]
                if y < 3:
                    link = link_of(rows, 1)
                    up = slice(at.start + 32, at.stop + 32)
                    hop = add(hop, forward(link, [cell(here, c, up) for c in range(6)]))
                    side = backward(link, v)
                if y > 0:
                    hop = add(hop, [py[c, own, :] for c in range(6)])
                if y < 3:
                    for c in range(6):
                        py[c, own, :] = side[c]
                link = link_of(rows, 2)
                far = forward(link, [cell(above, c, at) for c in range(6)])
                hop = [a + inside * b for a, b in zip(hop, far)]
                hop = add(hop, [pz[c, at, :] for c in range(6)])
                side = backward(link, v)
                for c in range(6):
                    pz[c, at, :] = side[c]
                    value = c0 * v[c] - c1 * hop[c]
                    if not first:
                        value = value - cp * cell(before_ref, c, at)
                    out[0, c * 128 + at.start : c * 128 + at.stop, :] = value
            for c in range(6):
                spot = slice(c * 128 + row, c * 128 + row + 32)
                out[0, spot, :] = out[0, spot, :] - c1 * pltpu.roll(wx[c], 1, 0)
        norm[...] = norm[...] + total

    block = pl.BlockSpec((1, 768, 128), lambda z: (z, 0, 0))
    next_block = pl.BlockSpec((1, 768, 128), lambda z: (jnp.minimum(z + 1, 7), 0, 0))
    link_block = pl.BlockSpec((1, 128, 128), lambda z: (z, 0, 0))
    out_specs = [block, pl.BlockSpec((8, 128), lambda z: (0, 0))]
    out_shape = [jax.ShapeDtypeStruct((8, 768, 128), F32), jax.ShapeDtypeStruct((8, 128), F32)]
    if first:
        in_specs = [pl.BlockSpec((1, 840, 128), lambda z: (z, 0, 0)), next_block]
        operands = [u, u]
        out_specs.append(link_block)
        out_shape.append(jax.ShapeDtypeStruct((8, 128, 128), F32))
    else:
        in_specs = [block, next_block, link_block, block]
        operands = [u, u, links, before]
    return pl.pallas_call(
        kernel,
        grid=(8,),
        in_specs=in_specs,
        out_specs=out_specs,
        out_shape=out_shape,
        scratch_shapes=[
            pltpu.VMEM((6, 32, 128), F32),
            pltpu.VMEM((6, 32, 128), F32),
            pltpu.VMEM((6, 32, 128), F32),
            pltpu.VMEM((6, 128, 128), F32),
        ],
        compiler_params=params(),
        cost_estimate=pl.CostEstimate(flops=12_000_000_000, bytes_accessed=12_000_000, transcendentals=0),
        name=name,
    )(*operands)


def boundary(partial, links, halo, z_links, c1, name):
    z_up, z_down, y_up, y_down = halo

    def kernel(part, link_ref, zu, zd, yu, yd, zl, out, y_low, y_high, z_low, z_high, turned):
        step = pl.program_id(0)

        def put(z, c, at, hop):
            spot = slice(c * 128 + at.start, c * 128 + at.stop)
            out[z, spot, :] = part[z, spot, :] - c1 * hop[c]

        def more(z, c, at, hop):
            spot = slice(c * 128 + at.start, c * 128 + at.stop)
            out[z, spot, :] = out[z, spot, :] - c1 * hop[c]

        for z in range(2):
            for g in range(4):
                own = slice(8 * g, 8 * g + 8)
                hop = backward(link_of(link_ref[z, own, :], 3), [yd[z, c, own, :] for c in range(6)])
                for c in range(6):
                    put(z, c, own, hop)
                at = slice(96 + 8 * g, 104 + 8 * g)
                hop = forward(link_of(link_ref[z, at, :], 1), [yu[z, c, own, :] for c in range(6)])
                for c in range(6):
                    put(z, c, at, hop)
            for c in range(6):
                spot = slice(c * 128 + 32, c * 128 + 96)
                out[z, spot, :] = part[z, spot, :]

        @pl.when(step == 0)
        def _():
            turned[...] = jnp.concatenate([zl[...], jnp.zeros((56, 128), F32)], axis=0).T
            for g in range(16):
                at = slice(8 * g, 8 * g + 8)
                hop = backward(link_of(turned[at, :], 2), [zd[c * 128 + at.start : c * 128 + at.stop, :] for c in range(6)])
                for c in range(6):
                    more(0, c, at, hop)
            z_low[...] = out[0]

        @pl.when(step == 3)
        def _():
            for g in range(16):
                at = slice(8 * g, 8 * g + 8)
                hop = forward(
                    link_of(link_ref[1, at, :], 2), [zu[c * 128 + at.start : c * 128 + at.stop, :] for c in range(6)]
                )
                for c in range(6):
                    more(1, c, at, hop)
            z_high[...] = out[1]

        for z in range(2):
            for c in range(6):
                y_low[z, c] = out[z, c * 128 : c * 128 + 32, :]
                y_high[z, c] = out[z, c * 128 + 96 : c * 128 + 128, :]

    block = pl.BlockSpec((2, 768, 128), lambda z: (z, 0, 0))
    y_face = pl.BlockSpec((2, 6, 32, 128), lambda z: (z, 0, 0, 0))
    z_face = pl.BlockSpec((768, 128), lambda z: (0, 0))
    return pl.pallas_call(
        kernel,
        grid=(4,),
        in_specs=[
            block,
            pl.BlockSpec((2, 128, 128), lambda z: (z, 0, 0)),
            z_face,
            z_face,
            y_face,
            y_face,
            pl.BlockSpec((72, 128), lambda z: (0, 0)),
        ],
        out_specs=(block, y_face, y_face, z_face, z_face),
        out_shape=(
            jax.ShapeDtypeStruct((8, 768, 128), F32),
            jax.ShapeDtypeStruct((8, 6, 32, 128), F32),
            jax.ShapeDtypeStruct((8, 6, 32, 128), F32),
            jax.ShapeDtypeStruct((768, 128), F32),
            jax.ShapeDtypeStruct((768, 128), F32),
        ),
        scratch_shapes=[pltpu.VMEM((128, 128), F32)],
        compiler_params=params(),
        cost_estimate=pl.CostEstimate(flops=6_000_000_000, bytes_accessed=9_000_000, transcendentals=0),
        name=name,
    )(partial, links, z_up, z_down, y_up, y_down, z_links)


def halves(value):
    high = value.astype(BF16)
    return high, (value - high.astype(F32)).astype(BF16)


def dot3(left, right):
    def dot(a, b):
        return jnp.dot(a, b, preferred_element_type=F32)

    return dot(left[0], right[0]) + (dot(left[0], right[1]) + dot(left[1], right[0]))


def transposed(ref, z, part):
    return jnp.concatenate([cell(ref, 3 * part + a, slice(0, 128), z).T for a in range(3)], axis=1)


def gram(u, first_norm, second_norm):
    def kernel(here, n1, n2, packed, acc):
        step = pl.program_id(0)

        @pl.when(step == 0)
        def _():
            acc[...] = jnp.zeros_like(acc)

        left = jnp.concatenate(
            [jnp.concatenate([transposed(here, z, part) for z in range(2)], axis=1) for part in range(2)], axis=0
        )
        right = jnp.concatenate([here[z, 0:384, :] for z in range(2)], axis=0)
        right = jnp.concatenate([right, jnp.concatenate([here[z, 384:768, :] for z in range(2)], axis=0)], axis=1)
        acc[...] = acc[...] + dot3(halves(left), halves(right))

        @pl.when(step == 3)
        def _():
            real = acc[0:128, 0:128] + acc[128:256, 128:256]
            imag = acc[0:128, 128:256] - acc[128:256, 0:128]
            row = lax.broadcasted_iota(jnp.int32, (128, 128), 0)
            column = lax.broadcasted_iota(jnp.int32, (128, 128), 1)
            packed[0:128, :] = jnp.where(column >= row, real, imag)
            packed[128:136, :] = n1[...]
            packed[136:144, :] = n2[...]

    fixed = pl.BlockSpec((8, 128), lambda z: (0, 0))
    return pl.pallas_call(
        kernel,
        grid=(4,),
        in_specs=[pl.BlockSpec((2, 768, 128), lambda z: (z, 0, 0)), fixed, fixed],
        out_specs=pl.BlockSpec((144, 128), lambda z: (0, 0)),
        out_shape=jax.ShapeDtypeStruct((144, 128), F32),
        scratch_shapes=[pltpu.VMEM((256, 256), F32)],
        compiler_params=params(),
        cost_estimate=pl.CostEstimate(flops=4_000_000_000, bytes_accessed=3_000_000, transcendentals=0),
        name="gram",
    )(u, first_norm, second_norm)


def put_halves(wide, carry, slots):
    for a in range(3):
        for k in range(slots):
            for part in range(2):
                hi, lo = halves(carry[k, 3 * part + a])
                spot = (k * 2 + part) * 128
                wide[0, a * 128 : (a + 1) * 128, spot : spot + 128] = hi
                wide[0, 384 + a * 128 : 512 + a * 128, spot : spot + 128] = lo
                wide[0, 768 + a * 128 : 896 + a * 128, spot : spot + 128] = hi


def add_hops(acc, here, carry, slots):
    left = jnp.concatenate([transposed(here, 0, part) for part in range(2)], axis=0)

    def summed(c):
        return carry[0, c] if slots == 1 else carry[0, c] + carry[1, c]

    right = jnp.concatenate(
        [jnp.concatenate([summed(a), summed(3 + a)], axis=1) for a in range(3)], axis=0
    )
    acc[...] = acc[...] + dot3(halves(left), halves(right))


def carry_x(u, links):
    def kernel(here, link_ref, wide, hops, px, carry, acc):
        z = pl.program_id(0)

        @pl.when(z == 0)
        def _():
            acc[...] = jnp.zeros_like(acc)

        for y in range(4):
            row = y * 32
            for c in range(6):
                px[c] = pltpu.roll(cell(here, c, slice(row, row + 32)), 31, 0)
            for g in range(4):
                at = slice(row + 8 * g, row + 8 * g + 8)
                own = slice(8 * g, 8 * g + 8)
                found = forward(link_of(link_ref[0, at, :], 0), [px[c, own, :] for c in range(6)])
                for c in range(6):
                    carry[0, c, at, :] = found[c]
        put_halves(wide, carry, 1)
        add_hops(acc, here, carry, 1)

        @pl.when(z == 7)
        def _():
            hops[...] = acc[...]

    block = pl.BlockSpec((1, 768, 128), lambda z: (z, 0, 0))
    return pl.pallas_call(
        kernel,
        grid=(8,),
        in_specs=[block, pl.BlockSpec((1, 128, 128), lambda z: (z, 0, 0))],
        out_specs=(pl.BlockSpec((1, 1152, 256), lambda z: (z, 0, 0)), pl.BlockSpec((256, 256), lambda z: (0, 0))),
        out_shape=(jax.ShapeDtypeStruct((8, 1152, 256), BF16), jax.ShapeDtypeStruct((256, 256), F32)),
        scratch_shapes=[
            pltpu.VMEM((6, 32, 128), F32),
            pltpu.VMEM((1, 6, 128, 128), F32),
            pltpu.VMEM((256, 256), F32),
        ],
        compiler_params=params(),
        cost_estimate=pl.CostEstimate(flops=7_000_000_000, bytes_accessed=8_000_000, transcendentals=0),
        name="carry_x",
    )(u, links)


def carry_yz(u, links, z_up, y_up, x_hops, packed_gram):
    def kernel(here, above, link_ref, zu, yu, hops_ref, gram_ref, wide, packed, carry, acc):
        z = pl.program_id(0)
        last = z == 7

        @pl.when(z == 0)
        def _():
            acc[...] = hops_ref[...]

        for y in range(4):
            row = y * 32
            for g in range(4):
                at = slice(row + 8 * g, row + 8 * g + 8)
                own = slice(8 * g, 8 * g + 8)
                rows = link_ref[0, at, :]
                if y < 3:
                    source = [cell(here, c, slice(at.start + 32, at.stop + 32)) for c in range(6)]
                else:
                    source = [yu[0, c, own, :] for c in range(6)]
                found = forward(link_of(rows, 1), source)
                for c in range(6):
                    carry[0, c, at, :] = found[c]
                source = [jnp.where(last, cell_flat(zu, c, at), cell(above, c, at)) for c in range(6)]
                found = forward(link_of(rows, 2), source)
                for c in range(6):
                    carry[1, c, at, :] = found[c]
        put_halves(wide, carry, 2)
        add_hops(acc, here, carry, 2)

        @pl.when(last)
        def _():
            gram_real, gram_imag = hermitian(gram_ref[0:128, :])
            hop_real = acc[0:128, 0:128] + acc[128:256, 128:256]
            hop_imag = acc[0:128, 128:256] - acc[128:256, 0:128]
            real = 6.0 * gram_real - (hop_real + hop_real.T)
            imag = 6.0 * gram_imag - (hop_imag - hop_imag.T)
            row = lax.broadcasted_iota(jnp.int32, (128, 128), 0)
            column = lax.broadcasted_iota(jnp.int32, (128, 128), 1)
            packed[...] = jnp.where(column >= row, real, imag)

    return pl.pallas_call(
        kernel,
        grid=(8,),
        in_specs=[
            pl.BlockSpec((1, 768, 128), lambda z: (z, 0, 0)),
            pl.BlockSpec((1, 768, 128), lambda z: (jnp.minimum(z + 1, 7), 0, 0)),
            pl.BlockSpec((1, 128, 128), lambda z: (z, 0, 0)),
            pl.BlockSpec((768, 128), lambda z: (0, 0)),
            pl.BlockSpec((1, 6, 32, 128), lambda z: (z, 0, 0, 0)),
            pl.BlockSpec((256, 256), lambda z: (0, 0)),
            pl.BlockSpec((144, 128), lambda z: (0, 0)),
        ],
        out_specs=(pl.BlockSpec((1, 1152, 512), lambda z: (z, 0, 0)), pl.BlockSpec((128, 128), lambda z: (0, 0))),
        out_shape=(jax.ShapeDtypeStruct((8, 1152, 512), BF16), jax.ShapeDtypeStruct((128, 128), F32)),
        scratch_shapes=[pltpu.VMEM((2, 6, 128, 128), F32), pltpu.VMEM((256, 256), F32)],
        compiler_params=params(),
        cost_estimate=pl.CostEstimate(flops=12_000_000_000, bytes_accessed=16_000_000, transcendentals=0),
        name="carry_yz",
    )(u, u, links, z_up, y_up, x_hops, packed_gram)


def elementals(z, u, right_x, right_yz, phases, first, count, name):
    def kernel(z_ref, here, rx, ryz, phase, out, left, acc):
        step = pl.program_id(0)

        @pl.when(step == 0)
        def _():
            acc[...] = jnp.zeros_like(acc)

        turned = [[here[zz, c * 128 : (c + 1) * 128, :].T for c in range(6)] for zz in range(2)]
        for m in range(count):
            mode = 2 * (first + m)
            for zz in range(2):
                cosine = phase[zz, mode : mode + 1, :]
                sine = phase[zz, mode + 1 : mode + 2, :]
                for a in range(3):
                    real, imag = turned[zz][a], turned[zz][3 + a]
                    spot = zz * 1152 + a * 128
                    pair = (real * cosine - imag * sine, -(real * sine + imag * cosine))
                    for part in range(2):
                        hi, lo = halves(pair[part])
                        rows = slice(m * 256 + part * 128, m * 256 + part * 128 + 128)
                        left[rows, spot : spot + 128] = hi
                        left[rows, spot + 384 : spot + 512] = hi
                        left[rows, spot + 768 : spot + 896] = lo
        found = jnp.dot(left[...], rx[...].reshape(2304, 256), preferred_element_type=F32)
        acc[:, 0:256] = acc[:, 0:256] + found
        found = jnp.dot(left[...], ryz[...].reshape(2304, 512), preferred_element_type=F32)
        acc[:, 256:768] = acc[:, 256:768] + found

        @pl.when(step == 3)
        def _():
            turn = halves(jnp.concatenate([z_ref[0].T, z_ref[1].T], axis=0))
            for m in range(count):
                real, imag = slice(m * 256, m * 256 + 128), slice(m * 256 + 128, m * 256 + 256)
                for k in range(3):
                    one, two = slice(256 * k, 256 * k + 128), slice(256 * k + 128, 256 * k + 256)
                    raw = [acc[real, one] - acc[imag, two], acc[real, two] + acc[imag, one]]
                    found = dot3(turn, halves(jnp.concatenate(raw, axis=1)))
                    top = found[0:128, 0:128] + found[128:256, 128:256]
                    bottom = found[0:128, 128:256] - found[128:256, 0:128]
                    place = (m * 3 + k) * 256
                    for core in range(2):
                        for chip in range(16):
                            row = chip * 8 + core * 4
                            out[core, chip, :, place : place + 128] = top[row : row + 4]
                            out[core, chip, :, place + 128 : place + 256] = bottom[row : row + 4]

    return pl.pallas_call(
        kernel,
        grid=(4,),
        in_specs=[
            pl.BlockSpec((2, 128, 128), lambda z: (0, 0, 0)),
            pl.BlockSpec((2, 768, 128), lambda z: (z, 0, 0)),
            pl.BlockSpec((2, 1152, 256), lambda z: (z, 0, 0)),
            pl.BlockSpec((2, 1152, 512), lambda z: (z, 0, 0)),
            pl.BlockSpec((2, 16, 128), lambda z: (z, 0, 0)),
        ],
        out_specs=pl.BlockSpec((2, 16, 4, count * 768), lambda z: (0, 0, 0, 0)),
        out_shape=jax.ShapeDtypeStruct((2, 16, 4, count * 768), F32),
        scratch_shapes=[
            pltpu.VMEM((count * 256, 2304), BF16),
            pltpu.VMEM((count * 256, 768), F32),
        ],
        compiler_params=params(),
        cost_estimate=pl.CostEstimate(flops=5_500_000_000 * count, bytes_accessed=16_000_000, transcendentals=0),
        name=name,
    )(z, u, right_x, right_yz, phases)


def hermitian(packed):
    row = lax.broadcasted_iota(jnp.int32, (128, 128), 0)
    column = lax.broadcasted_iota(jnp.int32, (128, 128), 1)
    diagonal = jnp.where(column == row, packed, 0.0)
    upper = jnp.where(column > row, packed, 0.0)
    lower = jnp.where(column < row, packed, 0.0)
    return upper + upper.T + diagonal, lower - lower.T


def exact(left, right):
    return jnp.dot(left, right, precision=HIGHEST, preferred_element_type=F32)


def complex_dot(left, right):
    top = jnp.concatenate([left[0], -left[1]], axis=1)
    bottom = jnp.concatenate([left[1], left[0]], axis=1)
    both = exact(jnp.concatenate([top, bottom], axis=0), jnp.concatenate([right[0], right[1]], axis=0))
    return both[0:128], both[128:256]


def newton(total):
    def kernel(ref, z_out):
        row = lax.broadcasted_iota(jnp.int32, (128, 128), 0)
        column = lax.broadcasted_iota(jnp.int32, (128, 128), 1)
        identity = jnp.where(row == column, 1.0, 0.0).astype(F32)
        g_real, g_imag = hermitian(ref[0:128, :])
        shrink = 1.0 / (RANGE * RANGE)
        n1 = jnp.sum(ref[128:136, :], axis=0, keepdims=True) * shrink / COUNT
        n2 = jnp.sum(ref[136:144, :], axis=0, keepdims=True) * shrink / COUNT
        n3 = jnp.sum(jnp.where(row == column, g_real, 0.0), axis=0, keepdims=True) * shrink / COUNT
        scale = lax.rsqrt(n1 + EPS)
        scale = scale * lax.rsqrt(scale * scale * n2 + EPS)
        scale = scale * lax.rsqrt(scale * scale * n3 + EPS)
        scale = jnp.broadcast_to(scale * (1.0 / RANGE), (128, 128))
        side = scale.T
        y = (side * g_real * scale / COUNT, side * g_imag * scale / COUNT)
        inverse = None
        for step in range(3):
            middle = y if inverse is None else complex_dot(inverse, y)
            factor = (1.5 * identity - 0.5 * middle[0], -0.5 * middle[1])
            if step < 2:
                y = complex_dot(y, factor)
            inverse = factor if inverse is None else complex_dot(factor, inverse)
        z_out[0] = side * inverse[0]
        z_out[1] = side * inverse[1]

    return pl.pallas_call(
        kernel,
        out_shape=jax.ShapeDtypeStruct((2, 128, 128), F32),
        compiler_params=params(),
        cost_estimate=pl.CostEstimate(flops=5_000_000_000, bytes_accessed=300_000, transcendentals=0),
        name="newton",
    )(total)


def rayleigh(total, z):
    def kernel(ref, z_ref, out):
        h = hermitian(ref[...])
        inverse = (z_ref[0], z_ref[1])
        half = complex_dot(h, inverse)
        full = complex_dot((inverse[0].T, -inverse[1].T), half)
        out[0] = full[0] / COUNT
        out[1] = full[1] / COUNT

    return pl.pallas_call(
        kernel,
        out_shape=jax.ShapeDtypeStruct((2, 128, 128), F32),
        compiler_params=params(),
        cost_estimate=pl.CostEstimate(flops=3_000_000_000, bytes_accessed=300_000, transcendentals=0),
        name="rayleigh",
    )(total, z)


def rotate(z, blocks):
    def kernel(z_ref, ref, out):
        top = jnp.concatenate([z_ref[0], z_ref[1]], axis=1)
        bottom = jnp.concatenate([-z_ref[1], z_ref[0]], axis=1)
        right = halves(jnp.concatenate([top, bottom], axis=0))
        for a in range(3):
            real, imag = slice(a * 128, a * 128 + 128), slice(384 + a * 128, 512 + a * 128)
            left = jnp.concatenate(
                [jnp.concatenate([ref[q, real, :], ref[q, imag, :]], axis=1) for q in range(2)], axis=0
            )
            found = dot3(halves(left), right)
            out[a] = found[:, 0:128]
            out[3 + a] = found[:, 128:256]

    return pl.pallas_call(
        kernel,
        grid=(4,),
        in_specs=[
            pl.BlockSpec((2, 128, 128), lambda i: (0, 0, 0)),
            pl.BlockSpec((2, 768, 128), lambda i: (i, 0, 0)),
        ],
        out_specs=pl.BlockSpec((6, 256, 128), lambda i: (0, i, 0)),
        out_shape=jax.ShapeDtypeStruct((6, 1024, 128), F32),
        compiler_params=params(),
        cost_estimate=pl.CostEstimate(flops=5_000_000_000, bytes_accessed=7_000_000, transcendentals=0),
        name="rotate",
    )(z, blocks)


def ring_pairs(step):
    return [(z * 8 + r, z * 8 + (r + step) % 8) for z in range(4) for r in range(8)]


def z_pairs(step):
    return [(i, (i + 8 * step) % 32) for i in range(32)]


def y_pairs(step):
    return ring_pairs(2 * step)


RINGS = [[z * 8 + r for r in range(8)] for z in range(4)]
CORES = [[2 * chip + core for chip in range(16)] for core in range(2)]
CORE_PAIRS = [(i, i ^ 1) for i in range(32)]


def move(value, pairs):
    return lax.ppermute(value, "sa", pairs)


def trade(value, groups=None):
    return lax.all_to_all(value, "sa", 0, 0, axis_index_groups=groups, tiled=True)


def spread(value, pairs):
    return [move(value, pairs(step)) for step in (2, 1, -1)]


def gathered(value, parts):
    return (value + parts[0]) + (parts[1] + parts[2])


def all_sum(value):
    value = value + move(value, CORE_PAIRS)
    value = gathered(value, spread(value, y_pairs))
    return gathered(value, spread(value, z_pairs))


def core_sum(value, core):
    given = lax.dynamic_index_in_dim(value, 1 - core, 0, False)
    return lax.dynamic_index_in_dim(value, core, 0, False) + move(given, CORE_PAIRS)


def local(start, links, momenta, displace):
    device = lax.axis_index("sa")
    ring = device % 8

    field = jnp.transpose(start.reshape(6, 8, 128, 128), (1, 0, 2, 3)).reshape(8, 768, 128)
    table = jnp.transpose(links.reshape(54, 8, 128), (1, 0, 2))
    under = jnp.transpose(jnp.roll(links[1], 1, 4).reshape(18, 8, 128), (1, 0, 2))
    u = trade(jnp.concatenate([field, table, under], axis=1), RINGS)

    zs = (device // 8) * 8 + jnp.arange(8, dtype=jnp.int32)[None, :, None, None]
    ys = ring * 4 + jnp.arange(4, dtype=jnp.int32)[None, None, :, None]
    xs = jnp.arange(32, dtype=jnp.int32)[None, None, None, :]
    along_x = momenta[:, 0][:, None, None, None]
    along_y = momenta[:, 1][:, None, None, None]
    along_z = momenta[:, 2][:, None, None, None]
    angles = TWO_PI * (
        (along_x * xs % 32).astype(F32) / 32
        + (along_y * ys % 32).astype(F32) / 32
        + (along_z * zs % 32).astype(F32) / 32
    )
    angles = angles.reshape(NMOM, 8, 128)
    phases = jnp.stack([jnp.cos(angles), jnp.sin(angles)], axis=1).reshape(2 * NMOM, 8, 128)
    phases = jnp.pad(jnp.transpose(phases, (1, 0, 2)), ((0, 0), (0, 2), (0, 0)))

    cells = u[:, 0:768].reshape(8, 6, 128, 128)
    z_low, z_high = u[0, 0:768], u[7]
    y_low, y_high = cells[:, :, 0:32], cells[:, :, 96:128]
    before = mesh_links = z_links = None
    norms = []
    for step in range(3):
        weight = (1.0 if step else RANGE) * (2.0 if step else 1.0)
        z_down = move(z_high, z_pairs(1))
        z_up = move(z_low, z_pairs(-1))
        y_down = move(y_high, ring_pairs(1))
        y_up = move(y_low, ring_pairs(-1))
        if step == 0:
            z_links = z_down[768:840]
        found = interior(
            u,
            mesh_links,
            before,
            weight * (6.0 * ALPHA - BETA),
            weight * ALPHA,
            RANGE if step == 1 else 1.0,
            f"interior_{step}",
        )
        if step == 0:
            mesh_links = found[2]
        norms.append(found[1])
        fresh, y_low, y_high, z_low, z_high = boundary(
            found[0], mesh_links, (z_up, z_down, y_up, y_down), z_links, weight * ALPHA, f"boundary_{step}"
        )
        before, u = u, fresh

    z_up = move(z_low, z_pairs(-1))
    y_up = move(y_low, ring_pairs(-1))
    back = trade(u, RINGS)
    packed_gram = gram(u, norms[1], norms[2])
    shared = packed_gram + move(packed_gram, CORE_PAIRS)
    ring_parts = spread(shared, y_pairs)
    right_x, x_hops = carry_x(u, mesh_links)
    ring_parts, x_hops, z_up, y_up = lax.optimization_barrier((ring_parts, x_hops, z_up, y_up))
    shared = gathered(shared, ring_parts)
    z_parts = spread(shared, z_pairs)
    right_yz, packed_h = carry_yz(u, mesh_links, z_up, y_up, x_hops, packed_gram)
    z_parts, packed_h = lax.optimization_barrier((z_parts, packed_h))
    total_gram = gathered(shared, z_parts)
    z = newton(total_gram)
    core = device % 2
    first = core_sum(elementals(z, u, right_x, right_yz, phases, 0, 4, "elementals_0"), core)
    first, back, u, packed_h = lax.optimization_barrier((first, back, u, packed_h))
    first = jnp.sum(trade(first, CORES), axis=0)
    second = core_sum(elementals(z, u, right_x, right_yz, phases, 4, 3, "elementals_1"), core)
    first, second, back, packed_h = lax.optimization_barrier((first, second, back, packed_h))
    sums = [first, jnp.sum(trade(second, CORES), axis=0)]
    total = all_sum(packed_h)
    ritz = rayleigh(total, z)
    basis = rotate(z, back).reshape(start.shape)

    rows = jnp.concatenate([part.reshape(4, -1, 2, 128) for part in sums], axis=1)
    real, imag = rows[:, :, 0].reshape(-1, 128), rows[:, :, 1].reshape(-1, 128)
    left = jnp.concatenate([real, imag], axis=1)
    top = jnp.concatenate([z[0], z[1]], axis=1)
    bottom = jnp.concatenate([-z[1], z[0]], axis=1)
    phi = jnp.dot(left, jnp.concatenate([top, bottom], axis=0), precision=HIGHEST)
    phi = (phi * (1.0 / math.sqrt(32768.0))).reshape(4, NMOM, 3, 2, 128)
    slots = displace[:, None] == jnp.arange(3, dtype=displace.dtype)[None, :]
    phi = jnp.sum(jnp.where(slots[None, None, :, :, None, None], phi[:, :, None], 0.0), axis=3)
    return (basis, ritz, phi)


def solution(mesh):
    in_specs = (
        P("ta", None, "sa", None, None, None),
        P("ta", None, None, None, "sa", None, None),
        P(),
        P(),
    )
    out_specs = (
        P("ta", None, "sa", None, None, None),
        P("ta", None, None),
        P("sa", "ta", None, None, None),
    )
    return jax.shard_map(local, mesh=mesh, in_specs=in_specs, out_specs=out_specs, check_vma=False)
```

```python
import math

import jax
import jax.numpy as jnp
from jax import lax
from jax.experimental import pallas as pl
from jax.experimental.pallas import tpu as pltpu
from jax.sharding import PartitionSpec as P

NMOM = 7
ALPHA = 2.0 / 11.0
BETA = 13.0 / 11.0
EPS = 1e-06
TWO_PI = 2.0 * math.pi
RANGE = 2.0**40
COUNT = 196608.0
HIGHEST = lax.Precision.HIGHEST
F32 = jnp.float32
BF16 = jnp.bfloat16
VMEM_LIMIT = 56 * 1024 * 1024


def params(**extra):
    return pltpu.CompilerParams(vmem_limit_bytes=VMEM_LIMIT, **extra)


def link_of(rows, direction):
    def entry(part, a, b):
        lane = ((direction * 2 + part) * 3 + a) * 3 + b
        return jnp.broadcast_to(rows[:, lane : lane + 1], rows.shape)

    real = [[entry(0, a, b) for b in range(3)] for a in range(2)]
    imag = [[entry(1, a, b) for b in range(3)] for a in range(2)]
    third_real, third_imag = [], []
    for b in range(3):
        p, q = (b + 1) % 3, (b + 2) % 3
        first = real[0][p] * real[1][q] - imag[0][p] * imag[1][q]
        second = real[0][q] * real[1][p] - imag[0][q] * imag[1][p]
        third_real.append(first - second)
        first = real[0][p] * imag[1][q] + imag[0][p] * real[1][q]
        second = real[0][q] * imag[1][p] + imag[0][q] * real[1][p]
        third_imag.append(second - first)
    return [real + [third_real], imag + [third_imag]]


def forward(link, v):
    real, imag = [], []
    for a in range(3):
        r = i = None
        for b in range(3):
            x = link[0][a][b] * v[b] - link[1][a][b] * v[3 + b]
            y = link[0][a][b] * v[3 + b] + link[1][a][b] * v[b]
            r = x if r is None else r + x
            i = y if i is None else i + y
        real.append(r)
        imag.append(i)
    return real + imag


def backward(link, v):
    real, imag = [], []
    for a in range(3):
        r = i = None
        for b in range(3):
            x = link[0][b][a] * v[b] + link[1][b][a] * v[3 + b]
            y = link[0][b][a] * v[3 + b] - link[1][b][a] * v[b]
            r = x if r is None else r + x
            i = y if i is None else i + y
        real.append(r)
        imag.append(i)
    return real + imag


def add(first, second):
    return [a + b for a, b in zip(first, second)]


def lay_out(field, links):
    def kernel(field_ref, link_ref, out):
        block = pl.program_id(0)
        for c in range(6):
            out[0, c * 128 : (c + 1) * 128, :] = field_ref[c]
        rows = [link_ref[:, pl.ds((4 * block + y + 31) % 32, 1), :].reshape(54, 32) for y in range(5)]
        out[0, 768:822, :] = jnp.concatenate(rows[1:], axis=1)
        out[0, 822:840, :] = jnp.concatenate([row[18:36] for row in rows[:4]], axis=1)

    return pl.pallas_call(
        kernel,
        grid=(8,),
        in_specs=[
            pl.BlockSpec((6, 128, 128), lambda q: (0, q, 0)),
            pl.BlockSpec((54, 32, 32), lambda q: (0, 0, 0)),
        ],
        out_specs=pl.BlockSpec((1, 840, 128), lambda q: (q, 0, 0)),
        out_shape=jax.ShapeDtypeStruct((8, 840, 128), F32),
        compiler_params=params(),
        cost_estimate=pl.CostEstimate(flops=3_000_000_000, bytes_accessed=7_000_000, transcendentals=0),
        name="lay_out",
    )(field, links)


def cell(ref, c, at, z=0):
    return ref[z, c * 128 + at.start : c * 128 + at.stop, :]


def cell_flat(ref, c, at):
    return ref[c * 128 + at.start : c * 128 + at.stop, :]


def interior(u, links, before, c0, c1, cp, name):
    first = links is None

    def kernel(*refs):
        if first:
            here, above, out, norm, link_ref, px, wx, py, pz = refs
            rows = jnp.concatenate([here[0, 768:840, :], jnp.zeros((56, 128), F32)], axis=0)
            link_ref[0] = rows.T
        else:
            here, above, link_ref, before_ref, out, norm, px, wx, py, pz = refs
        z = pl.program_id(0)
        inside = jnp.where(z < 7, 1.0, 0.0).astype(F32)

        @pl.when(z == 0)
        def _():
            norm[...] = jnp.zeros_like(norm)
            pz[...] = jnp.zeros_like(pz)

        total = jnp.zeros((8, 128), F32)
        for y in range(4):
            row = y * 32
            for c in range(6):
                px[c] = pltpu.roll(cell(here, c, slice(row, row + 32)), 31, 0)
            for g in range(4):
                at = slice(row + 8 * g, row + 8 * g + 8)
                own = slice(8 * g, 8 * g + 8)
                rows = link_ref[0, at, :]
                v = [cell(here, c, at) for c in range(6)]
                if not first:
                    for c in range(6):
                        total = total + v[c] * v[c]
                link = link_of(rows, 0)
                hop = forward(link, [px[c, own, :] for c in range(6)])
                side = backward(link, v)
                for c in range(6):
                    wx[c, own, :] = side[c]
                if y < 3:
                    link = link_of(rows, 1)
                    up = slice(at.start + 32, at.stop + 32)
                    hop = add(hop, forward(link, [cell(here, c, up) for c in range(6)]))
                    side = backward(link, v)
                if y > 0:
                    hop = add(hop, [py[c, own, :] for c in range(6)])
                if y < 3:
                    for c in range(6):
                        py[c, own, :] = side[c]
                link = link_of(rows, 2)
                far = forward(link, [cell(above, c, at) for c in range(6)])
                hop = [a + inside * b for a, b in zip(hop, far)]
                hop = add(hop, [pz[c, at, :] for c in range(6)])
                side = backward(link, v)
                for c in range(6):
                    pz[c, at, :] = side[c]
                    value = c0 * v[c] - c1 * hop[c]
                    if not first:
                        value = value - cp * cell(before_ref, c, at)
                    out[0, c * 128 + at.start : c * 128 + at.stop, :] = value
            for c in range(6):
                spot = slice(c * 128 + row, c * 128 + row + 32)
                out[0, spot, :] = out[0, spot, :] - c1 * pltpu.roll(wx[c], 1, 0)
        norm[...] = norm[...] + total

    block = pl.BlockSpec((1, 768, 128), lambda z: (z, 0, 0))
    next_block = pl.BlockSpec((1, 768, 128), lambda z: (jnp.minimum(z + 1, 7), 0, 0))
    link_block = pl.BlockSpec((1, 128, 128), lambda z: (z, 0, 0))
    out_specs = [block, pl.BlockSpec((8, 128), lambda z: (0, 0))]
    out_shape = [jax.ShapeDtypeStruct((8, 768, 128), F32), jax.ShapeDtypeStruct((8, 128), F32)]
    if first:
        in_specs = [pl.BlockSpec((1, 840, 128), lambda z: (z, 0, 0)), next_block]
        operands = [u, u]
        out_specs.append(link_block)
        out_shape.append(jax.ShapeDtypeStruct((8, 128, 128), F32))
    else:
        in_specs = [block, next_block, link_block, block]
        operands = [u, u, links, before]
    return pl.pallas_call(
        kernel,
        grid=(8,),
        in_specs=in_specs,
        out_specs=out_specs,
        out_shape=out_shape,
        scratch_shapes=[
            pltpu.VMEM((6, 32, 128), F32),
            pltpu.VMEM((6, 32, 128), F32),
            pltpu.VMEM((6, 32, 128), F32),
            pltpu.VMEM((6, 128, 128), F32),
        ],
        compiler_params=params(),
        cost_estimate=pl.CostEstimate(flops=12_000_000_000, bytes_accessed=12_000_000, transcendentals=0),
        name=name,
    )(*operands)


def boundary(partial, links, halo, z_links, c1, name):
    z_up, z_down, y_up, y_down = halo

    def kernel(part, link_ref, zu, zd, yu, yd, zl, out, y_low, y_high, z_low, z_high, turned):
        step = pl.program_id(0)

        def put(z, c, at, hop):
            spot = slice(c * 128 + at.start, c * 128 + at.stop)
            out[z, spot, :] = part[z, spot, :] - c1 * hop[c]

        def more(z, c, at, hop):
            spot = slice(c * 128 + at.start, c * 128 + at.stop)
            out[z, spot, :] = out[z, spot, :] - c1 * hop[c]

        for z in range(2):
            for g in range(4):
                own = slice(8 * g, 8 * g + 8)
                hop = backward(link_of(link_ref[z, own, :], 3), [yd[z, c, own, :] for c in range(6)])
                for c in range(6):
                    put(z, c, own, hop)
                at = slice(96 + 8 * g, 104 + 8 * g)
                hop = forward(link_of(link_ref[z, at, :], 1), [yu[z, c, own, :] for c in range(6)])
                for c in range(6):
                    put(z, c, at, hop)
            for c in range(6):
                spot = slice(c * 128 + 32, c * 128 + 96)
                out[z, spot, :] = part[z, spot, :]

        @pl.when(step == 0)
        def _():
            turned[...] = jnp.concatenate([zl[...], jnp.zeros((56, 128), F32)], axis=0).T
            for g in range(16):
                at = slice(8 * g, 8 * g + 8)
                hop = backward(link_of(turned[at, :], 2), [zd[c * 128 + at.start : c * 128 + at.stop, :] for c in range(6)])
                for c in range(6):
                    more(0, c, at, hop)
            z_low[...] = out[0]

        @pl.when(step == 3)
        def _():
            for g in range(16):
                at = slice(8 * g, 8 * g + 8)
                hop = forward(
                    link_of(link_ref[1, at, :], 2), [zu[c * 128 + at.start : c * 128 + at.stop, :] for c in range(6)]
                )
                for c in range(6):
                    more(1, c, at, hop)
            z_high[...] = out[1]

        for z in range(2):
            for c in range(6):
                y_low[z, c] = out[z, c * 128 : c * 128 + 32, :]
                y_high[z, c] = out[z, c * 128 + 96 : c * 128 + 128, :]

    block = pl.BlockSpec((2, 768, 128), lambda z: (z, 0, 0))
    y_face = pl.BlockSpec((2, 6, 32, 128), lambda z: (z, 0, 0, 0))
    z_face = pl.BlockSpec((768, 128), lambda z: (0, 0))
    return pl.pallas_call(
        kernel,
        grid=(4,),
        in_specs=[
            block,
            pl.BlockSpec((2, 128, 128), lambda z: (z, 0, 0)),
            z_face,
            z_face,
            y_face,
            y_face,
            pl.BlockSpec((72, 128), lambda z: (0, 0)),
        ],
        out_specs=(block, y_face, y_face, z_face, z_face),
        out_shape=(
            jax.ShapeDtypeStruct((8, 768, 128), F32),
            jax.ShapeDtypeStruct((8, 6, 32, 128), F32),
            jax.ShapeDtypeStruct((8, 6, 32, 128), F32),
            jax.ShapeDtypeStruct((768, 128), F32),
            jax.ShapeDtypeStruct((768, 128), F32),
        ),
        scratch_shapes=[pltpu.VMEM((128, 128), F32)],
        compiler_params=params(),
        cost_estimate=pl.CostEstimate(flops=6_000_000_000, bytes_accessed=9_000_000, transcendentals=0),
        name=name,
    )(partial, links, z_up, z_down, y_up, y_down, z_links)


def halves(value):
    high = value.astype(BF16)
    return high, (value - high.astype(F32)).astype(BF16)


def dot3(left, right):
    def dot(a, b):
        return jnp.dot(a, b, preferred_element_type=F32)

    return dot(left[0], right[0]) + (dot(left[0], right[1]) + dot(left[1], right[0]))


def transposed(ref, z, part):
    return jnp.concatenate([cell(ref, 3 * part + a, slice(0, 128), z).T for a in range(3)], axis=1)


def gram(u, first_norm, second_norm):
    def kernel(here, n1, n2, packed, acc):
        step = pl.program_id(0)

        @pl.when(step == 0)
        def _():
            acc[...] = jnp.zeros_like(acc)

        left = jnp.concatenate(
            [jnp.concatenate([transposed(here, z, part) for z in range(2)], axis=1) for part in range(2)], axis=0
        )
        right = jnp.concatenate([here[z, 0:384, :] for z in range(2)], axis=0)
        right = jnp.concatenate([right, jnp.concatenate([here[z, 384:768, :] for z in range(2)], axis=0)], axis=1)
        acc[...] = acc[...] + dot3(halves(left), halves(right))

        @pl.when(step == 3)
        def _():
            real = acc[0:128, 0:128] + acc[128:256, 128:256]
            imag = acc[0:128, 128:256] - acc[128:256, 0:128]
            row = lax.broadcasted_iota(jnp.int32, (128, 128), 0)
            column = lax.broadcasted_iota(jnp.int32, (128, 128), 1)
            packed[0:128, :] = jnp.where(column >= row, real, imag)
            packed[128:136, :] = n1[...]
            packed[136:144, :] = n2[...]

    fixed = pl.BlockSpec((8, 128), lambda z: (0, 0))
    return pl.pallas_call(
        kernel,
        grid=(4,),
        in_specs=[pl.BlockSpec((2, 768, 128), lambda z: (z, 0, 0)), fixed, fixed],
        out_specs=pl.BlockSpec((144, 128), lambda z: (0, 0)),
        out_shape=jax.ShapeDtypeStruct((144, 128), F32),
        scratch_shapes=[pltpu.VMEM((256, 256), F32)],
        compiler_params=params(),
        cost_estimate=pl.CostEstimate(flops=4_000_000_000, bytes_accessed=3_000_000, transcendentals=0),
        name="gram",
    )(u, first_norm, second_norm)


def put_halves(wide, carry, slots):
    for a in range(3):
        for k in range(slots):
            for part in range(2):
                hi, lo = halves(carry[k, 3 * part + a])
                spot = (k * 2 + part) * 128
                wide[0, a * 128 : (a + 1) * 128, spot : spot + 128] = hi
                wide[0, 384 + a * 128 : 512 + a * 128, spot : spot + 128] = lo
                wide[0, 768 + a * 128 : 896 + a * 128, spot : spot + 128] = hi


def add_hops(acc, here, carry, slots):
    left = jnp.concatenate([transposed(here, 0, part) for part in range(2)], axis=0)

    def summed(c):
        return carry[0, c] if slots == 1 else carry[0, c] + carry[1, c]

    right = jnp.concatenate(
        [jnp.concatenate([summed(a), summed(3 + a)], axis=1) for a in range(3)], axis=0
    )
    acc[...] = acc[...] + dot3(halves(left), halves(right))


def carry_x(u, links):
    def kernel(here, link_ref, wide, hops, px, carry, acc):
        z = pl.program_id(0)

        @pl.when(z == 0)
        def _():
            acc[...] = jnp.zeros_like(acc)

        for y in range(4):
            row = y * 32
            for c in range(6):
                px[c] = pltpu.roll(cell(here, c, slice(row, row + 32)), 31, 0)
            for g in range(4):
                at = slice(row + 8 * g, row + 8 * g + 8)
                own = slice(8 * g, 8 * g + 8)
                found = forward(link_of(link_ref[0, at, :], 0), [px[c, own, :] for c in range(6)])
                for c in range(6):
                    carry[0, c, at, :] = found[c]
        put_halves(wide, carry, 1)
        add_hops(acc, here, carry, 1)

        @pl.when(z == 7)
        def _():
            hops[...] = acc[...]

    block = pl.BlockSpec((1, 768, 128), lambda z: (z, 0, 0))
    return pl.pallas_call(
        kernel,
        grid=(8,),
        in_specs=[block, pl.BlockSpec((1, 128, 128), lambda z: (z, 0, 0))],
        out_specs=(pl.BlockSpec((1, 1152, 256), lambda z: (z, 0, 0)), pl.BlockSpec((256, 256), lambda z: (0, 0))),
        out_shape=(jax.ShapeDtypeStruct((8, 1152, 256), BF16), jax.ShapeDtypeStruct((256, 256), F32)),
        scratch_shapes=[
            pltpu.VMEM((6, 32, 128), F32),
            pltpu.VMEM((1, 6, 128, 128), F32),
            pltpu.VMEM((256, 256), F32),
        ],
        compiler_params=params(),
        cost_estimate=pl.CostEstimate(flops=7_000_000_000, bytes_accessed=8_000_000, transcendentals=0),
        name="carry_x",
    )(u, links)


def carry_yz(u, links, z_up, y_up, x_hops, packed_gram):
    def kernel(here, above, link_ref, zu, yu, hops_ref, gram_ref, wide, packed, carry, acc):
        z = pl.program_id(0)
        last = z == 7

        @pl.when(z == 0)
        def _():
            acc[...] = hops_ref[...]

        for y in range(4):
            row = y * 32
            for g in range(4):
                at = slice(row + 8 * g, row + 8 * g + 8)
                own = slice(8 * g, 8 * g + 8)
                rows = link_ref[0, at, :]
                if y < 3:
                    source = [cell(here, c, slice(at.start + 32, at.stop + 32)) for c in range(6)]
                else:
                    source = [yu[0, c, own, :] for c in range(6)]
                found = forward(link_of(rows, 1), source)
                for c in range(6):
                    carry[0, c, at, :] = found[c]
                source = [jnp.where(last, cell_flat(zu, c, at), cell(above, c, at)) for c in range(6)]
                found = forward(link_of(rows, 2), source)
                for c in range(6):
                    carry[1, c, at, :] = found[c]
        put_halves(wide, carry, 2)
        add_hops(acc, here, carry, 2)

        @pl.when(last)
        def _():
            gram_real, gram_imag = hermitian(gram_ref[0:128, :])
            hop_real = acc[0:128, 0:128] + acc[128:256, 128:256]
            hop_imag = acc[0:128, 128:256] - acc[128:256, 0:128]
            real = 6.0 * gram_real - (hop_real + hop_real.T)
            imag = 6.0 * gram_imag - (hop_imag - hop_imag.T)
            row = lax.broadcasted_iota(jnp.int32, (128, 128), 0)
            column = lax.broadcasted_iota(jnp.int32, (128, 128), 1)
            packed[...] = jnp.where(column >= row, real, imag)

    return pl.pallas_call(
        kernel,
        grid=(8,),
        in_specs=[
            pl.BlockSpec((1, 768, 128), lambda z: (z, 0, 0)),
            pl.BlockSpec((1, 768, 128), lambda z: (jnp.minimum(z + 1, 7), 0, 0)),
            pl.BlockSpec((1, 128, 128), lambda z: (z, 0, 0)),
            pl.BlockSpec((768, 128), lambda z: (0, 0)),
            pl.BlockSpec((1, 6, 32, 128), lambda z: (z, 0, 0, 0)),
            pl.BlockSpec((256, 256), lambda z: (0, 0)),
            pl.BlockSpec((144, 128), lambda z: (0, 0)),
        ],
        out_specs=(pl.BlockSpec((1, 1152, 512), lambda z: (z, 0, 0)), pl.BlockSpec((128, 128), lambda z: (0, 0))),
        out_shape=(jax.ShapeDtypeStruct((8, 1152, 512), BF16), jax.ShapeDtypeStruct((128, 128), F32)),
        scratch_shapes=[pltpu.VMEM((2, 6, 128, 128), F32), pltpu.VMEM((256, 256), F32)],
        compiler_params=params(),
        cost_estimate=pl.CostEstimate(flops=12_000_000_000, bytes_accessed=16_000_000, transcendentals=0),
        name="carry_yz",
    )(u, u, links, z_up, y_up, x_hops, packed_gram)


def elementals(z, u, right_x, right_yz, phases, first, count, extra, name):
    def kernel(z_ref, here, rx, ryz, phase, *refs):
        out, left, acc = refs[-3:]
        step = pl.program_id(0)

        @pl.when(step == 0)
        def _():
            acc[...] = jnp.zeros_like(acc)

        turned = [[here[zz, c * 128 : (c + 1) * 128, :].T for c in range(6)] for zz in range(2)]
        for m in range(count):
            mode = 2 * (first + m)
            for zz in range(2):
                cosine = phase[zz, mode : mode + 1, :]
                sine = phase[zz, mode + 1 : mode + 2, :]
                for a in range(3):
                    real, imag = turned[zz][a], turned[zz][3 + a]
                    spot = zz * 1152 + a * 128
                    pair = (real * cosine - imag * sine, -(real * sine + imag * cosine))
                    for part in range(2):
                        hi, lo = halves(pair[part])
                        rows = slice(m * 256 + part * 128, m * 256 + part * 128 + 128)
                        left[rows, spot : spot + 128] = hi
                        left[rows, spot + 384 : spot + 512] = hi
                        left[rows, spot + 768 : spot + 896] = lo
            if m % 2 == 0 and m != count - 1:
                continue
            done = slice((m - m % 2) * 256, (m + 1) * 256)
            found = jnp.dot(left[done, :], rx[...].reshape(2304, 256), preferred_element_type=F32)
            acc[done, 0:256] = acc[done, 0:256] + found
            found = jnp.dot(left[done, :], ryz[...].reshape(2304, 512), preferred_element_type=F32)
            acc[done, 256:768] = acc[done, 256:768] + found

        @pl.when(step == 3)
        def _():
            last = slice(count * 768, count * 768 + 128)
            for device in range(32):
                if extra is None:
                    out[device, :, last] = jnp.zeros((4, 128), F32)
                else:
                    out[device, :, last] = refs[0][device * 4 : device * 4 + 4, :]
            turn = halves(jnp.concatenate([z_ref[0].T, z_ref[1].T], axis=0))
            for m in range(count):
                real, imag = slice(m * 256, m * 256 + 128), slice(m * 256 + 128, m * 256 + 256)
                for k in range(3):
                    one, two = slice(256 * k, 256 * k + 128), slice(256 * k + 128, 256 * k + 256)
                    raw = [acc[real, one] - acc[imag, two], acc[real, two] + acc[imag, one]]
                    found = dot3(turn, halves(jnp.concatenate(raw, axis=1)))
                    top = found[0:128, 0:128] + found[128:256, 128:256]
                    bottom = found[0:128, 128:256] - found[128:256, 0:128]
                    place = (m * 3 + k) * 256
                    for device in range(32):
                        row = device * 4
                        out[device, :, place : place + 128] = top[row : row + 4]
                        out[device, :, place + 128 : place + 256] = bottom[row : row + 4]

    return pl.pallas_call(
        kernel,
        grid=(4,),
        in_specs=[
            pl.BlockSpec((2, 128, 128), lambda z: (0, 0, 0)),
            pl.BlockSpec((2, 768, 128), lambda z: (z, 0, 0)),
            pl.BlockSpec((2, 1152, 256), lambda z: (z, 0, 0)),
            pl.BlockSpec((2, 1152, 512), lambda z: (z, 0, 0)),
            pl.BlockSpec((2, 14, 128), lambda z: (z, 0, 0)),
        ]
        + [pl.BlockSpec((128, 128), lambda z: (0, 0))] * (extra is not None),
        out_specs=pl.BlockSpec((32, 4, count * 768 + 128), lambda z: (0, 0, 0)),
        out_shape=jax.ShapeDtypeStruct((32, 4, count * 768 + 128), F32),
        scratch_shapes=[
            pltpu.VMEM((count * 256, 2304), BF16),
            pltpu.VMEM((count * 256, 768), F32),
        ],
        compiler_params=params(),
        cost_estimate=pl.CostEstimate(flops=5_500_000_000 * count, bytes_accessed=16_000_000, transcendentals=0),
        name=name,
    )(z, u, right_x, right_yz, phases, *([] if extra is None else [extra]))


def hermitian(packed):
    row = lax.broadcasted_iota(jnp.int32, (128, 128), 0)
    column = lax.broadcasted_iota(jnp.int32, (128, 128), 1)
    diagonal = jnp.where(column == row, packed, 0.0)
    upper = jnp.where(column > row, packed, 0.0)
    lower = jnp.where(column < row, packed, 0.0)
    return upper + upper.T + diagonal, lower - lower.T


def exact(left, right):
    return jnp.dot(left, right, precision=HIGHEST, preferred_element_type=F32)


def complex_dot(left, right):
    top = jnp.concatenate([left[0], -left[1]], axis=1)
    bottom = jnp.concatenate([left[1], left[0]], axis=1)
    both = exact(jnp.concatenate([top, bottom], axis=0), jnp.concatenate([right[0], right[1]], axis=0))
    return both[0:128], both[128:256]


def newton(total):
    def kernel(ref, z_out):
        row = lax.broadcasted_iota(jnp.int32, (128, 128), 0)
        column = lax.broadcasted_iota(jnp.int32, (128, 128), 1)
        identity = jnp.where(row == column, 1.0, 0.0).astype(F32)
        g_real, g_imag = hermitian(ref[0:128, :])
        shrink = 1.0 / (RANGE * RANGE)
        n1 = jnp.sum(ref[128:136, :], axis=0, keepdims=True) * shrink / COUNT
        n2 = jnp.sum(ref[136:144, :], axis=0, keepdims=True) * shrink / COUNT
        n3 = jnp.sum(jnp.where(row == column, g_real, 0.0), axis=0, keepdims=True) * shrink / COUNT
        scale = lax.rsqrt(n1 + EPS)
        scale = scale * lax.rsqrt(scale * scale * n2 + EPS)
        scale = scale * lax.rsqrt(scale * scale * n3 + EPS)
        scale = jnp.broadcast_to(scale * (1.0 / RANGE), (128, 128))
        side = scale.T
        y = (side * g_real * scale / COUNT, side * g_imag * scale / COUNT)
        inverse = None
        for step in range(3):
            middle = y if inverse is None else complex_dot(inverse, y)
            factor = (1.5 * identity - 0.5 * middle[0], -0.5 * middle[1])
            if step < 2:
                y = complex_dot(y, factor)
            inverse = factor if inverse is None else complex_dot(factor, inverse)
        z_out[0] = side * inverse[0]
        z_out[1] = side * inverse[1]

    return pl.pallas_call(
        kernel,
        out_shape=jax.ShapeDtypeStruct((2, 128, 128), F32),
        compiler_params=params(),
        cost_estimate=pl.CostEstimate(flops=5_000_000_000, bytes_accessed=300_000, transcendentals=0),
        name="newton",
    )(total)


def rayleigh(total, z):
    def kernel(ref, z_ref, out):
        h = hermitian(ref[...])
        inverse = (z_ref[0], z_ref[1])
        half = complex_dot(h, inverse)
        full = complex_dot((inverse[0].T, -inverse[1].T), half)
        out[0] = full[0] / COUNT
        out[1] = full[1] / COUNT

    return pl.pallas_call(
        kernel,
        out_shape=jax.ShapeDtypeStruct((2, 128, 128), F32),
        compiler_params=params(),
        cost_estimate=pl.CostEstimate(flops=3_000_000_000, bytes_accessed=300_000, transcendentals=0),
        name="rayleigh",
    )(total, z)


def rotate(z, blocks):
    def kernel(z_ref, ref, out):
        top = jnp.concatenate([z_ref[0], z_ref[1]], axis=1)
        bottom = jnp.concatenate([-z_ref[1], z_ref[0]], axis=1)
        right = halves(jnp.concatenate([top, bottom], axis=0))
        for a in range(3):
            real, imag = slice(a * 128, a * 128 + 128), slice(384 + a * 128, 512 + a * 128)
            left = jnp.concatenate(
                [jnp.concatenate([ref[q, real, :], ref[q, imag, :]], axis=1) for q in range(2)], axis=0
            )
            found = dot3(halves(left), right)
            out[a] = found[:, 0:128]
            out[3 + a] = found[:, 128:256]

    return pl.pallas_call(
        kernel,
        grid=(4,),
        in_specs=[
            pl.BlockSpec((2, 128, 128), lambda i: (0, 0, 0)),
            pl.BlockSpec((2, 768, 128), lambda i: (i, 0, 0)),
        ],
        out_specs=pl.BlockSpec((6, 256, 128), lambda i: (0, i, 0)),
        out_shape=jax.ShapeDtypeStruct((6, 1024, 128), F32),
        compiler_params=params(),
        cost_estimate=pl.CostEstimate(flops=5_000_000_000, bytes_accessed=7_000_000, transcendentals=0),
        name="rotate",
    )(z, blocks)


def ring_pairs(step):
    return [(z * 8 + r, z * 8 + (r + step) % 8) for z in range(4) for r in range(8)]


def z_pairs(step):
    return [(i, (i + 8 * step) % 32) for i in range(32)]


def y_pairs(step):
    return ring_pairs(2 * step)


RINGS = [[z * 8 + r for r in range(8)] for z in range(4)]
CORE_PAIRS = [(i, i ^ 1) for i in range(32)]


def move(value, pairs):
    return lax.ppermute(value, "sa", pairs)


def trade(value, groups=None):
    return lax.all_to_all(value, "sa", 0, 0, axis_index_groups=groups, tiled=True)


def spread(value, pairs):
    return [move(value, pairs(step)) for step in (2, 1, -1)]


def gathered(value, parts):
    return (value + parts[0]) + (parts[1] + parts[2])


def local(start, links, momenta, displace):
    device = lax.axis_index("sa")
    ring = device % 8

    u = trade(lay_out(start.reshape(6, 1024, 128), links.reshape(54, 32, 32)), RINGS)

    zs = (device // 8) * 8 + jnp.arange(8, dtype=jnp.int32)[None, :, None, None]
    ys = ring * 4 + jnp.arange(4, dtype=jnp.int32)[None, None, :, None]
    xs = jnp.arange(32, dtype=jnp.int32)[None, None, None, :]
    along_x = momenta[:, 0][:, None, None, None]
    along_y = momenta[:, 1][:, None, None, None]
    along_z = momenta[:, 2][:, None, None, None]
    angles = TWO_PI * (
        (along_x * xs % 32).astype(F32) / 32
        + (along_y * ys % 32).astype(F32) / 32
        + (along_z * zs % 32).astype(F32) / 32
    )
    angles = angles.reshape(NMOM, 8, 128)
    phases = jnp.stack([jnp.cos(angles), jnp.sin(angles)], axis=1).reshape(2 * NMOM, 8, 128)
    phases = jnp.transpose(phases, (1, 0, 2))

    cells = u[:, 0:768].reshape(8, 6, 128, 128)
    z_low, z_high = u[0, 0:768], u[7]
    y_low, y_high = cells[:, :, 0:32], cells[:, :, 96:128]
    before = mesh_links = z_links = None
    norms = []
    for step in range(3):
        weight = (1.0 if step else RANGE) * (2.0 if step else 1.0)
        z_down = move(z_high, z_pairs(1))
        z_up = move(z_low, z_pairs(-1))
        y_down = move(y_high, ring_pairs(1))
        y_up = move(y_low, ring_pairs(-1))
        if step == 0:
            z_links = z_down[768:840]
        found = interior(
            u,
            mesh_links,
            before,
            weight * (6.0 * ALPHA - BETA),
            weight * ALPHA,
            RANGE if step == 1 else 1.0,
            f"interior_{step}",
        )
        if step == 0:
            mesh_links = found[2]
        norms.append(found[1])
        fresh, y_low, y_high, z_low, z_high = boundary(
            found[0], mesh_links, (z_up, z_down, y_up, y_down), z_links, weight * ALPHA, f"boundary_{step}"
        )
        before, u = u, fresh

    z_up = move(z_low, z_pairs(-1))
    y_up = move(y_low, ring_pairs(-1))
    back = trade(u, RINGS)
    packed_gram = gram(u, norms[1], norms[2])
    shared = packed_gram + move(packed_gram, CORE_PAIRS)
    ring_parts = spread(shared, y_pairs)
    right_x, x_hops = carry_x(u, mesh_links)
    ring_parts, x_hops, z_up, y_up = lax.optimization_barrier((ring_parts, x_hops, z_up, y_up))
    shared = gathered(shared, ring_parts)
    z_parts = spread(shared, z_pairs)
    right_yz, packed_h = carry_yz(u, mesh_links, z_up, y_up, x_hops, packed_gram)
    z_parts, packed_h = lax.optimization_barrier((z_parts, packed_h))
    total_gram = gathered(shared, z_parts)
    z = newton(total_gram)
    first = elementals(z, u, right_x, right_yz, phases, 0, 4, packed_h, "elementals_0")
    first, back, u = lax.optimization_barrier((first, back, u))
    first = jnp.sum(trade(first), axis=0)
    second = elementals(z, u, right_x, right_yz, phases, 4, 3, None, "elementals_1")
    first, second, back = lax.optimization_barrier((first, second, back))
    share = jnp.broadcast_to(first[:, 3072:], (32, 4, 128))
    second = trade(lax.dynamic_update_slice(second, share, (0, 0, 2304)))
    total = second[:, :, 2304:].reshape(128, 128)
    sums = [first[:, :3072], jnp.sum(second[:, :, :2304], axis=0)]
    ritz = rayleigh(total, z)
    basis = rotate(z, back).reshape(start.shape)

    rows = jnp.concatenate([part.reshape(4, -1, 2, 128) for part in sums], axis=1)
    real, imag = rows[:, :, 0].reshape(-1, 128), rows[:, :, 1].reshape(-1, 128)
    left = jnp.concatenate([real, imag], axis=1)
    top = jnp.concatenate([z[0], z[1]], axis=1)
    bottom = jnp.concatenate([-z[1], z[0]], axis=1)
    phi = jnp.dot(left, jnp.concatenate([top, bottom], axis=0), precision=HIGHEST)
    phi = (phi * (1.0 / math.sqrt(32768.0))).reshape(4, NMOM, 3, 2, 128)
    slots = displace[:, None] == jnp.arange(3, dtype=displace.dtype)[None, :]
    phi = jnp.sum(jnp.where(slots[None, None, :, :, None, None], phi[:, :, None], 0.0), axis=3)
    return (basis, ritz, phi)


def solution(mesh):
    in_specs = (
        P("ta", None, "sa", None, None, None),
        P("ta", None, None, None, "sa", None, None),
        P(),
        P(),
    )
    out_specs = (
        P("ta", None, "sa", None, None, None),
        P("ta", None, None),
        P("sa", "ta", None, None, None),
    )
    return jax.shard_map(local, mesh=mesh, in_specs=in_specs, out_specs=out_specs, check_vma=False)
```

```python
import math

import jax
import jax.numpy as jnp
from jax import lax
from jax.experimental import pallas as pl
from jax.experimental.pallas import tpu as pltpu
from jax.sharding import PartitionSpec as P

NMOM = 7
ALPHA = 2.0 / 11.0
BETA = 13.0 / 11.0
EPS = 1e-06
TWO_PI = 2.0 * math.pi
RANGE = 2.0**40
COUNT = 196608.0
HIGHEST = lax.Precision.HIGHEST
F32 = jnp.float32
BF16 = jnp.bfloat16
VMEM_LIMIT = 56 * 1024 * 1024
LAY, STEP, FACE, GRAM, CARRY_X, CARRY_YZ, TURN = 4, 1, 4, 4, 2, 2, 4


def params(**extra):
    return pltpu.CompilerParams(vmem_limit_bytes=VMEM_LIMIT, **extra)


def link_of(rows, direction):
    def entry(part, a, b):
        lane = ((direction * 2 + part) * 3 + a) * 3 + b
        return jnp.broadcast_to(rows[:, lane : lane + 1], rows.shape)

    real = [[entry(0, a, b) for b in range(3)] for a in range(2)]
    imag = [[entry(1, a, b) for b in range(3)] for a in range(2)]
    third_real, third_imag = [], []
    for b in range(3):
        p, q = (b + 1) % 3, (b + 2) % 3
        first = real[0][p] * real[1][q] - imag[0][p] * imag[1][q]
        second = real[0][q] * real[1][p] - imag[0][q] * imag[1][p]
        third_real.append(first - second)
        first = real[0][p] * imag[1][q] + imag[0][p] * real[1][q]
        second = real[0][q] * imag[1][p] + imag[0][q] * real[1][p]
        third_imag.append(second - first)
    return [real + [third_real], imag + [third_imag]]


def forward(link, v):
    real, imag = [], []
    for a in range(3):
        r = i = None
        for b in range(3):
            x = link[0][a][b] * v[b] - link[1][a][b] * v[3 + b]
            y = link[0][a][b] * v[3 + b] + link[1][a][b] * v[b]
            r = x if r is None else r + x
            i = y if i is None else i + y
        real.append(r)
        imag.append(i)
    return real + imag


def backward(link, v):
    real, imag = [], []
    for a in range(3):
        r = i = None
        for b in range(3):
            x = link[0][b][a] * v[b] + link[1][b][a] * v[3 + b]
            y = link[0][b][a] * v[3 + b] - link[1][b][a] * v[b]
            r = x if r is None else r + x
            i = y if i is None else i + y
        real.append(r)
        imag.append(i)
    return real + imag


def add(first, second):
    return [a + b for a, b in zip(first, second)]


def lay_out(field, links):
    def kernel(field_ref, link_ref, out):
        for q in range(LAY):
            block = pl.program_id(0) * LAY + q
            for c in range(6):
                out[q, c * 128 : (c + 1) * 128, :] = field_ref[c, q * 128 : (q + 1) * 128, :]
            rows = [link_ref[:, pl.ds((4 * block + y + 31) % 32, 1), :].reshape(54, 32) for y in range(5)]
            out[q, 768:822, :] = jnp.concatenate(rows[1:], axis=1)
            out[q, 822:840, :] = jnp.concatenate([row[18:36] for row in rows[:4]], axis=1)

    return pl.pallas_call(
        kernel,
        grid=(8 // LAY,),
        in_specs=[
            pl.BlockSpec((6, 128 * LAY, 128), lambda q: (0, q, 0)),
            pl.BlockSpec((54, 32, 32), lambda q: (0, 0, 0)),
        ],
        out_specs=pl.BlockSpec((LAY, 840, 128), lambda q: (q, 0, 0)),
        out_shape=jax.ShapeDtypeStruct((8, 840, 128), F32),
        compiler_params=params(),
        cost_estimate=pl.CostEstimate(flops=3_000_000_000, bytes_accessed=7_000_000, transcendentals=0),
        name="lay_out",
    )(field, links)


def cell(ref, c, at, z=0):
    return ref[z, c * 128 + at.start : c * 128 + at.stop, :]


def cell_flat(ref, c, at):
    return ref[c * 128 + at.start : c * 128 + at.stop, :]


def interior(u, links, before, c0, c1, cp, name):
    first = links is None

    def kernel(*refs):
        if first:
            here, above, out, norm, link_ref, px, wx, py, pz = refs
            for zz in range(STEP):
                rows = jnp.concatenate([here[zz, 768:840, :], jnp.zeros((56, 128), F32)], axis=0)
                link_ref[zz] = rows.T
        else:
            here, above, link_ref, before_ref, out, norm, px, wx, py, pz = refs
        z = pl.program_id(0)
        inside = jnp.where(z < 8 // STEP - 1, 1.0, 0.0).astype(F32)

        @pl.when(z == 0)
        def _():
            norm[...] = jnp.zeros_like(norm)
            pz[...] = jnp.zeros_like(pz)

        total = jnp.zeros((8, 128), F32)
        for zz in range(STEP):
            for y in range(4):
                row = y * 32
                for c in range(6):
                    px[c] = pltpu.roll(cell(here, c, slice(row, row + 32), zz), 31, 0)
                for g in range(4):
                    at = slice(row + 8 * g, row + 8 * g + 8)
                    own = slice(8 * g, 8 * g + 8)
                    rows = link_ref[zz, at, :]
                    v = [cell(here, c, at, zz) for c in range(6)]
                    if not first:
                        for c in range(6):
                            total = total + v[c] * v[c]
                    link = link_of(rows, 0)
                    hop = forward(link, [px[c, own, :] for c in range(6)])
                    side = backward(link, v)
                    for c in range(6):
                        wx[c, own, :] = side[c]
                    if y < 3:
                        link = link_of(rows, 1)
                        up = slice(at.start + 32, at.stop + 32)
                        hop = add(hop, forward(link, [cell(here, c, up, zz) for c in range(6)]))
                        side = backward(link, v)
                    if y > 0:
                        hop = add(hop, [py[c, own, :] for c in range(6)])
                    if y < 3:
                        for c in range(6):
                            py[c, own, :] = side[c]
                    link = link_of(rows, 2)
                    far = forward(link, [cell(here, c, at, zz + 1) if zz < STEP - 1 else cell(above, c, at) for c in range(6)])
                    hop = add(hop, far) if zz < STEP - 1 else [a + inside * b for a, b in zip(hop, far)]
                    hop = add(hop, [pz[c, at, :] for c in range(6)])
                    side = backward(link, v)
                    for c in range(6):
                        pz[c, at, :] = side[c]
                        value = c0 * v[c] - c1 * hop[c]
                        if not first:
                            value = value - cp * cell(before_ref, c, at, zz)
                        out[zz, c * 128 + at.start : c * 128 + at.stop, :] = value
                for c in range(6):
                    spot = slice(c * 128 + row, c * 128 + row + 32)
                    out[zz, spot, :] = out[zz, spot, :] - c1 * pltpu.roll(wx[c], 1, 0)
        norm[...] = norm[...] + total

    block = pl.BlockSpec((STEP, 768, 128), lambda z: (z, 0, 0))
    next_block = pl.BlockSpec((1, 768, 128), lambda z: (jnp.minimum(STEP * (z + 1), 7), 0, 0))
    link_block = pl.BlockSpec((STEP, 128, 128), lambda z: (z, 0, 0))
    out_specs = [block, pl.BlockSpec((8, 128), lambda z: (0, 0))]
    out_shape = [jax.ShapeDtypeStruct((8, 768, 128), F32), jax.ShapeDtypeStruct((8, 128), F32)]
    if first:
        in_specs = [pl.BlockSpec((STEP, 840, 128), lambda z: (z, 0, 0)), next_block]
        operands = [u, u]
        out_specs.append(link_block)
        out_shape.append(jax.ShapeDtypeStruct((8, 128, 128), F32))
    else:
        in_specs = [block, next_block, link_block, block]
        operands = [u, u, links, before]
    return pl.pallas_call(
        kernel,
        grid=(8 // STEP,),
        in_specs=in_specs,
        out_specs=out_specs,
        out_shape=out_shape,
        scratch_shapes=[
            pltpu.VMEM((6, 32, 128), F32),
            pltpu.VMEM((6, 32, 128), F32),
            pltpu.VMEM((6, 32, 128), F32),
            pltpu.VMEM((6, 128, 128), F32),
        ],
        compiler_params=params(),
        cost_estimate=pl.CostEstimate(flops=12_000_000_000, bytes_accessed=12_000_000, transcendentals=0),
        name=name,
    )(*operands)


def boundary(partial, links, halo, z_links, c1, name):
    z_up, z_down, y_up, y_down = halo

    def kernel(part, link_ref, zu, zd, yu, yd, zl, out, y_low, y_high, z_low, z_high, turned):
        step = pl.program_id(0)

        def put(z, c, at, hop):
            spot = slice(c * 128 + at.start, c * 128 + at.stop)
            out[z, spot, :] = part[z, spot, :] - c1 * hop[c]

        def more(z, c, at, hop):
            spot = slice(c * 128 + at.start, c * 128 + at.stop)
            out[z, spot, :] = out[z, spot, :] - c1 * hop[c]

        for z in range(FACE):
            for g in range(4):
                own = slice(8 * g, 8 * g + 8)
                hop = backward(link_of(link_ref[z, own, :], 3), [yd[z, c, own, :] for c in range(6)])
                for c in range(6):
                    put(z, c, own, hop)
                at = slice(96 + 8 * g, 104 + 8 * g)
                hop = forward(link_of(link_ref[z, at, :], 1), [yu[z, c, own, :] for c in range(6)])
                for c in range(6):
                    put(z, c, at, hop)
            for c in range(6):
                spot = slice(c * 128 + 32, c * 128 + 96)
                out[z, spot, :] = part[z, spot, :]

        @pl.when(step == 0)
        def _():
            turned[...] = jnp.concatenate([zl[...], jnp.zeros((56, 128), F32)], axis=0).T
            for g in range(16):
                at = slice(8 * g, 8 * g + 8)
                hop = backward(link_of(turned[at, :], 2), [zd[c * 128 + at.start : c * 128 + at.stop, :] for c in range(6)])
                for c in range(6):
                    more(0, c, at, hop)
            z_low[...] = out[0]

        @pl.when(step == 8 // FACE - 1)
        def _():
            for g in range(16):
                at = slice(8 * g, 8 * g + 8)
                hop = forward(
                    link_of(link_ref[FACE - 1, at, :], 2), [zu[c * 128 + at.start : c * 128 + at.stop, :] for c in range(6)]
                )
                for c in range(6):
                    more(FACE - 1, c, at, hop)
            z_high[...] = out[FACE - 1]

        for z in range(FACE):
            for c in range(6):
                y_low[z, c] = out[z, c * 128 : c * 128 + 32, :]
                y_high[z, c] = out[z, c * 128 + 96 : c * 128 + 128, :]

    block = pl.BlockSpec((FACE, 768, 128), lambda z: (z, 0, 0))
    y_face = pl.BlockSpec((FACE, 6, 32, 128), lambda z: (z, 0, 0, 0))
    z_face = pl.BlockSpec((768, 128), lambda z: (0, 0))
    return pl.pallas_call(
        kernel,
        grid=(8 // FACE,),
        in_specs=[
            block,
            pl.BlockSpec((FACE, 128, 128), lambda z: (z, 0, 0)),
            z_face,
            z_face,
            y_face,
            y_face,
            pl.BlockSpec((72, 128), lambda z: (0, 0)),
        ],
        out_specs=(block, y_face, y_face, z_face, z_face),
        out_shape=(
            jax.ShapeDtypeStruct((8, 768, 128), F32),
            jax.ShapeDtypeStruct((8, 6, 32, 128), F32),
            jax.ShapeDtypeStruct((8, 6, 32, 128), F32),
            jax.ShapeDtypeStruct((768, 128), F32),
            jax.ShapeDtypeStruct((768, 128), F32),
        ),
        scratch_shapes=[pltpu.VMEM((128, 128), F32)],
        compiler_params=params(),
        cost_estimate=pl.CostEstimate(flops=6_000_000_000, bytes_accessed=9_000_000, transcendentals=0),
        name=name,
    )(partial, links, z_up, z_down, y_up, y_down, z_links)


def halves(value):
    high = value.astype(BF16)
    return high, (value - high.astype(F32)).astype(BF16)


def dot3(left, right):
    def dot(a, b):
        return jnp.dot(a, b, preferred_element_type=F32)

    return dot(left[0], right[0]) + (dot(left[0], right[1]) + dot(left[1], right[0]))


def transposed(ref, z, part):
    return jnp.concatenate([cell(ref, 3 * part + a, slice(0, 128), z).T for a in range(3)], axis=1)


def gram(u, first_norm, second_norm):
    def kernel(here, n1, n2, packed, acc):
        step = pl.program_id(0)

        @pl.when(step == 0)
        def _():
            acc[...] = jnp.zeros_like(acc)

        left = jnp.concatenate(
            [jnp.concatenate([transposed(here, z, part) for z in range(GRAM)], axis=1) for part in range(2)], axis=0
        )
        right = jnp.concatenate([here[z, 0:384, :] for z in range(GRAM)], axis=0)
        right = jnp.concatenate([right, jnp.concatenate([here[z, 384:768, :] for z in range(GRAM)], axis=0)], axis=1)
        acc[...] = acc[...] + dot3(halves(left), halves(right))

        @pl.when(step == 8 // GRAM - 1)
        def _():
            real = acc[0:128, 0:128] + acc[128:256, 128:256]
            imag = acc[0:128, 128:256] - acc[128:256, 0:128]
            row = lax.broadcasted_iota(jnp.int32, (128, 128), 0)
            column = lax.broadcasted_iota(jnp.int32, (128, 128), 1)
            packed[0:128, :] = jnp.where(column >= row, real, imag)
            packed[128:136, :] = n1[...]
            packed[136:144, :] = n2[...]

    fixed = pl.BlockSpec((8, 128), lambda z: (0, 0))
    return pl.pallas_call(
        kernel,
        grid=(8 // GRAM,),
        in_specs=[pl.BlockSpec((GRAM, 768, 128), lambda z: (z, 0, 0)), fixed, fixed],
        out_specs=pl.BlockSpec((144, 128), lambda z: (0, 0)),
        out_shape=jax.ShapeDtypeStruct((144, 128), F32),
        scratch_shapes=[pltpu.VMEM((256, 256), F32)],
        compiler_params=params(),
        cost_estimate=pl.CostEstimate(flops=4_000_000_000, bytes_accessed=3_000_000, transcendentals=0),
        name="gram",
    )(u, first_norm, second_norm)


def put_halves(wide, zz, carry, slots):
    for a in range(3):
        for k in range(slots):
            for part in range(2):
                hi, lo = halves(carry[k, 3 * part + a])
                spot = (k * 2 + part) * 128
                wide[zz, a * 128 : (a + 1) * 128, spot : spot + 128] = hi
                wide[zz, 384 + a * 128 : 512 + a * 128, spot : spot + 128] = lo
                wide[zz, 768 + a * 128 : 896 + a * 128, spot : spot + 128] = hi


def add_hops(acc, here, zz, carry, slots):
    left = jnp.concatenate([transposed(here, zz, part) for part in range(2)], axis=0)

    def summed(c):
        return carry[0, c] if slots == 1 else carry[0, c] + carry[1, c]

    right = jnp.concatenate(
        [jnp.concatenate([summed(a), summed(3 + a)], axis=1) for a in range(3)], axis=0
    )
    acc[...] = acc[...] + dot3(halves(left), halves(right))


def carry_x(u, links):
    def kernel(here, link_ref, wide, hops, px, carry, acc):
        z = pl.program_id(0)

        @pl.when(z == 0)
        def _():
            acc[...] = jnp.zeros_like(acc)

        for zz in range(CARRY_X):
            for y in range(4):
                row = y * 32
                for c in range(6):
                    px[c] = pltpu.roll(cell(here, c, slice(row, row + 32), zz), 31, 0)
                for g in range(4):
                    at = slice(row + 8 * g, row + 8 * g + 8)
                    own = slice(8 * g, 8 * g + 8)
                    found = forward(link_of(link_ref[zz, at, :], 0), [px[c, own, :] for c in range(6)])
                    for c in range(6):
                        carry[0, c, at, :] = found[c]
            put_halves(wide, zz, carry, 1)
            add_hops(acc, here, zz, carry, 1)

        @pl.when(z == 8 // CARRY_X - 1)
        def _():
            hops[...] = acc[...]

    block = pl.BlockSpec((CARRY_X, 768, 128), lambda z: (z, 0, 0))
    return pl.pallas_call(
        kernel,
        grid=(8 // CARRY_X,),
        in_specs=[block, pl.BlockSpec((CARRY_X, 128, 128), lambda z: (z, 0, 0))],
        out_specs=(pl.BlockSpec((CARRY_X, 1152, 256), lambda z: (z, 0, 0)), pl.BlockSpec((256, 256), lambda z: (0, 0))),
        out_shape=(jax.ShapeDtypeStruct((8, 1152, 256), BF16), jax.ShapeDtypeStruct((256, 256), F32)),
        scratch_shapes=[
            pltpu.VMEM((6, 32, 128), F32),
            pltpu.VMEM((1, 6, 128, 128), F32),
            pltpu.VMEM((256, 256), F32),
        ],
        compiler_params=params(),
        cost_estimate=pl.CostEstimate(flops=7_000_000_000, bytes_accessed=8_000_000, transcendentals=0),
        name="carry_x",
    )(u, links)


def carry_yz(u, links, z_up, y_up, x_hops, packed_gram):
    def kernel(here, above, link_ref, zu, yu, hops_ref, gram_ref, wide, packed, carry, acc):
        z = pl.program_id(0)
        last = z == 8 // CARRY_YZ - 1

        @pl.when(z == 0)
        def _():
            acc[...] = hops_ref[...]

        for zz in range(CARRY_YZ):
            for y in range(4):
                row = y * 32
                for g in range(4):
                    at = slice(row + 8 * g, row + 8 * g + 8)
                    own = slice(8 * g, 8 * g + 8)
                    rows = link_ref[zz, at, :]
                    if y < 3:
                        source = [cell(here, c, slice(at.start + 32, at.stop + 32), zz) for c in range(6)]
                    else:
                        source = [yu[zz, c, own, :] for c in range(6)]
                    found = forward(link_of(rows, 1), source)
                    for c in range(6):
                        carry[0, c, at, :] = found[c]
                    if zz < CARRY_YZ - 1:
                        source = [cell(here, c, at, zz + 1) for c in range(6)]
                    else:
                        source = [jnp.where(last, cell_flat(zu, c, at), cell(above, c, at)) for c in range(6)]
                    found = forward(link_of(rows, 2), source)
                    for c in range(6):
                        carry[1, c, at, :] = found[c]
            put_halves(wide, zz, carry, 2)
            add_hops(acc, here, zz, carry, 2)

        @pl.when(last)
        def _():
            gram_real, gram_imag = hermitian(gram_ref[0:128, :])
            hop_real = acc[0:128, 0:128] + acc[128:256, 128:256]
            hop_imag = acc[0:128, 128:256] - acc[128:256, 0:128]
            real = 6.0 * gram_real - (hop_real + hop_real.T)
            imag = 6.0 * gram_imag - (hop_imag - hop_imag.T)
            row = lax.broadcasted_iota(jnp.int32, (128, 128), 0)
            column = lax.broadcasted_iota(jnp.int32, (128, 128), 1)
            packed[...] = jnp.where(column >= row, real, imag)

    return pl.pallas_call(
        kernel,
        grid=(8 // CARRY_YZ,),
        in_specs=[
            pl.BlockSpec((CARRY_YZ, 768, 128), lambda z: (z, 0, 0)),
            pl.BlockSpec((1, 768, 128), lambda z: (jnp.minimum(CARRY_YZ * (z + 1), 7), 0, 0)),
            pl.BlockSpec((CARRY_YZ, 128, 128), lambda z: (z, 0, 0)),
            pl.BlockSpec((768, 128), lambda z: (0, 0)),
            pl.BlockSpec((CARRY_YZ, 6, 32, 128), lambda z: (z, 0, 0, 0)),
            pl.BlockSpec((256, 256), lambda z: (0, 0)),
            pl.BlockSpec((144, 128), lambda z: (0, 0)),
        ],
        out_specs=(pl.BlockSpec((CARRY_YZ, 1152, 512), lambda z: (z, 0, 0)), pl.BlockSpec((128, 128), lambda z: (0, 0))),
        out_shape=(jax.ShapeDtypeStruct((8, 1152, 512), BF16), jax.ShapeDtypeStruct((128, 128), F32)),
        scratch_shapes=[pltpu.VMEM((2, 6, 128, 128), F32), pltpu.VMEM((256, 256), F32)],
        compiler_params=params(),
        cost_estimate=pl.CostEstimate(flops=12_000_000_000, bytes_accessed=16_000_000, transcendentals=0),
        name="carry_yz",
    )(u, u, links, z_up, y_up, x_hops, packed_gram)


def elementals(core, z, u, right_x, right_yz, phases, first, count, extra, spare, name):
    def kernel(core_ref, z_ref, here, rx, ryz, phase, *refs):
        kept, given, left, acc = refs[-4:]
        step = pl.program_id(0)
        own = core_ref[0] == 0

        @pl.when(step == 0)
        def _():
            acc[...] = jnp.zeros_like(acc)

        turned = [[here[zz, c * 128 : (c + 1) * 128, :].T for c in range(6)] for zz in range(2)]
        minus = [[-turned[zz][a] for a in range(3)] for zz in range(2)]

        def build(m):
            mode = 2 * (first + m)
            for zz in range(2):
                cosine = phase[zz, mode : mode + 1, :]
                sine = phase[zz, mode + 1 : mode + 2, :]
                for a in range(3):
                    real, imag = turned[zz][a], turned[zz][3 + a]
                    spot = zz * 1152 + a * 128
                    pair = (real * cosine - imag * sine, minus[zz][a] * sine - imag * cosine)
                    for part in range(2):
                        hi, lo = halves(pair[part])
                        rows = slice(m * 256 + part * 128, m * 256 + part * 128 + 128)
                        left[rows, spot : spot + 128] = hi
                        left[rows, spot + 384 : spot + 512] = hi
                        left[rows, spot + 768 : spot + 896] = lo

        def multiply(low, high):
            done = slice(low * 256, high * 256)
            found = jnp.dot(left[done, :], rx[...].reshape(2304, 256), preferred_element_type=F32)
            acc[done, 0:256] = acc[done, 0:256] + found
            found = jnp.dot(left[done, :], ryz[...].reshape(2304, 512), preferred_element_type=F32)
            acc[done, 256:768] = acc[done, 256:768] + found

        for m in range(2):
            build(m)
        for m in range(2, count):
            build(m)
        for low in range(0, count, 2):
            multiply(low, min(low + 2, count))

        @pl.when(step == 3)
        def _():
            def share(lanes, value):
                for chip in range(16):
                    low, high = value[chip * 8 : chip * 8 + 4], value[chip * 8 + 4 : chip * 8 + 8]
                    kept[chip, :, lanes] = jnp.where(own, low, high)
                    given[chip, :, lanes] = jnp.where(own, high, low)

            width = spare * 128
            lanes = slice(count * 768, count * 768 + width)
            share(lanes, jnp.zeros((128, width), F32) if extra is None else refs[0][...])
            turn = halves(jnp.concatenate([z_ref[0].T, z_ref[1].T], axis=0))
            for m in range(count):
                real, imag = slice(m * 256, m * 256 + 128), slice(m * 256 + 128, m * 256 + 256)
                for k in range(3):
                    one, two = slice(256 * k, 256 * k + 128), slice(256 * k + 128, 256 * k + 256)
                    raw = [acc[real, one] - acc[imag, two], acc[real, two] + acc[imag, one]]
                    found = dot3(turn, halves(jnp.concatenate(raw, axis=1)))
                    place = (m * 3 + k) * 256
                    share(slice(place, place + 128), found[0:128, 0:128] + found[128:256, 128:256])
                    share(slice(place + 128, place + 256), found[0:128, 128:256] - found[128:256, 0:128])

    shape = (16, 4, count * 768 + spare * 128)
    return pl.pallas_call(
        kernel,
        grid=(4,),
        in_specs=[
            pl.BlockSpec(memory_space=pltpu.SMEM),
            pl.BlockSpec((2, 128, 128), lambda z: (0, 0, 0)),
            pl.BlockSpec((2, 768, 128), lambda z: (z, 0, 0)),
            pl.BlockSpec((2, 1152, 256), lambda z: (z, 0, 0)),
            pl.BlockSpec((2, 1152, 512), lambda z: (z, 0, 0)),
            pl.BlockSpec((2, 14, 128), lambda z: (z, 0, 0)),
        ]
        + [pl.BlockSpec((128, 128), lambda z: (0, 0))] * (extra is not None),
        out_specs=[pl.BlockSpec(shape, lambda z: (0, 0, 0))] * 2,
        out_shape=[jax.ShapeDtypeStruct(shape, F32)] * 2,
        scratch_shapes=[
            pltpu.VMEM((count * 256, 2304), BF16),
            pltpu.VMEM((count * 256, 768), F32),
        ],
        compiler_params=params(),
        cost_estimate=pl.CostEstimate(flops=5_500_000_000 * count, bytes_accessed=16_000_000, transcendentals=0),
        name=name,
    )(core, z, u, right_x, right_yz, phases, *([] if extra is None else [extra]))


def hermitian(packed):
    row = lax.broadcasted_iota(jnp.int32, (128, 128), 0)
    column = lax.broadcasted_iota(jnp.int32, (128, 128), 1)
    diagonal = jnp.where(column == row, packed, 0.0)
    upper = jnp.where(column > row, packed, 0.0)
    lower = jnp.where(column < row, packed, 0.0)
    return upper + upper.T + diagonal, lower - lower.T


def exact(left, right):
    return jnp.dot(left, right, precision=HIGHEST, preferred_element_type=F32)


def complex_dot(left, right):
    top = jnp.concatenate([left[0], -left[1]], axis=1)
    bottom = jnp.concatenate([left[1], left[0]], axis=1)
    both = exact(jnp.concatenate([top, bottom], axis=0), jnp.concatenate([right[0], right[1]], axis=0))
    return both[0:128], both[128:256]


def newton(total):
    def kernel(ref, z_out):
        row = lax.broadcasted_iota(jnp.int32, (128, 128), 0)
        column = lax.broadcasted_iota(jnp.int32, (128, 128), 1)
        identity = jnp.where(row == column, 1.0, 0.0).astype(F32)
        g_real, g_imag = hermitian(ref[0:128, :])
        shrink = 1.0 / (RANGE * RANGE)
        n1 = jnp.sum(ref[128:136, :], axis=0, keepdims=True) * shrink / COUNT
        n2 = jnp.sum(ref[136:144, :], axis=0, keepdims=True) * shrink / COUNT
        n3 = jnp.sum(jnp.where(row == column, g_real, 0.0), axis=0, keepdims=True) * shrink / COUNT
        scale = lax.rsqrt(n1 + EPS)
        scale = scale * lax.rsqrt(scale * scale * n2 + EPS)
        scale = scale * lax.rsqrt(scale * scale * n3 + EPS)
        scale = jnp.broadcast_to(scale * (1.0 / RANGE), (128, 128))
        side = scale.T
        y = (side * g_real * scale / COUNT, side * g_imag * scale / COUNT)
        inverse = None
        for step in range(3):
            middle = y if inverse is None else complex_dot(inverse, y)
            factor = (1.5 * identity - 0.5 * middle[0], -0.5 * middle[1])
            if step < 2:
                y = complex_dot(y, factor)
            inverse = factor if inverse is None else complex_dot(factor, inverse)
        z_out[0] = side * inverse[0]
        z_out[1] = side * inverse[1]

    return pl.pallas_call(
        kernel,
        out_shape=jax.ShapeDtypeStruct((2, 128, 128), F32),
        compiler_params=params(),
        cost_estimate=pl.CostEstimate(flops=5_000_000_000, bytes_accessed=300_000, transcendentals=0),
        name="newton",
    )(total)


def rayleigh(total, z):
    def kernel(ref, z_ref, out):
        h = hermitian(ref[...])
        inverse = (z_ref[0], z_ref[1])
        half = complex_dot(h, inverse)
        full = complex_dot((inverse[0].T, -inverse[1].T), half)
        out[0] = full[0] / COUNT
        out[1] = full[1] / COUNT

    return pl.pallas_call(
        kernel,
        out_shape=jax.ShapeDtypeStruct((2, 128, 128), F32),
        compiler_params=params(),
        cost_estimate=pl.CostEstimate(flops=3_000_000_000, bytes_accessed=300_000, transcendentals=0),
        name="rayleigh",
    )(total, z)


def rotate(z, blocks):
    def kernel(z_ref, ref, out):
        top = jnp.concatenate([z_ref[0], z_ref[1]], axis=1)
        bottom = jnp.concatenate([-z_ref[1], z_ref[0]], axis=1)
        right = halves(jnp.concatenate([top, bottom], axis=0))
        for a in range(3):
            real, imag = slice(a * 128, a * 128 + 128), slice(384 + a * 128, 512 + a * 128)
            left = jnp.concatenate(
                [jnp.concatenate([ref[q, real, :], ref[q, imag, :]], axis=1) for q in range(TURN)], axis=0
            )
            found = dot3(halves(left), right)
            out[a] = found[:, 0:128]
            out[3 + a] = found[:, 128:256]

    return pl.pallas_call(
        kernel,
        grid=(8 // TURN,),
        in_specs=[
            pl.BlockSpec((2, 128, 128), lambda i: (0, 0, 0)),
            pl.BlockSpec((TURN, 768, 128), lambda i: (i, 0, 0)),
        ],
        out_specs=pl.BlockSpec((6, 128 * TURN, 128), lambda i: (0, i, 0)),
        out_shape=jax.ShapeDtypeStruct((6, 1024, 128), F32),
        compiler_params=params(),
        cost_estimate=pl.CostEstimate(flops=5_000_000_000, bytes_accessed=7_000_000, transcendentals=0),
        name="rotate",
    )(z, blocks)


def ring_pairs(step):
    return [(z * 8 + r, z * 8 + (r + step) % 8) for z in range(4) for r in range(8)]


def z_pairs(step):
    return [(i, (i + 8 * step) % 32) for i in range(32)]


def y_pairs(step):
    return ring_pairs(2 * step)


RINGS = [[z * 8 + r for r in range(8)] for z in range(4)]
CORES = [[2 * chip + core for chip in range(16)] for core in range(2)]
CORE_PAIRS = [(i, i ^ 1) for i in range(32)]


def move(value, pairs):
    return lax.ppermute(value, "sa", pairs)


def trade(value, groups=None):
    return lax.all_to_all(value, "sa", 0, 0, axis_index_groups=groups, tiled=True)


def spread(value, pairs):
    return [move(value, pairs(step)) for step in (2, 1, -1)]


def gathered(value, parts):
    return (value + parts[0]) + (parts[1] + parts[2])


def local(start, links, momenta, displace):
    device = lax.axis_index("sa")
    ring = device % 8

    u = trade(lay_out(start.reshape(6, 1024, 128), links.reshape(54, 32, 32)), RINGS)

    zs = (device // 8) * 8 + jnp.arange(8, dtype=jnp.int32)[None, :, None, None]
    ys = ring * 4 + jnp.arange(4, dtype=jnp.int32)[None, None, :, None]
    xs = jnp.arange(32, dtype=jnp.int32)[None, None, None, :]
    along_x = momenta[:, 0][:, None, None, None]
    along_y = momenta[:, 1][:, None, None, None]
    along_z = momenta[:, 2][:, None, None, None]
    angles = TWO_PI * (
        (along_x * xs % 32).astype(F32) / 32
        + (along_y * ys % 32).astype(F32) / 32
        + (along_z * zs % 32).astype(F32) / 32
    )
    angles = angles.reshape(NMOM, 8, 128)
    phases = jnp.stack([jnp.cos(angles), jnp.sin(angles)], axis=1).reshape(2 * NMOM, 8, 128)
    phases = jnp.transpose(phases, (1, 0, 2))

    cells = u[:, 0:768].reshape(8, 6, 128, 128)
    z_low, z_high = u[0, 0:768], u[7]
    y_low, y_high = cells[:, :, 0:32], cells[:, :, 96:128]
    before = mesh_links = z_links = None
    norms = []
    for step in range(3):
        weight = (1.0 if step else RANGE) * (2.0 if step else 1.0)
        z_down = move(z_high, z_pairs(1))
        z_up = move(z_low, z_pairs(-1))
        y_down = move(y_high, ring_pairs(1))
        y_up = move(y_low, ring_pairs(-1))
        if step == 0:
            z_links = z_down[768:840]
        found = interior(
            u,
            mesh_links,
            before,
            weight * (6.0 * ALPHA - BETA),
            weight * ALPHA,
            RANGE if step == 1 else 1.0,
            f"interior_{step}",
        )
        if step == 0:
            mesh_links = found[2]
        norms.append(found[1])
        fresh, y_low, y_high, z_low, z_high = boundary(
            found[0], mesh_links, (z_up, z_down, y_up, y_down), z_links, weight * ALPHA, f"boundary_{step}"
        )
        before, u = u, fresh

    z_up = move(z_low, z_pairs(-1))
    y_up = move(y_low, ring_pairs(-1))
    back = trade(u, RINGS)
    packed_gram = gram(u, norms[1], norms[2])
    shared = packed_gram + move(packed_gram, CORE_PAIRS)
    ring_parts = spread(shared, y_pairs)
    right_x, x_hops = carry_x(u, mesh_links)
    ring_parts, x_hops, z_up, y_up = lax.optimization_barrier((ring_parts, x_hops, z_up, y_up))
    shared = gathered(shared, ring_parts)
    z_parts = spread(shared, z_pairs)
    right_yz, packed_h = carry_yz(u, mesh_links, z_up, y_up, x_hops, packed_gram)
    z_parts, packed_h = lax.optimization_barrier((z_parts, packed_h))
    total_gram = gathered(shared, z_parts)
    z = newton(total_gram)
    core = device % 2
    where = core.reshape(1).astype(jnp.int32)
    kept, given = elementals(where, z, u, right_x, right_yz, phases, 0, 4, packed_h, 1, "elementals_0")
    first = kept + move(given, CORE_PAIRS)
    first, back, u = lax.optimization_barrier((first, back, u))
    first = jnp.sum(trade(first, CORES), axis=0)
    kept, given = elementals(where, z, u, right_x, right_yz, phases, 4, 3, None, 2, "elementals_1")
    first, kept, given = lax.optimization_barrier((first, kept, given))
    share = jnp.broadcast_to(first[:, 3072:], (16, 4, 128))
    given = lax.dynamic_update_slice(given, share, (0, 0, 2432))
    second = lax.dynamic_update_slice(kept, share, (0, 0, 2304)) + move(given, CORE_PAIRS)
    second, back = lax.optimization_barrier((second, back))
    second = trade(second, CORES)
    mine, others = second[:, :, 2304:2432], second[:, :, 2432:]
    low, high = jnp.where(core == 0, mine, others), jnp.where(core == 0, others, mine)
    total = jnp.stack([low, high], axis=1).reshape(128, 128)
    sums = [first[:, :3072], jnp.sum(second[:, :, :2304], axis=0)]
    ritz = rayleigh(total, z)
    basis = rotate(z, back).reshape(start.shape)

    rows = jnp.concatenate([part.reshape(4, -1, 2, 128) for part in sums], axis=1)
    real, imag = rows[:, :, 0].reshape(-1, 128), rows[:, :, 1].reshape(-1, 128)
    left = jnp.concatenate([real, imag], axis=1)
    top = jnp.concatenate([z[0], z[1]], axis=1)
    bottom = jnp.concatenate([-z[1], z[0]], axis=1)
    phi = jnp.dot(left, jnp.concatenate([top, bottom], axis=0), precision=HIGHEST)
    phi = (phi * (1.0 / math.sqrt(32768.0))).reshape(4, NMOM, 3, 2, 128)
    slots = displace[:, None] == jnp.arange(3, dtype=displace.dtype)[None, :]
    phi = jnp.sum(jnp.where(slots[None, None, :, :, None, None], phi[:, :, None], 0.0), axis=3)
    return (basis, ritz, phi)


def solution(mesh):
    in_specs = (
        P("ta", None, "sa", None, None, None),
        P("ta", None, None, None, "sa", None, None),
        P(),
        P(),
    )
    out_specs = (
        P("ta", None, "sa", None, None, None),
        P("ta", None, None),
        P("sa", "ta", None, None, None),
    )
    return jax.shard_map(local, mesh=mesh, in_specs=in_specs, out_specs=out_specs, check_vma=False)
```

```python
import math

import jax
import jax.numpy as jnp
from jax import lax
from jax.experimental import pallas as pl
from jax.experimental.pallas import tpu as pltpu
from jax.sharding import PartitionSpec as P

NMOM = 7
ALPHA = 2.0 / 11.0
BETA = 13.0 / 11.0
EPS = 1e-06
TWO_PI = 2.0 * math.pi
RANGE = 2.0**40
COUNT = 196608.0
HIGHEST = lax.Precision.HIGHEST
F32 = jnp.float32
BF16 = jnp.bfloat16
VMEM_LIMIT = 56 * 1024 * 1024
LAY, STEP, FACE, GRAM, CARRY_X, CARRY_YZ, TURN = 4, 1, 4, 4, 2, 2, 4


def params(**extra):
    return pltpu.CompilerParams(vmem_limit_bytes=VMEM_LIMIT, **extra)


def link_of(rows, direction):
    def entry(part, a, b):
        lane = ((direction * 2 + part) * 3 + a) * 3 + b
        return jnp.broadcast_to(rows[:, lane : lane + 1], rows.shape)

    real = [[entry(0, a, b) for b in range(3)] for a in range(2)]
    imag = [[entry(1, a, b) for b in range(3)] for a in range(2)]
    third_real, third_imag = [], []
    for b in range(3):
        p, q = (b + 1) % 3, (b + 2) % 3
        first = real[0][p] * real[1][q] - imag[0][p] * imag[1][q]
        second = real[0][q] * real[1][p] - imag[0][q] * imag[1][p]
        third_real.append(first - second)
        first = real[0][p] * imag[1][q] + imag[0][p] * real[1][q]
        second = real[0][q] * imag[1][p] + imag[0][q] * real[1][p]
        third_imag.append(second - first)
    return [real + [third_real], imag + [third_imag]]


def forward(link, v):
    real, imag = [], []
    for a in range(3):
        r = i = None
        for b in range(3):
            x = link[0][a][b] * v[b] - link[1][a][b] * v[3 + b]
            y = link[0][a][b] * v[3 + b] + link[1][a][b] * v[b]
            r = x if r is None else r + x
            i = y if i is None else i + y
        real.append(r)
        imag.append(i)
    return real + imag


def backward(link, v):
    real, imag = [], []
    for a in range(3):
        r = i = None
        for b in range(3):
            x = link[0][b][a] * v[b] + link[1][b][a] * v[3 + b]
            y = link[0][b][a] * v[3 + b] - link[1][b][a] * v[b]
            r = x if r is None else r + x
            i = y if i is None else i + y
        real.append(r)
        imag.append(i)
    return real + imag


def add(first, second):
    return [a + b for a, b in zip(first, second)]


def lay_out(field, links):
    def kernel(field_ref, link_ref, out):
        for q in range(LAY):
            block = pl.program_id(0) * LAY + q
            for c in range(6):
                out[q, c * 128 : (c + 1) * 128, :] = field_ref[c, q * 128 : (q + 1) * 128, :]
            rows = [link_ref[:, pl.ds((4 * block + y + 31) % 32, 1), :].reshape(54, 32) for y in range(5)]
            out[q, 768:822, :] = jnp.concatenate(rows[1:], axis=1)
            out[q, 822:840, :] = jnp.concatenate([row[18:36] for row in rows[:4]], axis=1)

    return pl.pallas_call(
        kernel,
        grid=(8 // LAY,),
        in_specs=[
            pl.BlockSpec((6, 128 * LAY, 128), lambda q: (0, q, 0)),
            pl.BlockSpec((54, 32, 32), lambda q: (0, 0, 0)),
        ],
        out_specs=pl.BlockSpec((LAY, 840, 128), lambda q: (q, 0, 0)),
        out_shape=jax.ShapeDtypeStruct((8, 840, 128), F32),
        compiler_params=params(),
        cost_estimate=pl.CostEstimate(flops=3_000_000_000, bytes_accessed=7_000_000, transcendentals=0),
        name="lay_out",
    )(field, links)


def cell(ref, c, at, z=0):
    return ref[z, c * 128 + at.start : c * 128 + at.stop, :]


def cell_flat(ref, c, at):
    return ref[c * 128 + at.start : c * 128 + at.stop, :]


def interior(u, links, before, c0, c1, cp, name):
    first = links is None

    def kernel(*refs):
        if first:
            here, above, out, norm, link_ref, px, wx, py, pz = refs
            for zz in range(STEP):
                rows = jnp.concatenate([here[zz, 768:840, :], jnp.zeros((56, 128), F32)], axis=0)
                link_ref[zz] = rows.T
        else:
            here, above, link_ref, before_ref, out, norm, px, wx, py, pz = refs
        z = pl.program_id(0)
        inside = jnp.where(z < 8 // STEP - 1, 1.0, 0.0).astype(F32)

        @pl.when(z == 0)
        def _():
            norm[...] = jnp.zeros_like(norm)
            pz[...] = jnp.zeros_like(pz)

        total = jnp.zeros((8, 128), F32)
        for zz in range(STEP):
            for y in range(4):
                row = y * 32
                for c in range(6):
                    px[c] = pltpu.roll(cell(here, c, slice(row, row + 32), zz), 31, 0)
                for g in range(4):
                    at = slice(row + 8 * g, row + 8 * g + 8)
                    own = slice(8 * g, 8 * g + 8)
                    rows = link_ref[zz, at, :]
                    v = [cell(here, c, at, zz) for c in range(6)]
                    if not first:
                        for c in range(6):
                            total = total + v[c] * v[c]
                    link = link_of(rows, 0)
                    hop = forward(link, [px[c, own, :] for c in range(6)])
                    side = backward(link, v)
                    for c in range(6):
                        wx[c, own, :] = side[c]
                    if y < 3:
                        link = link_of(rows, 1)
                        up = slice(at.start + 32, at.stop + 32)
                        hop = add(hop, forward(link, [cell(here, c, up, zz) for c in range(6)]))
                        side = backward(link, v)
                    if y > 0:
                        hop = add(hop, [py[c, own, :] for c in range(6)])
                    if y < 3:
                        for c in range(6):
                            py[c, own, :] = side[c]
                    link = link_of(rows, 2)
                    far = forward(link, [cell(here, c, at, zz + 1) if zz < STEP - 1 else cell(above, c, at) for c in range(6)])
                    hop = add(hop, far) if zz < STEP - 1 else [a + inside * b for a, b in zip(hop, far)]
                    hop = add(hop, [pz[c, at, :] for c in range(6)])
                    side = backward(link, v)
                    for c in range(6):
                        pz[c, at, :] = side[c]
                        value = c0 * v[c] - c1 * hop[c]
                        if not first:
                            value = value - cp * cell(before_ref, c, at, zz)
                        out[zz, c * 128 + at.start : c * 128 + at.stop, :] = value
                for c in range(6):
                    spot = slice(c * 128 + row, c * 128 + row + 32)
                    out[zz, spot, :] = out[zz, spot, :] - c1 * pltpu.roll(wx[c], 1, 0)
        norm[...] = norm[...] + total

    block = pl.BlockSpec((STEP, 768, 128), lambda z: (z, 0, 0))
    next_block = pl.BlockSpec((1, 768, 128), lambda z: (jnp.minimum(STEP * (z + 1), 7), 0, 0))
    link_block = pl.BlockSpec((STEP, 128, 128), lambda z: (z, 0, 0))
    out_specs = [block, pl.BlockSpec((8, 128), lambda z: (0, 0))]
    out_shape = [jax.ShapeDtypeStruct((8, 768, 128), F32), jax.ShapeDtypeStruct((8, 128), F32)]
    if first:
        in_specs = [pl.BlockSpec((STEP, 840, 128), lambda z: (z, 0, 0)), next_block]
        operands = [u, u]
        out_specs.append(link_block)
        out_shape.append(jax.ShapeDtypeStruct((8, 128, 128), F32))
    else:
        in_specs = [block, next_block, link_block, block]
        operands = [u, u, links, before]
    return pl.pallas_call(
        kernel,
        grid=(8 // STEP,),
        in_specs=in_specs,
        out_specs=out_specs,
        out_shape=out_shape,
        scratch_shapes=[
            pltpu.VMEM((6, 32, 128), F32),
            pltpu.VMEM((6, 32, 128), F32),
            pltpu.VMEM((6, 32, 128), F32),
            pltpu.VMEM((6, 128, 128), F32),
        ],
        compiler_params=params(),
        cost_estimate=pl.CostEstimate(flops=12_000_000_000, bytes_accessed=12_000_000, transcendentals=0),
        name=name,
    )(*operands)


def boundary(partial, links, halo, z_links, c1, name):
    z_up, z_down, y_up, y_down = halo

    def kernel(part, link_ref, zu, zd, yu, yd, zl, out, y_low, y_high, z_low, z_high, turned):
        step = pl.program_id(0)

        def put(z, c, at, hop):
            spot = slice(c * 128 + at.start, c * 128 + at.stop)
            out[z, spot, :] = part[z, spot, :] - c1 * hop[c]

        def more(z, c, at, hop):
            spot = slice(c * 128 + at.start, c * 128 + at.stop)
            out[z, spot, :] = out[z, spot, :] - c1 * hop[c]

        for z in range(FACE):
            for g in range(4):
                own = slice(8 * g, 8 * g + 8)
                hop = backward(link_of(link_ref[z, own, :], 3), [yd[z, c, own, :] for c in range(6)])
                for c in range(6):
                    put(z, c, own, hop)
                at = slice(96 + 8 * g, 104 + 8 * g)
                hop = forward(link_of(link_ref[z, at, :], 1), [yu[z, c, own, :] for c in range(6)])
                for c in range(6):
                    put(z, c, at, hop)
            for c in range(6):
                spot = slice(c * 128 + 32, c * 128 + 96)
                out[z, spot, :] = part[z, spot, :]

        @pl.when(step == 0)
        def _():
            turned[...] = jnp.concatenate([zl[...], jnp.zeros((56, 128), F32)], axis=0).T
            for g in range(16):
                at = slice(8 * g, 8 * g + 8)
                hop = backward(link_of(turned[at, :], 2), [zd[c * 128 + at.start : c * 128 + at.stop, :] for c in range(6)])
                for c in range(6):
                    more(0, c, at, hop)
            z_low[...] = out[0]

        @pl.when(step == 8 // FACE - 1)
        def _():
            for g in range(16):
                at = slice(8 * g, 8 * g + 8)
                hop = forward(
                    link_of(link_ref[FACE - 1, at, :], 2), [zu[c * 128 + at.start : c * 128 + at.stop, :] for c in range(6)]
                )
                for c in range(6):
                    more(FACE - 1, c, at, hop)
            z_high[...] = out[FACE - 1]

        for z in range(FACE):
            for c in range(6):
                y_low[z, c] = out[z, c * 128 : c * 128 + 32, :]
                y_high[z, c] = out[z, c * 128 + 96 : c * 128 + 128, :]

    block = pl.BlockSpec((FACE, 768, 128), lambda z: (z, 0, 0))
    y_face = pl.BlockSpec((FACE, 6, 32, 128), lambda z: (z, 0, 0, 0))
    z_face = pl.BlockSpec((768, 128), lambda z: (0, 0))
    return pl.pallas_call(
        kernel,
        grid=(8 // FACE,),
        in_specs=[
            block,
            pl.BlockSpec((FACE, 128, 128), lambda z: (z, 0, 0)),
            z_face,
            z_face,
            y_face,
            y_face,
            pl.BlockSpec((72, 128), lambda z: (0, 0)),
        ],
        out_specs=(block, y_face, y_face, z_face, z_face),
        out_shape=(
            jax.ShapeDtypeStruct((8, 768, 128), F32),
            jax.ShapeDtypeStruct((8, 6, 32, 128), F32),
            jax.ShapeDtypeStruct((8, 6, 32, 128), F32),
            jax.ShapeDtypeStruct((768, 128), F32),
            jax.ShapeDtypeStruct((768, 128), F32),
        ),
        scratch_shapes=[pltpu.VMEM((128, 128), F32)],
        compiler_params=params(),
        cost_estimate=pl.CostEstimate(flops=6_000_000_000, bytes_accessed=9_000_000, transcendentals=0),
        name=name,
    )(partial, links, z_up, z_down, y_up, y_down, z_links)


def halves(value):
    high = value.astype(BF16)
    return high, (value - high.astype(F32)).astype(BF16)


def dot3(left, right):
    def dot(a, b):
        return jnp.dot(a, b, preferred_element_type=F32)

    return dot(left[0], right[0]) + (dot(left[0], right[1]) + dot(left[1], right[0]))


def columns(ref, z, part):
    return jnp.concatenate([cell(ref, 3 * part + a, slice(0, 128), z) for a in range(3)], axis=1)


def gram(u, first_norm, second_norm):
    def kernel(here, n1, n2, packed, turned, acc):
        step = pl.program_id(0)

        @pl.when(step == 0)
        def _():
            acc[...] = jnp.zeros_like(acc)

        for z in range(GRAM):
            for c in range(6):
                turned[z, c * 128 : (c + 1) * 128, :] = cell(here, c, slice(0, 128), z).T
        left = jnp.concatenate(
            [jnp.concatenate([columns(turned, z, part) for z in range(GRAM)], axis=1) for part in range(2)], axis=0
        )
        right = jnp.concatenate([here[z, 0:384, :] for z in range(GRAM)], axis=0)
        right = jnp.concatenate([right, jnp.concatenate([here[z, 384:768, :] for z in range(GRAM)], axis=0)], axis=1)
        acc[...] = acc[...] + dot3(halves(left), halves(right))

        @pl.when(step == 8 // GRAM - 1)
        def _():
            real = acc[0:128, 0:128] + acc[128:256, 128:256]
            imag = acc[0:128, 128:256] - acc[128:256, 0:128]
            row = lax.broadcasted_iota(jnp.int32, (128, 128), 0)
            column = lax.broadcasted_iota(jnp.int32, (128, 128), 1)
            packed[0:128, :] = jnp.where(column >= row, real, imag)
            packed[128:136, :] = n1[...]
            packed[136:144, :] = n2[...]

    fixed = pl.BlockSpec((8, 128), lambda z: (0, 0))
    return pl.pallas_call(
        kernel,
        grid=(8 // GRAM,),
        in_specs=[pl.BlockSpec((GRAM, 768, 128), lambda z: (z, 0, 0)), fixed, fixed],
        out_specs=(pl.BlockSpec((144, 128), lambda z: (0, 0)), pl.BlockSpec((GRAM, 768, 128), lambda z: (z, 0, 0))),
        out_shape=(jax.ShapeDtypeStruct((144, 128), F32), jax.ShapeDtypeStruct((8, 768, 128), F32)),
        scratch_shapes=[pltpu.VMEM((256, 256), F32)],
        compiler_params=params(),
        cost_estimate=pl.CostEstimate(flops=4_000_000_000, bytes_accessed=3_000_000, transcendentals=0),
        name="gram",
    )(u, first_norm, second_norm)


def put_halves(wide, zz, carry, slots):
    for a in range(3):
        for k in range(slots):
            for part in range(2):
                hi, lo = halves(carry[k, 3 * part + a])
                spot = (k * 2 + part) * 128
                wide[zz, a * 128 : (a + 1) * 128, spot : spot + 128] = hi
                wide[zz, 384 + a * 128 : 512 + a * 128, spot : spot + 128] = lo
                wide[zz, 768 + a * 128 : 896 + a * 128, spot : spot + 128] = hi


def add_hops(acc, turned, zz, carry, slots):
    left = jnp.concatenate([columns(turned, zz, part) for part in range(2)], axis=0)

    def summed(c):
        return carry[0, c] if slots == 1 else carry[0, c] + carry[1, c]

    right = jnp.concatenate(
        [jnp.concatenate([summed(a), summed(3 + a)], axis=1) for a in range(3)], axis=0
    )
    acc[...] = acc[...] + dot3(halves(left), halves(right))


def carry_x(u, turned, links):
    def kernel(here, turned, link_ref, wide, hops, px, carry, acc):
        z = pl.program_id(0)

        @pl.when(z == 0)
        def _():
            acc[...] = jnp.zeros_like(acc)

        for zz in range(CARRY_X):
            for y in range(4):
                row = y * 32
                for c in range(6):
                    px[c] = pltpu.roll(cell(here, c, slice(row, row + 32), zz), 31, 0)
                for g in range(4):
                    at = slice(row + 8 * g, row + 8 * g + 8)
                    own = slice(8 * g, 8 * g + 8)
                    found = forward(link_of(link_ref[zz, at, :], 0), [px[c, own, :] for c in range(6)])
                    for c in range(6):
                        carry[0, c, at, :] = found[c]
            put_halves(wide, zz, carry, 1)
            add_hops(acc, turned, zz, carry, 1)

        @pl.when(z == 8 // CARRY_X - 1)
        def _():
            hops[...] = acc[...]

    block = pl.BlockSpec((CARRY_X, 768, 128), lambda z: (z, 0, 0))
    return pl.pallas_call(
        kernel,
        grid=(8 // CARRY_X,),
        in_specs=[block, block, pl.BlockSpec((CARRY_X, 128, 128), lambda z: (z, 0, 0))],
        out_specs=(pl.BlockSpec((CARRY_X, 1152, 256), lambda z: (z, 0, 0)), pl.BlockSpec((256, 256), lambda z: (0, 0))),
        out_shape=(jax.ShapeDtypeStruct((8, 1152, 256), BF16), jax.ShapeDtypeStruct((256, 256), F32)),
        scratch_shapes=[
            pltpu.VMEM((6, 32, 128), F32),
            pltpu.VMEM((1, 6, 128, 128), F32),
            pltpu.VMEM((256, 256), F32),
        ],
        compiler_params=params(),
        cost_estimate=pl.CostEstimate(flops=7_000_000_000, bytes_accessed=8_000_000, transcendentals=0),
        name="carry_x",
    )(u, turned, links)


def carry_yz(u, turned, links, z_up, y_up, x_hops, packed_gram):
    def kernel(here, turned, above, link_ref, zu, yu, hops_ref, gram_ref, wide, packed, carry, acc):
        z = pl.program_id(0)
        last = z == 8 // CARRY_YZ - 1

        @pl.when(z == 0)
        def _():
            acc[...] = hops_ref[...]

        for zz in range(CARRY_YZ):
            for y in range(4):
                row = y * 32
                for g in range(4):
                    at = slice(row + 8 * g, row + 8 * g + 8)
                    own = slice(8 * g, 8 * g + 8)
                    rows = link_ref[zz, at, :]
                    if y < 3:
                        source = [cell(here, c, slice(at.start + 32, at.stop + 32), zz) for c in range(6)]
                    else:
                        source = [yu[zz, c, own, :] for c in range(6)]
                    found = forward(link_of(rows, 1), source)
                    for c in range(6):
                        carry[0, c, at, :] = found[c]
                    if zz < CARRY_YZ - 1:
                        source = [cell(here, c, at, zz + 1) for c in range(6)]
                    else:
                        source = [jnp.where(last, cell_flat(zu, c, at), cell(above, c, at)) for c in range(6)]
                    found = forward(link_of(rows, 2), source)
                    for c in range(6):
                        carry[1, c, at, :] = found[c]
            put_halves(wide, zz, carry, 2)
            add_hops(acc, turned, zz, carry, 2)

        @pl.when(last)
        def _():
            gram_real, gram_imag = hermitian(gram_ref[0:128, :])
            hop_real = acc[0:128, 0:128] + acc[128:256, 128:256]
            hop_imag = acc[0:128, 128:256] - acc[128:256, 0:128]
            real = 6.0 * gram_real - (hop_real + hop_real.T)
            imag = 6.0 * gram_imag - (hop_imag - hop_imag.T)
            row = lax.broadcasted_iota(jnp.int32, (128, 128), 0)
            column = lax.broadcasted_iota(jnp.int32, (128, 128), 1)
            packed[...] = jnp.where(column >= row, real, imag)

    return pl.pallas_call(
        kernel,
        grid=(8 // CARRY_YZ,),
        in_specs=[
            pl.BlockSpec((CARRY_YZ, 768, 128), lambda z: (z, 0, 0)),
            pl.BlockSpec((CARRY_YZ, 768, 128), lambda z: (z, 0, 0)),
            pl.BlockSpec((1, 768, 128), lambda z: (jnp.minimum(CARRY_YZ * (z + 1), 7), 0, 0)),
            pl.BlockSpec((CARRY_YZ, 128, 128), lambda z: (z, 0, 0)),
            pl.BlockSpec((768, 128), lambda z: (0, 0)),
            pl.BlockSpec((CARRY_YZ, 6, 32, 128), lambda z: (z, 0, 0, 0)),
            pl.BlockSpec((256, 256), lambda z: (0, 0)),
            pl.BlockSpec((144, 128), lambda z: (0, 0)),
        ],
        out_specs=(pl.BlockSpec((CARRY_YZ, 1152, 512), lambda z: (z, 0, 0)), pl.BlockSpec((128, 128), lambda z: (0, 0))),
        out_shape=(jax.ShapeDtypeStruct((8, 1152, 512), BF16), jax.ShapeDtypeStruct((128, 128), F32)),
        scratch_shapes=[pltpu.VMEM((2, 6, 128, 128), F32), pltpu.VMEM((256, 256), F32)],
        compiler_params=params(),
        cost_estimate=pl.CostEstimate(flops=12_000_000_000, bytes_accessed=16_000_000, transcendentals=0),
        name="carry_yz",
    )(u, turned, u, links, z_up, y_up, x_hops, packed_gram)


def elementals(core, z, turned_u, right_x, right_yz, phases, first, count, extra, spare, name):
    def kernel(core_ref, z_ref, here, rx, ryz, phase, *refs):
        kept, given, left, acc = refs[-4:]
        step = pl.program_id(0)
        own = core_ref[0] == 0

        @pl.when(step == 0)
        def _():
            acc[...] = jnp.zeros_like(acc)

        turned = [[here[zz, c * 128 : (c + 1) * 128, :] for c in range(6)] for zz in range(2)]
        minus = [[-turned[zz][a] for a in range(3)] for zz in range(2)]

        def build(m):
            mode = 2 * (first + m)
            for zz in range(2):
                cosine = phase[zz, mode : mode + 1, :]
                sine = phase[zz, mode + 1 : mode + 2, :]
                for a in range(3):
                    real, imag = turned[zz][a], turned[zz][3 + a]
                    spot = zz * 1152 + a * 128
                    pair = (real * cosine - imag * sine, minus[zz][a] * sine - imag * cosine)
                    for part in range(2):
                        hi, lo = halves(pair[part])
                        rows = slice(m * 256 + part * 128, m * 256 + part * 128 + 128)
                        left[rows, spot : spot + 128] = hi
                        left[rows, spot + 384 : spot + 512] = hi
                        left[rows, spot + 768 : spot + 896] = lo

        def multiply(low, high):
            done = slice(low * 256, high * 256)
            found = jnp.dot(left[done, :], rx[...].reshape(2304, 256), preferred_element_type=F32)
            acc[done, 0:256] = acc[done, 0:256] + found
            found = jnp.dot(left[done, :], ryz[...].reshape(2304, 512), preferred_element_type=F32)
            acc[done, 256:768] = acc[done, 256:768] + found

        for m in range(2):
            build(m)
        for m in range(2, count):
            build(m)
        for low in range(0, count, 2):
            multiply(low, min(low + 2, count))

        @pl.when(step == 3)
        def _():
            def share(lanes, value):
                for chip in range(16):
                    low, high = value[chip * 8 : chip * 8 + 4], value[chip * 8 + 4 : chip * 8 + 8]
                    kept[chip, :, lanes] = jnp.where(own, low, high)
                    given[chip, :, lanes] = jnp.where(own, high, low)

            width = spare * 128
            lanes = slice(count * 768, count * 768 + width)
            share(lanes, jnp.zeros((128, width), F32) if extra is None else refs[0][...])
            turn = halves(jnp.concatenate([z_ref[0].T, z_ref[1].T], axis=0))
            for m in range(count):
                real, imag = slice(m * 256, m * 256 + 128), slice(m * 256 + 128, m * 256 + 256)
                for k in range(3):
                    one, two = slice(256 * k, 256 * k + 128), slice(256 * k + 128, 256 * k + 256)
                    raw = [acc[real, one] - acc[imag, two], acc[real, two] + acc[imag, one]]
                    found = dot3(turn, halves(jnp.concatenate(raw, axis=1)))
                    place = (m * 3 + k) * 256
                    share(slice(place, place + 128), found[0:128, 0:128] + found[128:256, 128:256])
                    share(slice(place + 128, place + 256), found[0:128, 128:256] - found[128:256, 0:128])

    shape = (16, 4, count * 768 + spare * 128)
    return pl.pallas_call(
        kernel,
        grid=(4,),
        in_specs=[
            pl.BlockSpec(memory_space=pltpu.SMEM),
            pl.BlockSpec((2, 128, 128), lambda z: (0, 0, 0)),
            pl.BlockSpec((2, 768, 128), lambda z: (z, 0, 0)),
            pl.BlockSpec((2, 1152, 256), lambda z: (z, 0, 0)),
            pl.BlockSpec((2, 1152, 512), lambda z: (z, 0, 0)),
            pl.BlockSpec((2, 14, 128), lambda z: (z, 0, 0)),
        ]
        + [pl.BlockSpec((128, 128), lambda z: (0, 0))] * (extra is not None),
        out_specs=[pl.BlockSpec(shape, lambda z: (0, 0, 0))] * 2,
        out_shape=[jax.ShapeDtypeStruct(shape, F32)] * 2,
        scratch_shapes=[
            pltpu.VMEM((count * 256, 2304), BF16),
            pltpu.VMEM((count * 256, 768), F32),
        ],
        compiler_params=params(),
        cost_estimate=pl.CostEstimate(flops=5_500_000_000 * count, bytes_accessed=16_000_000, transcendentals=0),
        name=name,
    )(core, z, turned_u, right_x, right_yz, phases, *([] if extra is None else [extra]))


def hermitian(packed):
    row = lax.broadcasted_iota(jnp.int32, (128, 128), 0)
    column = lax.broadcasted_iota(jnp.int32, (128, 128), 1)
    diagonal = jnp.where(column == row, packed, 0.0)
    upper = jnp.where(column > row, packed, 0.0)
    lower = jnp.where(column < row, packed, 0.0)
    return upper + upper.T + diagonal, lower - lower.T


def complex_dot(left, right):
    top = jnp.concatenate([left[0], -left[1]], axis=1)
    bottom = jnp.concatenate([left[1], left[0]], axis=1)
    both = dot3(halves(jnp.concatenate([top, bottom], axis=0)), halves(jnp.concatenate([right[0], right[1]], axis=0)))
    return both[0:128], both[128:256]


def newton(total):
    def kernel(ref, z_out):
        row = lax.broadcasted_iota(jnp.int32, (128, 128), 0)
        column = lax.broadcasted_iota(jnp.int32, (128, 128), 1)
        identity = jnp.where(row == column, 1.0, 0.0).astype(F32)
        g_real, g_imag = hermitian(ref[0:128, :])
        shrink = 1.0 / (RANGE * RANGE)
        n1 = jnp.sum(ref[128:136, :], axis=0, keepdims=True) * shrink / COUNT
        n2 = jnp.sum(ref[136:144, :], axis=0, keepdims=True) * shrink / COUNT
        n3 = jnp.sum(jnp.where(row == column, g_real, 0.0), axis=0, keepdims=True) * shrink / COUNT
        scale = lax.rsqrt(n1 + EPS)
        scale = scale * lax.rsqrt(scale * scale * n2 + EPS)
        scale = scale * lax.rsqrt(scale * scale * n3 + EPS)
        scale = jnp.broadcast_to(scale * (1.0 / RANGE), (128, 128))
        side = scale.T
        y = (side * g_real * scale / COUNT, side * g_imag * scale / COUNT)
        inverse = None
        for step in range(3):
            middle = y if inverse is None else complex_dot(inverse, y)
            factor = (1.5 * identity - 0.5 * middle[0], -0.5 * middle[1])
            if step < 2:
                y = complex_dot(y, factor)
            inverse = factor if inverse is None else complex_dot(factor, inverse)
        z_out[0] = side * inverse[0]
        z_out[1] = side * inverse[1]

    return pl.pallas_call(
        kernel,
        out_shape=jax.ShapeDtypeStruct((2, 128, 128), F32),
        compiler_params=params(),
        cost_estimate=pl.CostEstimate(flops=5_000_000_000, bytes_accessed=300_000, transcendentals=0),
        name="newton",
    )(total)


def rayleigh(total, z):
    def kernel(ref, z_ref, out):
        h = hermitian(ref[...])
        inverse = (z_ref[0], z_ref[1])
        half = complex_dot(h, inverse)
        full = complex_dot((inverse[0].T, -inverse[1].T), half)
        out[0] = full[0] / COUNT
        out[1] = full[1] / COUNT

    return pl.pallas_call(
        kernel,
        out_shape=jax.ShapeDtypeStruct((2, 128, 128), F32),
        compiler_params=params(),
        cost_estimate=pl.CostEstimate(flops=3_000_000_000, bytes_accessed=300_000, transcendentals=0),
        name="rayleigh",
    )(total, z)


def rotate(z, blocks):
    def kernel(z_ref, ref, out):
        top = jnp.concatenate([z_ref[0], z_ref[1]], axis=1)
        bottom = jnp.concatenate([-z_ref[1], z_ref[0]], axis=1)
        right = halves(jnp.concatenate([top, bottom], axis=0))
        for a in range(3):
            real, imag = slice(a * 128, a * 128 + 128), slice(384 + a * 128, 512 + a * 128)
            left = jnp.concatenate(
                [jnp.concatenate([ref[q, real, :], ref[q, imag, :]], axis=1) for q in range(TURN)], axis=0
            )
            found = dot3(halves(left), right)
            out[a] = found[:, 0:128]
            out[3 + a] = found[:, 128:256]

    return pl.pallas_call(
        kernel,
        grid=(8 // TURN,),
        in_specs=[
            pl.BlockSpec((2, 128, 128), lambda i: (0, 0, 0)),
            pl.BlockSpec((TURN, 768, 128), lambda i: (i, 0, 0)),
        ],
        out_specs=pl.BlockSpec((6, 128 * TURN, 128), lambda i: (0, i, 0)),
        out_shape=jax.ShapeDtypeStruct((6, 1024, 128), F32),
        compiler_params=params(),
        cost_estimate=pl.CostEstimate(flops=5_000_000_000, bytes_accessed=7_000_000, transcendentals=0),
        name="rotate",
    )(z, blocks)


def ring_pairs(step):
    return [(z * 8 + r, z * 8 + (r + step) % 8) for z in range(4) for r in range(8)]


def z_pairs(step):
    return [(i, (i + 8 * step) % 32) for i in range(32)]


def y_pairs(step):
    return ring_pairs(2 * step)


RINGS = [[z * 8 + r for r in range(8)] for z in range(4)]
CORES = [[2 * chip + core for chip in range(16)] for core in range(2)]
CORE_PAIRS = [(i, i ^ 1) for i in range(32)]


def move(value, pairs):
    return lax.ppermute(value, "sa", pairs)


def trade(value, groups=None):
    return lax.all_to_all(value, "sa", 0, 0, axis_index_groups=groups, tiled=True)


def spread(value, pairs):
    return [move(value, pairs(step)) for step in (2, 1, -1)]


def gathered(value, parts):
    return (value + parts[0]) + (parts[1] + parts[2])


def local(start, links, momenta, displace):
    device = lax.axis_index("sa")
    ring = device % 8

    u = trade(lay_out(start.reshape(6, 1024, 128), links.reshape(54, 32, 32)), RINGS)

    zs = (device // 8) * 8 + jnp.arange(8, dtype=jnp.int32)[None, :, None, None]
    ys = ring * 4 + jnp.arange(4, dtype=jnp.int32)[None, None, :, None]
    xs = jnp.arange(32, dtype=jnp.int32)[None, None, None, :]
    along_x = momenta[:, 0][:, None, None, None]
    along_y = momenta[:, 1][:, None, None, None]
    along_z = momenta[:, 2][:, None, None, None]
    angles = TWO_PI * (
        (along_x * xs % 32).astype(F32) / 32
        + (along_y * ys % 32).astype(F32) / 32
        + (along_z * zs % 32).astype(F32) / 32
    )
    angles = angles.reshape(NMOM, 8, 128)
    phases = jnp.stack([jnp.cos(angles), jnp.sin(angles)], axis=1).reshape(2 * NMOM, 8, 128)
    phases = jnp.transpose(phases, (1, 0, 2))

    cells = u[:, 0:768].reshape(8, 6, 128, 128)
    z_low, z_high = u[0, 0:768], u[7]
    y_low, y_high = cells[:, :, 0:32], cells[:, :, 96:128]
    before = mesh_links = z_links = None
    norms = []
    for step in range(3):
        weight = (1.0 if step else RANGE) * (2.0 if step else 1.0)
        z_down = move(z_high, z_pairs(1))
        z_up = move(z_low, z_pairs(-1))
        y_down = move(y_high, ring_pairs(1))
        y_up = move(y_low, ring_pairs(-1))
        if step == 0:
            z_links = z_down[768:840]
        found = interior(
            u,
            mesh_links,
            before,
            weight * (6.0 * ALPHA - BETA),
            weight * ALPHA,
            RANGE if step == 1 else 1.0,
            f"interior_{step}",
        )
        if step == 0:
            mesh_links = found[2]
        norms.append(found[1])
        fresh, y_low, y_high, z_low, z_high = boundary(
            found[0], mesh_links, (z_up, z_down, y_up, y_down), z_links, weight * ALPHA, f"boundary_{step}"
        )
        before, u = u, fresh

    z_up = move(z_low, z_pairs(-1))
    y_up = move(y_low, ring_pairs(-1))
    packed_gram, turned = gram(u, norms[1], norms[2])
    shared = packed_gram + move(packed_gram, CORE_PAIRS)
    ring_parts = spread(shared, y_pairs)
    right_x, x_hops = carry_x(u, turned, mesh_links)
    ring_parts, x_hops, z_up, y_up, u = lax.optimization_barrier((ring_parts, x_hops, z_up, y_up, u))
    back = trade(u, RINGS)
    shared = gathered(shared, ring_parts)
    z_parts = spread(shared, z_pairs)
    right_yz, packed_h = carry_yz(u, turned, mesh_links, z_up, y_up, x_hops, packed_gram)
    z_parts, packed_h = lax.optimization_barrier((z_parts, packed_h))
    total_gram = gathered(shared, z_parts)
    z = newton(total_gram)
    core = device % 2
    where = core.reshape(1).astype(jnp.int32)
    kept, given = elementals(where, z, turned, right_x, right_yz, phases, 0, 4, packed_h, 1, "elementals_0")
    first = kept + move(given, CORE_PAIRS)
    first, back, turned = lax.optimization_barrier((first, back, turned))
    first = jnp.sum(trade(first, CORES), axis=0)
    kept, given = elementals(where, z, turned, right_x, right_yz, phases, 4, 3, None, 2, "elementals_1")
    first, kept, given = lax.optimization_barrier((first, kept, given))
    share = jnp.broadcast_to(first[:, 3072:], (16, 4, 128))
    given = lax.dynamic_update_slice(given, share, (0, 0, 2432))
    second = lax.dynamic_update_slice(kept, share, (0, 0, 2304)) + move(given, CORE_PAIRS)
    second, back = lax.optimization_barrier((second, back))
    second = trade(second, CORES)
    mine, others = second[:, :, 2304:2432], second[:, :, 2432:]
    low, high = jnp.where(core == 0, mine, others), jnp.where(core == 0, others, mine)
    total = jnp.stack([low, high], axis=1).reshape(128, 128)
    sums = [first[:, :3072], jnp.sum(second[:, :, :2304], axis=0)]
    ritz = rayleigh(total, z)
    basis = rotate(z, back).reshape(start.shape)

    rows = jnp.concatenate([part.reshape(4, -1, 2, 128) for part in sums], axis=1)
    real, imag = rows[:, :, 0].reshape(-1, 128), rows[:, :, 1].reshape(-1, 128)
    left = jnp.concatenate([real, imag], axis=1)
    top = jnp.concatenate([z[0], z[1]], axis=1)
    bottom = jnp.concatenate([-z[1], z[0]], axis=1)
    phi = jnp.dot(left, jnp.concatenate([top, bottom], axis=0), precision=HIGHEST)
    phi = (phi * (1.0 / math.sqrt(32768.0))).reshape(4, NMOM, 3, 2, 128)
    slots = displace[:, None] == jnp.arange(3, dtype=displace.dtype)[None, :]
    phi = jnp.sum(jnp.where(slots[None, None, :, :, None, None], phi[:, :, None], 0.0), axis=3)
    return (basis, ritz, phi)


def solution(mesh):
    in_specs = (
        P("ta", None, "sa", None, None, None),
        P("ta", None, None, None, "sa", None, None),
        P(),
        P(),
    )
    out_specs = (
        P("ta", None, "sa", None, None, None),
        P("ta", None, None),
        P("sa", "ta", None, None, None),
    )
    return jax.shard_map(local, mesh=mesh, in_specs=in_specs, out_specs=out_specs, check_vma=False)
```

```python
import math

import jax
import jax.numpy as jnp
from jax import lax
from jax.experimental import pallas as pl
from jax.experimental.pallas import tpu as pltpu
from jax.sharding import PartitionSpec as P

NMOM = 7
ALPHA = 2.0 / 11.0
BETA = 13.0 / 11.0
EPS = 1e-06
TWO_PI = 2.0 * math.pi
RANGE = 2.0**40
COUNT = 196608.0
HIGHEST = lax.Precision.HIGHEST
F32 = jnp.float32
BF16 = jnp.bfloat16
LAY, STEP, FACE, GRAM, CARRY_X, CARRY_YZ, TURN = 4, 1, 4, 4, 2, 2, 4


def params(mebibytes):
    return pltpu.CompilerParams(vmem_limit_bytes=mebibytes * 1024 * 1024)


def link_of(rows, direction):
    def entry(part, a, b):
        lane = ((direction * 2 + part) * 3 + a) * 3 + b
        return jnp.broadcast_to(rows[:, lane : lane + 1], rows.shape)

    real = [[entry(0, a, b) for b in range(3)] for a in range(2)]
    imag = [[entry(1, a, b) for b in range(3)] for a in range(2)]
    third_real, third_imag = [], []
    for b in range(3):
        p, q = (b + 1) % 3, (b + 2) % 3
        first = real[0][p] * real[1][q] - imag[0][p] * imag[1][q]
        second = real[0][q] * real[1][p] - imag[0][q] * imag[1][p]
        third_real.append(first - second)
        first = real[0][p] * imag[1][q] + imag[0][p] * real[1][q]
        second = real[0][q] * imag[1][p] + imag[0][q] * real[1][p]
        third_imag.append(second - first)
    return [real + [third_real], imag + [third_imag]]


def forward(link, v):
    real, imag = [], []
    for a in range(3):
        r = i = None
        for b in range(3):
            x = link[0][a][b] * v[b] - link[1][a][b] * v[3 + b]
            y = link[0][a][b] * v[3 + b] + link[1][a][b] * v[b]
            r = x if r is None else r + x
            i = y if i is None else i + y
        real.append(r)
        imag.append(i)
    return real + imag


def backward(link, v):
    real, imag = [], []
    for a in range(3):
        r = i = None
        for b in range(3):
            x = link[0][b][a] * v[b] + link[1][b][a] * v[3 + b]
            y = link[0][b][a] * v[3 + b] - link[1][b][a] * v[b]
            r = x if r is None else r + x
            i = y if i is None else i + y
        real.append(r)
        imag.append(i)
    return real + imag


def add(first, second):
    return [a + b for a, b in zip(first, second)]


def lay_out(field, links):
    def kernel(field_ref, link_ref, out):
        for q in range(LAY):
            block = pl.program_id(0) * LAY + q
            for c in range(6):
                out[q, c * 128 : (c + 1) * 128, :] = field_ref[c, q * 128 : (q + 1) * 128, :]
            rows = [link_ref[:, pl.ds((4 * block + y + 31) % 32, 1), :].reshape(54, 32) for y in range(5)]
            out[q, 768:822, :] = jnp.concatenate(rows[1:], axis=1)
            out[q, 822:840, :] = jnp.concatenate([row[18:36] for row in rows[:4]], axis=1)

    return pl.pallas_call(
        kernel,
        grid=(8 // LAY,),
        in_specs=[
            pl.BlockSpec((6, 128 * LAY, 128), lambda q: (0, q, 0)),
            pl.BlockSpec((54, 32, 32), lambda q: (0, 0, 0)),
        ],
        out_specs=pl.BlockSpec((LAY, 840, 128), lambda q: (q, 0, 0)),
        out_shape=jax.ShapeDtypeStruct((8, 840, 128), F32),
        compiler_params=params(16),
        cost_estimate=pl.CostEstimate(flops=3_000_000_000, bytes_accessed=7_000_000, transcendentals=0),
        name="lay_out",
    )(field, links)


def cell(ref, c, at, z=0):
    return ref[z, c * 128 + at.start : c * 128 + at.stop, :]


def cell_flat(ref, c, at):
    return ref[c * 128 + at.start : c * 128 + at.stop, :]


def interior(u, links, before, c0, c1, cp, name):
    first = links is None

    def kernel(*refs):
        if first:
            here, above, out, norm, link_ref, px, wx, py, pz = refs
            for zz in range(STEP):
                rows = jnp.concatenate([here[zz, 768:840, :], jnp.zeros((56, 128), F32)], axis=0)
                link_ref[zz] = rows.T
        else:
            here, above, link_ref, before_ref, out, norm, px, wx, py, pz = refs
        z = pl.program_id(0)
        inside = jnp.where(z < 8 // STEP - 1, 1.0, 0.0).astype(F32)

        @pl.when(z == 0)
        def _():
            norm[...] = jnp.zeros_like(norm)
            pz[...] = jnp.zeros_like(pz)

        total = jnp.zeros((8, 128), F32)
        for zz in range(STEP):
            for y in range(4):
                row = y * 32
                for c in range(6):
                    px[c] = pltpu.roll(cell(here, c, slice(row, row + 32), zz), 31, 0)
                for g in range(4):
                    at = slice(row + 8 * g, row + 8 * g + 8)
                    own = slice(8 * g, 8 * g + 8)
                    rows = link_ref[zz, at, :]
                    v = [cell(here, c, at, zz) for c in range(6)]
                    if not first:
                        for c in range(6):
                            total = total + v[c] * v[c]
                    link = link_of(rows, 0)
                    hop = forward(link, [px[c, own, :] for c in range(6)])
                    side = backward(link, v)
                    for c in range(6):
                        wx[c, own, :] = side[c]
                    if y < 3:
                        link = link_of(rows, 1)
                        up = slice(at.start + 32, at.stop + 32)
                        hop = add(hop, forward(link, [cell(here, c, up, zz) for c in range(6)]))
                        side = backward(link, v)
                    if y > 0:
                        hop = add(hop, [py[c, own, :] for c in range(6)])
                    if y < 3:
                        for c in range(6):
                            py[c, own, :] = side[c]
                    link = link_of(rows, 2)
                    far = forward(link, [cell(here, c, at, zz + 1) if zz < STEP - 1 else cell(above, c, at) for c in range(6)])
                    hop = add(hop, far) if zz < STEP - 1 else [a + inside * b for a, b in zip(hop, far)]
                    hop = add(hop, [pz[c, at, :] for c in range(6)])
                    side = backward(link, v)
                    for c in range(6):
                        pz[c, at, :] = side[c]
                        value = c0 * v[c] - c1 * hop[c]
                        if not first:
                            value = value - cp * cell(before_ref, c, at, zz)
                        out[zz, c * 128 + at.start : c * 128 + at.stop, :] = value
                for c in range(6):
                    spot = slice(c * 128 + row, c * 128 + row + 32)
                    out[zz, spot, :] = out[zz, spot, :] - c1 * pltpu.roll(wx[c], 1, 0)
        norm[...] = norm[...] + total

    block = pl.BlockSpec((STEP, 768, 128), lambda z: (z, 0, 0))
    next_block = pl.BlockSpec((1, 768, 128), lambda z: (jnp.minimum(STEP * (z + 1), 7), 0, 0))
    link_block = pl.BlockSpec((STEP, 128, 128), lambda z: (z, 0, 0))
    out_specs = [block, pl.BlockSpec((8, 128), lambda z: (0, 0))]
    out_shape = [jax.ShapeDtypeStruct((8, 768, 128), F32), jax.ShapeDtypeStruct((8, 128), F32)]
    if first:
        in_specs = [pl.BlockSpec((STEP, 840, 128), lambda z: (z, 0, 0)), next_block]
        operands = [u, u]
        out_specs.append(link_block)
        out_shape.append(jax.ShapeDtypeStruct((8, 128, 128), F32))
    else:
        in_specs = [block, next_block, link_block, block]
        operands = [u, u, links, before]
    return pl.pallas_call(
        kernel,
        grid=(8 // STEP,),
        in_specs=in_specs,
        out_specs=out_specs,
        out_shape=out_shape,
        scratch_shapes=[
            pltpu.VMEM((6, 32, 128), F32),
            pltpu.VMEM((6, 32, 128), F32),
            pltpu.VMEM((6, 32, 128), F32),
            pltpu.VMEM((6, 128, 128), F32),
        ],
        compiler_params=params(12),
        cost_estimate=pl.CostEstimate(flops=12_000_000_000, bytes_accessed=12_000_000, transcendentals=0),
        name=name,
    )(*operands)


def boundary(partial, links, halo, z_links, c1, name):
    z_up, z_down, y_up, y_down = halo

    def kernel(part, link_ref, zu, zd, yu, yd, zl, out, y_low, y_high, z_low, z_high, turned):
        step = pl.program_id(0)

        def put(z, c, at, hop):
            spot = slice(c * 128 + at.start, c * 128 + at.stop)
            out[z, spot, :] = part[z, spot, :] - c1 * hop[c]

        def more(z, c, at, hop):
            spot = slice(c * 128 + at.start, c * 128 + at.stop)
            out[z, spot, :] = out[z, spot, :] - c1 * hop[c]

        for z in range(FACE):
            for g in range(4):
                own = slice(8 * g, 8 * g + 8)
                hop = backward(link_of(link_ref[z, own, :], 3), [yd[z, c, own, :] for c in range(6)])
                for c in range(6):
                    put(z, c, own, hop)
                at = slice(96 + 8 * g, 104 + 8 * g)
                hop = forward(link_of(link_ref[z, at, :], 1), [yu[z, c, own, :] for c in range(6)])
                for c in range(6):
                    put(z, c, at, hop)
            for c in range(6):
                spot = slice(c * 128 + 32, c * 128 + 96)
                out[z, spot, :] = part[z, spot, :]

        @pl.when(step == 0)
        def _():
            turned[...] = jnp.concatenate([zl[...], jnp.zeros((56, 128), F32)], axis=0).T
            for g in range(16):
                at = slice(8 * g, 8 * g + 8)
                hop = backward(link_of(turned[at, :], 2), [zd[c * 128 + at.start : c * 128 + at.stop, :] for c in range(6)])
                for c in range(6):
                    more(0, c, at, hop)
            z_low[...] = out[0]

        @pl.when(step == 8 // FACE - 1)
        def _():
            for g in range(16):
                at = slice(8 * g, 8 * g + 8)
                hop = forward(
                    link_of(link_ref[FACE - 1, at, :], 2), [zu[c * 128 + at.start : c * 128 + at.stop, :] for c in range(6)]
                )
                for c in range(6):
                    more(FACE - 1, c, at, hop)
            z_high[...] = out[FACE - 1]

        for z in range(FACE):
            for c in range(6):
                y_low[z, c] = out[z, c * 128 : c * 128 + 32, :]
                y_high[z, c] = out[z, c * 128 + 96 : c * 128 + 128, :]

    block = pl.BlockSpec((FACE, 768, 128), lambda z: (z, 0, 0))
    y_face = pl.BlockSpec((FACE, 6, 32, 128), lambda z: (z, 0, 0, 0))
    z_face = pl.BlockSpec((768, 128), lambda z: (0, 0))
    return pl.pallas_call(
        kernel,
        grid=(8 // FACE,),
        in_specs=[
            block,
            pl.BlockSpec((FACE, 128, 128), lambda z: (z, 0, 0)),
            z_face,
            z_face,
            y_face,
            y_face,
            pl.BlockSpec((72, 128), lambda z: (0, 0)),
        ],
        out_specs=(block, y_face, y_face, z_face, z_face),
        out_shape=(
            jax.ShapeDtypeStruct((8, 768, 128), F32),
            jax.ShapeDtypeStruct((8, 6, 32, 128), F32),
            jax.ShapeDtypeStruct((8, 6, 32, 128), F32),
            jax.ShapeDtypeStruct((768, 128), F32),
            jax.ShapeDtypeStruct((768, 128), F32),
        ),
        scratch_shapes=[pltpu.VMEM((128, 128), F32)],
        compiler_params=params(20),
        cost_estimate=pl.CostEstimate(flops=6_000_000_000, bytes_accessed=9_000_000, transcendentals=0),
        name=name,
    )(partial, links, z_up, z_down, y_up, y_down, z_links)


def halves(value):
    high = value.astype(BF16)
    return high, (value - high.astype(F32)).astype(BF16)


def dot3(left, right):
    def dot(a, b):
        return jnp.dot(a, b, preferred_element_type=F32)

    return dot(left[0], right[0]) + (dot(left[0], right[1]) + dot(left[1], right[0]))


def columns(ref, z, part):
    return jnp.concatenate([cell(ref, 3 * part + a, slice(0, 128), z) for a in range(3)], axis=1)


def gram(u, first_norm, second_norm):
    def kernel(here, n1, n2, packed, turned, acc):
        step = pl.program_id(0)

        @pl.when(step == 0)
        def _():
            acc[...] = jnp.zeros_like(acc)

        for z in range(GRAM):
            for c in range(6):
                turned[z, c * 128 : (c + 1) * 128, :] = cell(here, c, slice(0, 128), z).T
        left = jnp.concatenate(
            [jnp.concatenate([columns(turned, z, part) for z in range(GRAM)], axis=1) for part in range(2)], axis=0
        )
        right = jnp.concatenate([here[z, 0:384, :] for z in range(GRAM)], axis=0)
        right = jnp.concatenate([right, jnp.concatenate([here[z, 384:768, :] for z in range(GRAM)], axis=0)], axis=1)
        acc[...] = acc[...] + dot3(halves(left), halves(right))

        @pl.when(step == 8 // GRAM - 1)
        def _():
            real = acc[0:128, 0:128] + acc[128:256, 128:256]
            imag = acc[0:128, 128:256] - acc[128:256, 0:128]
            row = lax.broadcasted_iota(jnp.int32, (128, 128), 0)
            column = lax.broadcasted_iota(jnp.int32, (128, 128), 1)
            packed[0:128, :] = jnp.where(column >= row, real, imag)
            packed[128:136, :] = n1[...]
            packed[136:144, :] = n2[...]

    fixed = pl.BlockSpec((8, 128), lambda z: (0, 0))
    return pl.pallas_call(
        kernel,
        grid=(8 // GRAM,),
        in_specs=[pl.BlockSpec((GRAM, 768, 128), lambda z: (z, 0, 0)), fixed, fixed],
        out_specs=(pl.BlockSpec((144, 128), lambda z: (0, 0)), pl.BlockSpec((GRAM, 768, 128), lambda z: (z, 0, 0))),
        out_shape=(jax.ShapeDtypeStruct((144, 128), F32), jax.ShapeDtypeStruct((8, 768, 128), F32)),
        scratch_shapes=[pltpu.VMEM((256, 256), F32)],
        compiler_params=params(28),
        cost_estimate=pl.CostEstimate(flops=4_000_000_000, bytes_accessed=3_000_000, transcendentals=0),
        name="gram",
    )(u, first_norm, second_norm)


def put_halves(wide, zz, carry, slots):
    for a in range(3):
        for k in range(slots):
            for part in range(2):
                hi, lo = halves(carry[k, 3 * part + a])
                spot = (k * 2 + part) * 128
                wide[zz, a * 128 : (a + 1) * 128, spot : spot + 128] = hi
                wide[zz, 384 + a * 128 : 512 + a * 128, spot : spot + 128] = lo
                wide[zz, 768 + a * 128 : 896 + a * 128, spot : spot + 128] = hi


def add_hops(acc, turned, zz, carry, slots):
    left = jnp.concatenate([columns(turned, zz, part) for part in range(2)], axis=0)

    def summed(c):
        return carry[0, c] if slots == 1 else carry[0, c] + carry[1, c]

    right = jnp.concatenate(
        [jnp.concatenate([summed(a), summed(3 + a)], axis=1) for a in range(3)], axis=0
    )
    acc[...] = acc[...] + dot3(halves(left), halves(right))


def carry_x(u, turned, links):
    def kernel(here, turned, link_ref, wide, hops, px, carry, acc):
        z = pl.program_id(0)

        @pl.when(z == 0)
        def _():
            acc[...] = jnp.zeros_like(acc)

        for zz in range(CARRY_X):
            for y in range(4):
                row = y * 32
                for c in range(6):
                    px[c] = pltpu.roll(cell(here, c, slice(row, row + 32), zz), 31, 0)
                for g in range(4):
                    at = slice(row + 8 * g, row + 8 * g + 8)
                    own = slice(8 * g, 8 * g + 8)
                    found = forward(link_of(link_ref[zz, at, :], 0), [px[c, own, :] for c in range(6)])
                    for c in range(6):
                        carry[0, c, at, :] = found[c]
            put_halves(wide, zz, carry, 1)
            add_hops(acc, turned, zz, carry, 1)

        @pl.when(z == 8 // CARRY_X - 1)
        def _():
            hops[...] = acc[...]

    block = pl.BlockSpec((CARRY_X, 768, 128), lambda z: (z, 0, 0))
    return pl.pallas_call(
        kernel,
        grid=(8 // CARRY_X,),
        in_specs=[block, block, pl.BlockSpec((CARRY_X, 128, 128), lambda z: (z, 0, 0))],
        out_specs=(pl.BlockSpec((CARRY_X, 1152, 256), lambda z: (z, 0, 0)), pl.BlockSpec((256, 256), lambda z: (0, 0))),
        out_shape=(jax.ShapeDtypeStruct((8, 1152, 256), BF16), jax.ShapeDtypeStruct((256, 256), F32)),
        scratch_shapes=[
            pltpu.VMEM((6, 32, 128), F32),
            pltpu.VMEM((1, 6, 128, 128), F32),
            pltpu.VMEM((256, 256), F32),
        ],
        compiler_params=params(20),
        cost_estimate=pl.CostEstimate(flops=7_000_000_000, bytes_accessed=8_000_000, transcendentals=0),
        name="carry_x",
    )(u, turned, links)


def carry_yz(u, turned, links, z_up, y_up, x_hops, packed_gram):
    def kernel(here, turned, above, link_ref, zu, yu, hops_ref, gram_ref, wide, packed, carry, acc):
        z = pl.program_id(0)
        last = z == 8 // CARRY_YZ - 1

        @pl.when(z == 0)
        def _():
            acc[...] = hops_ref[...]

        for zz in range(CARRY_YZ):
            for y in range(4):
                row = y * 32
                for g in range(4):
                    at = slice(row + 8 * g, row + 8 * g + 8)
                    own = slice(8 * g, 8 * g + 8)
                    rows = link_ref[zz, at, :]
                    if y < 3:
                        source = [cell(here, c, slice(at.start + 32, at.stop + 32), zz) for c in range(6)]
                    else:
                        source = [yu[zz, c, own, :] for c in range(6)]
                    found = forward(link_of(rows, 1), source)
                    for c in range(6):
                        carry[0, c, at, :] = found[c]
                    if zz < CARRY_YZ - 1:
                        source = [cell(here, c, at, zz + 1) for c in range(6)]
                    else:
                        source = [jnp.where(last, cell_flat(zu, c, at), cell(above, c, at)) for c in range(6)]
                    found = forward(link_of(rows, 2), source)
                    for c in range(6):
                        carry[1, c, at, :] = found[c]
            put_halves(wide, zz, carry, 2)
            add_hops(acc, turned, zz, carry, 2)

        @pl.when(last)
        def _():
            gram_real, gram_imag = hermitian(gram_ref[0:128, :])
            hop_real = acc[0:128, 0:128] + acc[128:256, 128:256]
            hop_imag = acc[0:128, 128:256] - acc[128:256, 0:128]
            real = 6.0 * gram_real - (hop_real + hop_real.T)
            imag = 6.0 * gram_imag - (hop_imag - hop_imag.T)
            row = lax.broadcasted_iota(jnp.int32, (128, 128), 0)
            column = lax.broadcasted_iota(jnp.int32, (128, 128), 1)
            packed[...] = jnp.where(column >= row, real, imag)

    return pl.pallas_call(
        kernel,
        grid=(8 // CARRY_YZ,),
        in_specs=[
            pl.BlockSpec((CARRY_YZ, 768, 128), lambda z: (z, 0, 0)),
            pl.BlockSpec((CARRY_YZ, 768, 128), lambda z: (z, 0, 0)),
            pl.BlockSpec((1, 768, 128), lambda z: (jnp.minimum(CARRY_YZ * (z + 1), 7), 0, 0)),
            pl.BlockSpec((CARRY_YZ, 128, 128), lambda z: (z, 0, 0)),
            pl.BlockSpec((768, 128), lambda z: (0, 0)),
            pl.BlockSpec((CARRY_YZ, 6, 32, 128), lambda z: (z, 0, 0, 0)),
            pl.BlockSpec((256, 256), lambda z: (0, 0)),
            pl.BlockSpec((144, 128), lambda z: (0, 0)),
        ],
        out_specs=(pl.BlockSpec((CARRY_YZ, 1152, 512), lambda z: (z, 0, 0)), pl.BlockSpec((128, 128), lambda z: (0, 0))),
        out_shape=(jax.ShapeDtypeStruct((8, 1152, 512), BF16), jax.ShapeDtypeStruct((128, 128), F32)),
        scratch_shapes=[pltpu.VMEM((2, 6, 128, 128), F32), pltpu.VMEM((256, 256), F32)],
        compiler_params=params(24),
        cost_estimate=pl.CostEstimate(flops=12_000_000_000, bytes_accessed=16_000_000, transcendentals=0),
        name="carry_yz",
    )(u, turned, u, links, z_up, y_up, x_hops, packed_gram)


def elementals(core, z, turned_u, right_x, right_yz, phases, first, count, extra, spare, name):
    def kernel(core_ref, z_ref, here, rx, ryz, phase, *refs):
        kept, given, left, acc = refs[-4:]
        step = pl.program_id(0)
        own = core_ref[0] == 0

        @pl.when(step == 0)
        def _():
            acc[...] = jnp.zeros_like(acc)

        turned = [[here[zz, c * 128 : (c + 1) * 128, :] for c in range(6)] for zz in range(2)]
        minus = [[-turned[zz][a] for a in range(3)] for zz in range(2)]

        def build(m):
            mode = 2 * (first + m)
            for zz in range(2):
                cosine = phase[zz, mode : mode + 1, :]
                sine = phase[zz, mode + 1 : mode + 2, :]
                for a in range(3):
                    real, imag = turned[zz][a], turned[zz][3 + a]
                    spot = zz * 1152 + a * 128
                    pair = (real * cosine - imag * sine, minus[zz][a] * sine - imag * cosine)
                    for part in range(2):
                        hi, lo = halves(pair[part])
                        rows = slice(m * 256 + part * 128, m * 256 + part * 128 + 128)
                        left[rows, spot : spot + 128] = hi
                        left[rows, spot + 384 : spot + 512] = hi
                        left[rows, spot + 768 : spot + 896] = lo

        def multiply(low, high):
            done = slice(low * 256, high * 256)
            found = jnp.dot(left[done, :], rx[...].reshape(2304, 256), preferred_element_type=F32)
            acc[done, 0:256] = acc[done, 0:256] + found
            found = jnp.dot(left[done, :], ryz[...].reshape(2304, 512), preferred_element_type=F32)
            acc[done, 256:768] = acc[done, 256:768] + found

        for m in range(2):
            build(m)
        for m in range(2, count):
            build(m)
        for low in range(0, count, 2):
            multiply(low, min(low + 2, count))

        @pl.when(step == 3)
        def _():
            def share(lanes, value):
                for chip in range(16):
                    low, high = value[chip * 8 : chip * 8 + 4], value[chip * 8 + 4 : chip * 8 + 8]
                    kept[chip, :, lanes] = jnp.where(own, low, high)
                    given[chip, :, lanes] = jnp.where(own, high, low)

            width = spare * 128
            lanes = slice(count * 768, count * 768 + width)
            share(lanes, jnp.zeros((128, width), F32) if extra is None else refs[0][...])
            turn = halves(jnp.concatenate([z_ref[0].T, z_ref[1].T], axis=0))
            for m in range(count):
                real, imag = slice(m * 256, m * 256 + 128), slice(m * 256 + 128, m * 256 + 256)
                for k in range(3):
                    one, two = slice(256 * k, 256 * k + 128), slice(256 * k + 128, 256 * k + 256)
                    raw = [acc[real, one] - acc[imag, two], acc[real, two] + acc[imag, one]]
                    found = dot3(turn, halves(jnp.concatenate(raw, axis=1)))
                    place = (m * 3 + k) * 256
                    share(slice(place, place + 128), found[0:128, 0:128] + found[128:256, 128:256])
                    share(slice(place + 128, place + 256), found[0:128, 128:256] - found[128:256, 0:128])

    shape = (16, 4, count * 768 + spare * 128)
    return pl.pallas_call(
        kernel,
        grid=(4,),
        in_specs=[
            pl.BlockSpec(memory_space=pltpu.SMEM),
            pl.BlockSpec((2, 128, 128), lambda z: (0, 0, 0)),
            pl.BlockSpec((2, 768, 128), lambda z: (z, 0, 0)),
            pl.BlockSpec((2, 1152, 256), lambda z: (z, 0, 0)),
            pl.BlockSpec((2, 1152, 512), lambda z: (z, 0, 0)),
            pl.BlockSpec((2, 14, 128), lambda z: (z, 0, 0)),
        ]
        + [pl.BlockSpec((128, 128), lambda z: (0, 0))] * (extra is not None),
        out_specs=[pl.BlockSpec(shape, lambda z: (0, 0, 0))] * 2,
        out_shape=[jax.ShapeDtypeStruct(shape, F32)] * 2,
        scratch_shapes=[
            pltpu.VMEM((count * 256, 2304), BF16),
            pltpu.VMEM((count * 256, 768), F32),
        ],
        compiler_params=params(40),
        cost_estimate=pl.CostEstimate(flops=5_500_000_000 * count, bytes_accessed=16_000_000, transcendentals=0),
        name=name,
    )(core, z, turned_u, right_x, right_yz, phases, *([] if extra is None else [extra]))


def hermitian(packed):
    row = lax.broadcasted_iota(jnp.int32, (128, 128), 0)
    column = lax.broadcasted_iota(jnp.int32, (128, 128), 1)
    diagonal = jnp.where(column == row, packed, 0.0)
    upper = jnp.where(column > row, packed, 0.0)
    lower = jnp.where(column < row, packed, 0.0)
    return upper + upper.T + diagonal, lower - lower.T


def complex_dot(left, right):
    top = jnp.concatenate([left[0], -left[1]], axis=1)
    bottom = jnp.concatenate([left[1], left[0]], axis=1)
    both = dot3(halves(jnp.concatenate([top, bottom], axis=0)), halves(jnp.concatenate([right[0], right[1]], axis=0)))
    return both[0:128], both[128:256]


def newton(total):
    def kernel(ref, z_out):
        row = lax.broadcasted_iota(jnp.int32, (128, 128), 0)
        column = lax.broadcasted_iota(jnp.int32, (128, 128), 1)
        identity = jnp.where(row == column, 1.0, 0.0).astype(F32)
        g_real, g_imag = hermitian(ref[0:128, :])
        shrink = 1.0 / (RANGE * RANGE)
        n1 = jnp.sum(ref[128:136, :], axis=0, keepdims=True) * shrink / COUNT
        n2 = jnp.sum(ref[136:144, :], axis=0, keepdims=True) * shrink / COUNT
        n3 = jnp.sum(jnp.where(row == column, g_real, 0.0), axis=0, keepdims=True) * shrink / COUNT
        scale = lax.rsqrt(n1 + EPS)
        scale = scale * lax.rsqrt(scale * scale * n2 + EPS)
        scale = scale * lax.rsqrt(scale * scale * n3 + EPS)
        scale = jnp.broadcast_to(scale * (1.0 / RANGE), (128, 128))
        side = scale.T
        y = (side * g_real * scale / COUNT, side * g_imag * scale / COUNT)
        inverse = None
        for step in range(3):
            middle = y if inverse is None else complex_dot(inverse, y)
            factor = (1.5 * identity - 0.5 * middle[0], -0.5 * middle[1])
            if step < 2:
                y = complex_dot(y, factor)
            inverse = factor if inverse is None else complex_dot(factor, inverse)
        z_out[0] = side * inverse[0]
        z_out[1] = side * inverse[1]

    return pl.pallas_call(
        kernel,
        out_shape=jax.ShapeDtypeStruct((2, 128, 128), F32),
        compiler_params=params(12),
        cost_estimate=pl.CostEstimate(flops=5_000_000_000, bytes_accessed=300_000, transcendentals=0),
        name="newton",
    )(total)


def rayleigh(total, z):
    def kernel(ref, z_ref, out):
        h = hermitian(ref[...])
        inverse = (z_ref[0], z_ref[1])
        half = complex_dot(h, inverse)
        full = complex_dot((inverse[0].T, -inverse[1].T), half)
        out[0] = full[0] / COUNT
        out[1] = full[1] / COUNT

    return pl.pallas_call(
        kernel,
        out_shape=jax.ShapeDtypeStruct((2, 128, 128), F32),
        compiler_params=params(12),
        cost_estimate=pl.CostEstimate(flops=3_000_000_000, bytes_accessed=300_000, transcendentals=0),
        name="rayleigh",
    )(total, z)


def rotate(z, blocks):
    def kernel(z_ref, ref, out):
        top = jnp.concatenate([z_ref[0], z_ref[1]], axis=1)
        bottom = jnp.concatenate([-z_ref[1], z_ref[0]], axis=1)
        right = halves(jnp.concatenate([top, bottom], axis=0))
        for a in range(3):
            real, imag = slice(a * 128, a * 128 + 128), slice(384 + a * 128, 512 + a * 128)
            left = jnp.concatenate(
                [jnp.concatenate([ref[q, real, :], ref[q, imag, :]], axis=1) for q in range(TURN)], axis=0
            )
            found = dot3(halves(left), right)
            out[a] = found[:, 0:128]
            out[3 + a] = found[:, 128:256]

    return pl.pallas_call(
        kernel,
        grid=(8 // TURN,),
        in_specs=[
            pl.BlockSpec((2, 128, 128), lambda i: (0, 0, 0)),
            pl.BlockSpec((TURN, 768, 128), lambda i: (i, 0, 0)),
        ],
        out_specs=pl.BlockSpec((6, 128 * TURN, 128), lambda i: (0, i, 0)),
        out_shape=jax.ShapeDtypeStruct((6, 1024, 128), F32),
        compiler_params=params(24),
        cost_estimate=pl.CostEstimate(flops=5_000_000_000, bytes_accessed=7_000_000, transcendentals=0),
        name="rotate",
    )(z, blocks)


def ring_pairs(step):
    return [(z * 8 + r, z * 8 + (r + step) % 8) for z in range(4) for r in range(8)]


def z_pairs(step):
    return [(i, (i + 8 * step) % 32) for i in range(32)]


def y_pairs(step):
    return ring_pairs(2 * step)


RINGS = [[z * 8 + r for r in range(8)] for z in range(4)]
CORES = [[2 * chip + core for chip in range(16)] for core in range(2)]
CORE_PAIRS = [(i, i ^ 1) for i in range(32)]


def move(value, pairs):
    return lax.ppermute(value, "sa", pairs)


def trade(value, groups=None):
    return lax.all_to_all(value, "sa", 0, 0, axis_index_groups=groups, tiled=True)


def spread(value, pairs):
    return [move(value, pairs(step)) for step in (2, 1, -1)]


def gathered(value, parts):
    return (value + parts[0]) + (parts[1] + parts[2])


def local(start, links, momenta, displace):
    device = lax.axis_index("sa")
    ring = device % 8

    u = trade(lay_out(start.reshape(6, 1024, 128), links.reshape(54, 32, 32)), RINGS)

    zs = (device // 8) * 8 + jnp.arange(8, dtype=jnp.int32)[None, :, None, None]
    ys = ring * 4 + jnp.arange(4, dtype=jnp.int32)[None, None, :, None]
    xs = jnp.arange(32, dtype=jnp.int32)[None, None, None, :]
    along_x = momenta[:, 0][:, None, None, None]
    along_y = momenta[:, 1][:, None, None, None]
    along_z = momenta[:, 2][:, None, None, None]
    angles = TWO_PI * (
        (along_x * xs % 32).astype(F32) / 32
        + (along_y * ys % 32).astype(F32) / 32
        + (along_z * zs % 32).astype(F32) / 32
    )
    angles = angles.reshape(NMOM, 8, 128)
    phases = jnp.stack([jnp.cos(angles), jnp.sin(angles)], axis=1).reshape(2 * NMOM, 8, 128)
    phases = jnp.transpose(phases, (1, 0, 2))

    cells = u[:, 0:768].reshape(8, 6, 128, 128)
    z_low, z_high = u[0, 0:768], u[7]
    y_low, y_high = cells[:, :, 0:32], cells[:, :, 96:128]
    before = mesh_links = z_links = None
    norms = []
    for step in range(3):
        weight = (1.0 if step else RANGE) * (2.0 if step else 1.0)
        z_down = move(z_high, z_pairs(1))
        z_up = move(z_low, z_pairs(-1))
        y_down = move(y_high, ring_pairs(1))
        y_up = move(y_low, ring_pairs(-1))
        if step == 0:
            z_links = z_down[768:840]
        found = interior(
            u,
            mesh_links,
            before,
            weight * (6.0 * ALPHA - BETA),
            weight * ALPHA,
            RANGE if step == 1 else 1.0,
            f"interior_{step}",
        )
        if step == 0:
            mesh_links = found[2]
        norms.append(found[1])
        fresh, y_low, y_high, z_low, z_high = boundary(
            found[0], mesh_links, (z_up, z_down, y_up, y_down), z_links, weight * ALPHA, f"boundary_{step}"
        )
        before, u = u, fresh

    z_up = move(z_low, z_pairs(-1))
    y_up = move(y_low, ring_pairs(-1))
    packed_gram, turned = gram(u, norms[1], norms[2])
    shared = packed_gram + move(packed_gram, CORE_PAIRS)
    ring_parts = spread(shared, y_pairs)
    right_x, x_hops = carry_x(u, turned, mesh_links)
    ring_parts, x_hops, z_up, y_up, u = lax.optimization_barrier((ring_parts, x_hops, z_up, y_up, u))
    back = trade(u, RINGS)
    shared = gathered(shared, ring_parts)
    z_parts = spread(shared, z_pairs)
    right_yz, packed_h = carry_yz(u, turned, mesh_links, z_up, y_up, x_hops, packed_gram)
    z_parts, packed_h = lax.optimization_barrier((z_parts, packed_h))
    total_gram = gathered(shared, z_parts)
    z = newton(total_gram)
    core = device % 2
    where = core.reshape(1).astype(jnp.int32)
    kept, given = elementals(where, z, turned, right_x, right_yz, phases, 0, 4, packed_h, 1, "elementals_0")
    first = kept + move(given, CORE_PAIRS)
    first, back, turned = lax.optimization_barrier((first, back, turned))
    first = jnp.sum(trade(first, CORES), axis=0)
    kept, given = elementals(where, z, turned, right_x, right_yz, phases, 4, 3, None, 2, "elementals_1")
    first, kept, given = lax.optimization_barrier((first, kept, given))
    share = jnp.broadcast_to(first[:, 3072:], (16, 4, 128))
    given = lax.dynamic_update_slice(given, share, (0, 0, 2432))
    second = lax.dynamic_update_slice(kept, share, (0, 0, 2304)) + move(given, CORE_PAIRS)
    second, back = lax.optimization_barrier((second, back))
    second = trade(second, CORES)
    mine, others = second[:, :, 2304:2432], second[:, :, 2432:]
    low, high = jnp.where(core == 0, mine, others), jnp.where(core == 0, others, mine)
    total = jnp.stack([low, high], axis=1).reshape(128, 128)
    sums = [first[:, :3072], jnp.sum(second[:, :, :2304], axis=0)]
    ritz = rayleigh(total, z)
    basis = rotate(z, back).reshape(start.shape)

    rows = jnp.concatenate([part.reshape(4, -1, 2, 128) for part in sums], axis=1)
    real, imag = rows[:, :, 0].reshape(-1, 128), rows[:, :, 1].reshape(-1, 128)
    left = jnp.concatenate([real, imag], axis=1)
    top = jnp.concatenate([z[0], z[1]], axis=1)
    bottom = jnp.concatenate([-z[1], z[0]], axis=1)
    phi = jnp.dot(left, jnp.concatenate([top, bottom], axis=0), precision=HIGHEST)
    phi = (phi * (1.0 / math.sqrt(32768.0))).reshape(4, NMOM, 3, 2, 128)
    slots = displace[:, None] == jnp.arange(3, dtype=displace.dtype)[None, :]
    phi = jnp.sum(jnp.where(slots[None, None, :, :, None, None], phi[:, :, None], 0.0), axis=3)
    return (basis, ritz, phi)


def solution(mesh):
    in_specs = (
        P("ta", None, "sa", None, None, None),
        P("ta", None, None, None, "sa", None, None),
        P(),
        P(),
    )
    out_specs = (
        P("ta", None, "sa", None, None, None),
        P("ta", None, None),
        P("sa", "ta", None, None, None),
    )
    return jax.shard_map(local, mesh=mesh, in_specs=in_specs, out_specs=out_specs, check_vma=False)
```

```python
import math

import jax
import jax.numpy as jnp
from jax import lax
from jax.experimental import pallas as pl
from jax.experimental.pallas import tpu as pltpu
from jax.sharding import PartitionSpec as P

NMOM = 7
ALPHA = 2.0 / 11.0
BETA = 13.0 / 11.0
EPS = 1e-06
TWO_PI = 2.0 * math.pi
RANGE = 2.0**40
COUNT = 196608.0
HIGHEST = lax.Precision.HIGHEST
F32 = jnp.float32
BF16 = jnp.bfloat16
LAY, STEP, FACE, GRAM, CARRY_X, CARRY_YZ, TURN = 4, 1, 4, 4, 2, 2, 4


def params(mebibytes):
    return pltpu.CompilerParams(vmem_limit_bytes=mebibytes * 1024 * 1024)


def link_of(rows, direction):
    def entry(part, a, b):
        lane = ((direction * 2 + part) * 3 + a) * 3 + b
        return jnp.broadcast_to(rows[:, lane : lane + 1], rows.shape)

    real = [[entry(0, a, b) for b in range(3)] for a in range(2)]
    imag = [[entry(1, a, b) for b in range(3)] for a in range(2)]
    third_real, third_imag = [], []
    for b in range(3):
        p, q = (b + 1) % 3, (b + 2) % 3
        first = real[0][p] * real[1][q] - imag[0][p] * imag[1][q]
        second = real[0][q] * real[1][p] - imag[0][q] * imag[1][p]
        third_real.append(first - second)
        first = real[0][p] * imag[1][q] + imag[0][p] * real[1][q]
        second = real[0][q] * imag[1][p] + imag[0][q] * real[1][p]
        third_imag.append(second - first)
    return [real + [third_real], imag + [third_imag]]


def forward(link, v):
    real, imag = [], []
    for a in range(3):
        r = i = None
        for b in range(3):
            x = link[0][a][b] * v[b] - link[1][a][b] * v[3 + b]
            y = link[0][a][b] * v[3 + b] + link[1][a][b] * v[b]
            r = x if r is None else r + x
            i = y if i is None else i + y
        real.append(r)
        imag.append(i)
    return real + imag


def backward(link, v):
    real, imag = [], []
    for a in range(3):
        r = i = None
        for b in range(3):
            x = link[0][b][a] * v[b] + link[1][b][a] * v[3 + b]
            y = link[0][b][a] * v[3 + b] - link[1][b][a] * v[b]
            r = x if r is None else r + x
            i = y if i is None else i + y
        real.append(r)
        imag.append(i)
    return real + imag


def add(first, second):
    return [a + b for a, b in zip(first, second)]


def lay_out(field, links):
    def kernel(field_ref, link_ref, out):
        for q in range(LAY):
            block = pl.program_id(0) * LAY + q
            for c in range(6):
                out[q, c * 128 : (c + 1) * 128, :] = field_ref[c, q * 128 : (q + 1) * 128, :]
            rows = [link_ref[:, pl.ds((4 * block + y + 31) % 32, 1), :].reshape(54, 32) for y in range(5)]
            out[q, 768:822, :] = jnp.concatenate(rows[1:], axis=1)
            out[q, 822:840, :] = jnp.concatenate([row[18:36] for row in rows[:4]], axis=1)

    return pl.pallas_call(
        kernel,
        grid=(8 // LAY,),
        in_specs=[
            pl.BlockSpec((6, 128 * LAY, 128), lambda q: (0, q, 0)),
            pl.BlockSpec((54, 32, 32), lambda q: (0, 0, 0)),
        ],
        out_specs=pl.BlockSpec((LAY, 840, 128), lambda q: (q, 0, 0)),
        out_shape=jax.ShapeDtypeStruct((8, 840, 128), F32),
        compiler_params=params(16),
        cost_estimate=pl.CostEstimate(flops=3_000_000_000, bytes_accessed=7_000_000, transcendentals=0),
        name="lay_out",
    )(field, links)


def cell(ref, c, at, z=0):
    return ref[z, c * 128 + at.start : c * 128 + at.stop, :]


def cell_flat(ref, c, at):
    return ref[c * 128 + at.start : c * 128 + at.stop, :]


def interior(u, links, before, c0, c1, cp, name):
    first = links is None

    def kernel(*refs):
        if first:
            here, above, out, norm, link_ref, px, wx, py, pz = refs
            for zz in range(STEP):
                rows = jnp.concatenate([here[zz, 768:840, :], jnp.zeros((56, 128), F32)], axis=0)
                link_ref[zz] = rows.T
        else:
            here, above, link_ref, before_ref, out, norm, px, wx, py, pz = refs
        z = pl.program_id(0)
        inside = jnp.where(z < 8 // STEP - 1, 1.0, 0.0).astype(F32)

        @pl.when(z == 0)
        def _():
            norm[...] = jnp.zeros_like(norm)
            pz[...] = jnp.zeros_like(pz)

        total = jnp.zeros((8, 128), F32)
        for zz in range(STEP):
            for y in range(4):
                row = y * 32
                for c in range(6):
                    px[c] = pltpu.roll(cell(here, c, slice(row, row + 32), zz), 31, 0)
                for g in range(4):
                    at = slice(row + 8 * g, row + 8 * g + 8)
                    own = slice(8 * g, 8 * g + 8)
                    rows = link_ref[zz, at, :]
                    v = [cell(here, c, at, zz) for c in range(6)]
                    if not first:
                        for c in range(6):
                            total = total + v[c] * v[c]
                    link = link_of(rows, 0)
                    hop = forward(link, [px[c, own, :] for c in range(6)])
                    side = backward(link, v)
                    for c in range(6):
                        wx[c, own, :] = side[c]
                    if y < 3:
                        link = link_of(rows, 1)
                        up = slice(at.start + 32, at.stop + 32)
                        hop = add(hop, forward(link, [cell(here, c, up, zz) for c in range(6)]))
                        side = backward(link, v)
                    if y > 0:
                        hop = add(hop, [py[c, own, :] for c in range(6)])
                    if y < 3:
                        for c in range(6):
                            py[c, own, :] = side[c]
                    link = link_of(rows, 2)
                    far = forward(link, [cell(here, c, at, zz + 1) if zz < STEP - 1 else cell(above, c, at) for c in range(6)])
                    hop = add(hop, far) if zz < STEP - 1 else [a + inside * b for a, b in zip(hop, far)]
                    hop = add(hop, [pz[c, at, :] for c in range(6)])
                    side = backward(link, v)
                    for c in range(6):
                        pz[c, at, :] = side[c]
                        value = c0 * v[c] - c1 * hop[c]
                        if not first:
                            value = value - cp * cell(before_ref, c, at, zz)
                        out[zz, c * 128 + at.start : c * 128 + at.stop, :] = value
                for c in range(6):
                    spot = slice(c * 128 + row, c * 128 + row + 32)
                    out[zz, spot, :] = out[zz, spot, :] - c1 * pltpu.roll(wx[c], 1, 0)
        norm[...] = norm[...] + total

    block = pl.BlockSpec((STEP, 768, 128), lambda z: (z, 0, 0))
    next_block = pl.BlockSpec((1, 768, 128), lambda z: (jnp.minimum(STEP * (z + 1), 7), 0, 0))
    link_block = pl.BlockSpec((STEP, 128, 128), lambda z: (z, 0, 0))
    out_specs = [block, pl.BlockSpec((8, 128), lambda z: (0, 0))]
    out_shape = [jax.ShapeDtypeStruct((8, 768, 128), F32), jax.ShapeDtypeStruct((8, 128), F32)]
    if first:
        in_specs = [pl.BlockSpec((STEP, 840, 128), lambda z: (z, 0, 0)), next_block]
        operands = [u, u]
        out_specs.append(link_block)
        out_shape.append(jax.ShapeDtypeStruct((8, 128, 128), F32))
    else:
        in_specs = [block, next_block, link_block, block]
        operands = [u, u, links, before]
    return pl.pallas_call(
        kernel,
        grid=(8 // STEP,),
        in_specs=in_specs,
        out_specs=out_specs,
        out_shape=out_shape,
        scratch_shapes=[
            pltpu.VMEM((6, 32, 128), F32),
            pltpu.VMEM((6, 32, 128), F32),
            pltpu.VMEM((6, 32, 128), F32),
            pltpu.VMEM((6, 128, 128), F32),
        ],
        compiler_params=params(12),
        cost_estimate=pl.CostEstimate(flops=12_000_000_000, bytes_accessed=12_000_000, transcendentals=0),
        name=name,
    )(*operands)


def boundary(partial, links, halo, z_links, c1, name):
    z_up, z_down, y_up, y_down = halo

    def kernel(part, link_ref, zu, zd, yu, yd, zl, out, y_low, y_high, z_low, z_high, turned):
        step = pl.program_id(0)

        def put(z, c, at, hop):
            spot = slice(c * 128 + at.start, c * 128 + at.stop)
            out[z, spot, :] = part[z, spot, :] - c1 * hop[c]

        def more(z, c, at, hop):
            spot = slice(c * 128 + at.start, c * 128 + at.stop)
            out[z, spot, :] = out[z, spot, :] - c1 * hop[c]

        for z in range(FACE):
            for g in range(4):
                own = slice(8 * g, 8 * g + 8)
                hop = backward(link_of(link_ref[z, own, :], 3), [yd[z, c, own, :] for c in range(6)])
                for c in range(6):
                    put(z, c, own, hop)
                at = slice(96 + 8 * g, 104 + 8 * g)
                hop = forward(link_of(link_ref[z, at, :], 1), [yu[z, c, own, :] for c in range(6)])
                for c in range(6):
                    put(z, c, at, hop)
            for c in range(6):
                spot = slice(c * 128 + 32, c * 128 + 96)
                out[z, spot, :] = part[z, spot, :]

        @pl.when(step == 0)
        def _():
            turned[...] = jnp.concatenate([zl[...], jnp.zeros((56, 128), F32)], axis=0).T
            for g in range(16):
                at = slice(8 * g, 8 * g + 8)
                hop = backward(link_of(turned[at, :], 2), [zd[c * 128 + at.start : c * 128 + at.stop, :] for c in range(6)])
                for c in range(6):
                    more(0, c, at, hop)
            z_low[...] = out[0]

        @pl.when(step == 8 // FACE - 1)
        def _():
            for g in range(16):
                at = slice(8 * g, 8 * g + 8)
                hop = forward(
                    link_of(link_ref[FACE - 1, at, :], 2), [zu[c * 128 + at.start : c * 128 + at.stop, :] for c in range(6)]
                )
                for c in range(6):
                    more(FACE - 1, c, at, hop)
            z_high[...] = out[FACE - 1]

        for z in range(FACE):
            for c in range(6):
                y_low[z, c] = out[z, c * 128 : c * 128 + 32, :]
                y_high[z, c] = out[z, c * 128 + 96 : c * 128 + 128, :]

    block = pl.BlockSpec((FACE, 768, 128), lambda z: (z, 0, 0))
    y_face = pl.BlockSpec((FACE, 6, 32, 128), lambda z: (z, 0, 0, 0))
    z_face = pl.BlockSpec((768, 128), lambda z: (0, 0))
    return pl.pallas_call(
        kernel,
        grid=(8 // FACE,),
        in_specs=[
            block,
            pl.BlockSpec((FACE, 128, 128), lambda z: (z, 0, 0)),
            z_face,
            z_face,
            y_face,
            y_face,
            pl.BlockSpec((72, 128), lambda z: (0, 0)),
        ],
        out_specs=(block, y_face, y_face, z_face, z_face),
        out_shape=(
            jax.ShapeDtypeStruct((8, 768, 128), F32),
            jax.ShapeDtypeStruct((8, 6, 32, 128), F32),
            jax.ShapeDtypeStruct((8, 6, 32, 128), F32),
            jax.ShapeDtypeStruct((768, 128), F32),
            jax.ShapeDtypeStruct((768, 128), F32),
        ),
        scratch_shapes=[pltpu.VMEM((128, 128), F32)],
        compiler_params=params(20),
        cost_estimate=pl.CostEstimate(flops=6_000_000_000, bytes_accessed=9_000_000, transcendentals=0),
        name=name,
    )(partial, links, z_up, z_down, y_up, y_down, z_links)


def halves(value):
    high = value.astype(BF16)
    return high, (value - high.astype(F32)).astype(BF16)


def dot3(left, right):
    def dot(a, b):
        return jnp.dot(a, b, preferred_element_type=F32)

    return dot(left[0], right[0]) + (dot(left[0], right[1]) + dot(left[1], right[0]))


def columns(ref, z, part):
    return jnp.concatenate([cell(ref, 3 * part + a, slice(0, 128), z) for a in range(3)], axis=1)


def gram(u, first_norm, second_norm):
    def kernel(here, n1, n2, packed, turned, acc):
        step = pl.program_id(0)

        @pl.when(step == 0)
        def _():
            acc[...] = jnp.zeros_like(acc)

        for z in range(GRAM):
            for c in range(6):
                turned[z, c * 128 : (c + 1) * 128, :] = cell(here, c, slice(0, 128), z).T
        left = jnp.concatenate(
            [jnp.concatenate([columns(turned, z, part) for z in range(GRAM)], axis=1) for part in range(2)], axis=0
        )
        right = jnp.concatenate([here[z, 0:384, :] for z in range(GRAM)], axis=0)
        right = jnp.concatenate([right, jnp.concatenate([here[z, 384:768, :] for z in range(GRAM)], axis=0)], axis=1)
        acc[...] = acc[...] + dot3(halves(left), halves(right))

        @pl.when(step == 8 // GRAM - 1)
        def _():
            real = acc[0:128, 0:128] + acc[128:256, 128:256]
            imag = acc[0:128, 128:256] - acc[128:256, 0:128]
            row = lax.broadcasted_iota(jnp.int32, (128, 128), 0)
            column = lax.broadcasted_iota(jnp.int32, (128, 128), 1)
            packed[0:128, :] = jnp.where(column >= row, real, imag)
            packed[128:136, :] = n1[...]
            packed[136:144, :] = n2[...]

    fixed = pl.BlockSpec((8, 128), lambda z: (0, 0))
    return pl.pallas_call(
        kernel,
        grid=(8 // GRAM,),
        in_specs=[pl.BlockSpec((GRAM, 768, 128), lambda z: (z, 0, 0)), fixed, fixed],
        out_specs=(pl.BlockSpec((144, 128), lambda z: (0, 0)), pl.BlockSpec((GRAM, 768, 128), lambda z: (z, 0, 0))),
        out_shape=(jax.ShapeDtypeStruct((144, 128), F32), jax.ShapeDtypeStruct((8, 768, 128), F32)),
        scratch_shapes=[pltpu.VMEM((256, 256), F32)],
        compiler_params=params(56),
        cost_estimate=pl.CostEstimate(flops=4_000_000_000, bytes_accessed=3_000_000, transcendentals=0),
        name="gram",
    )(u, first_norm, second_norm)


def put_halves(wide, zz, carry, slots):
    for a in range(3):
        for k in range(slots):
            for part in range(2):
                hi, lo = halves(carry[k, 3 * part + a])
                spot = (k * 2 + part) * 128
                wide[zz, a * 128 : (a + 1) * 128, spot : spot + 128] = hi
                wide[zz, 384 + a * 128 : 512 + a * 128, spot : spot + 128] = lo
                wide[zz, 768 + a * 128 : 896 + a * 128, spot : spot + 128] = hi


def add_hops(acc, turned, zz, carry, slots):
    left = jnp.concatenate([columns(turned, zz, part) for part in range(2)], axis=0)

    def summed(c):
        return carry[0, c] if slots == 1 else carry[0, c] + carry[1, c]

    right = jnp.concatenate(
        [jnp.concatenate([summed(a), summed(3 + a)], axis=1) for a in range(3)], axis=0
    )
    acc[...] = acc[...] + dot3(halves(left), halves(right))


def carry_x(u, turned, links):
    def kernel(here, turned, link_ref, wide, hops, px, carry, acc):
        z = pl.program_id(0)

        @pl.when(z == 0)
        def _():
            acc[...] = jnp.zeros_like(acc)

        for zz in range(CARRY_X):
            for y in range(4):
                row = y * 32
                for c in range(6):
                    px[c] = pltpu.roll(cell(here, c, slice(row, row + 32), zz), 31, 0)
                for g in range(4):
                    at = slice(row + 8 * g, row + 8 * g + 8)
                    own = slice(8 * g, 8 * g + 8)
                    found = forward(link_of(link_ref[zz, at, :], 0), [px[c, own, :] for c in range(6)])
                    for c in range(6):
                        carry[0, c, at, :] = found[c]
            put_halves(wide, zz, carry, 1)
            add_hops(acc, turned, zz, carry, 1)

        @pl.when(z == 8 // CARRY_X - 1)
        def _():
            hops[...] = acc[...]

    block = pl.BlockSpec((CARRY_X, 768, 128), lambda z: (z, 0, 0))
    return pl.pallas_call(
        kernel,
        grid=(8 // CARRY_X,),
        in_specs=[block, block, pl.BlockSpec((CARRY_X, 128, 128), lambda z: (z, 0, 0))],
        out_specs=(pl.BlockSpec((CARRY_X, 1152, 256), lambda z: (z, 0, 0)), pl.BlockSpec((256, 256), lambda z: (0, 0))),
        out_shape=(jax.ShapeDtypeStruct((8, 1152, 256), BF16), jax.ShapeDtypeStruct((256, 256), F32)),
        scratch_shapes=[
            pltpu.VMEM((6, 32, 128), F32),
            pltpu.VMEM((1, 6, 128, 128), F32),
            pltpu.VMEM((256, 256), F32),
        ],
        compiler_params=params(56),
        cost_estimate=pl.CostEstimate(flops=7_000_000_000, bytes_accessed=8_000_000, transcendentals=0),
        name="carry_x",
    )(u, turned, links)


def carry_yz(u, turned, links, z_up, y_up, x_hops, packed_gram):
    def kernel(here, turned, above, link_ref, zu, yu, hops_ref, gram_ref, wide, packed, carry, acc):
        z = pl.program_id(0)
        last = z == 8 // CARRY_YZ - 1

        @pl.when(z == 0)
        def _():
            acc[...] = hops_ref[...]

        for zz in range(CARRY_YZ):
            for y in range(4):
                row = y * 32
                for g in range(4):
                    at = slice(row + 8 * g, row + 8 * g + 8)
                    own = slice(8 * g, 8 * g + 8)
                    rows = link_ref[zz, at, :]
                    if y < 3:
                        source = [cell(here, c, slice(at.start + 32, at.stop + 32), zz) for c in range(6)]
                    else:
                        source = [yu[zz, c, own, :] for c in range(6)]
                    found = forward(link_of(rows, 1), source)
                    for c in range(6):
                        carry[0, c, at, :] = found[c]
                    if zz < CARRY_YZ - 1:
                        source = [cell(here, c, at, zz + 1) for c in range(6)]
                    else:
                        source = [jnp.where(last, cell_flat(zu, c, at), cell(above, c, at)) for c in range(6)]
                    found = forward(link_of(rows, 2), source)
                    for c in range(6):
                        carry[1, c, at, :] = found[c]
            put_halves(wide, zz, carry, 2)
            add_hops(acc, turned, zz, carry, 2)

        @pl.when(last)
        def _():
            gram_real, gram_imag = hermitian(gram_ref[0:128, :])
            hop_real = acc[0:128, 0:128] + acc[128:256, 128:256]
            hop_imag = acc[0:128, 128:256] - acc[128:256, 0:128]
            real = 6.0 * gram_real - (hop_real + hop_real.T)
            imag = 6.0 * gram_imag - (hop_imag - hop_imag.T)
            row = lax.broadcasted_iota(jnp.int32, (128, 128), 0)
            column = lax.broadcasted_iota(jnp.int32, (128, 128), 1)
            packed[...] = jnp.where(column >= row, real, imag)

    return pl.pallas_call(
        kernel,
        grid=(8 // CARRY_YZ,),
        in_specs=[
            pl.BlockSpec((CARRY_YZ, 768, 128), lambda z: (z, 0, 0)),
            pl.BlockSpec((CARRY_YZ, 768, 128), lambda z: (z, 0, 0)),
            pl.BlockSpec((1, 768, 128), lambda z: (jnp.minimum(CARRY_YZ * (z + 1), 7), 0, 0)),
            pl.BlockSpec((CARRY_YZ, 128, 128), lambda z: (z, 0, 0)),
            pl.BlockSpec((768, 128), lambda z: (0, 0)),
            pl.BlockSpec((CARRY_YZ, 6, 32, 128), lambda z: (z, 0, 0, 0)),
            pl.BlockSpec((256, 256), lambda z: (0, 0)),
            pl.BlockSpec((144, 128), lambda z: (0, 0)),
        ],
        out_specs=(pl.BlockSpec((CARRY_YZ, 1152, 512), lambda z: (z, 0, 0)), pl.BlockSpec((128, 128), lambda z: (0, 0))),
        out_shape=(jax.ShapeDtypeStruct((8, 1152, 512), BF16), jax.ShapeDtypeStruct((128, 128), F32)),
        scratch_shapes=[pltpu.VMEM((2, 6, 128, 128), F32), pltpu.VMEM((256, 256), F32)],
        compiler_params=params(56),
        cost_estimate=pl.CostEstimate(flops=12_000_000_000, bytes_accessed=16_000_000, transcendentals=0),
        name="carry_yz",
    )(u, turned, u, links, z_up, y_up, x_hops, packed_gram)


def elementals(core, z, turned_u, right_x, right_yz, phases, first, count, extra, spare, name):
    def kernel(core_ref, z_ref, here, rx, ryz, phase, *refs):
        kept, given, left, acc = refs[-4:]
        step = pl.program_id(0)
        own = core_ref[0] == 0

        @pl.when(step == 0)
        def _():
            acc[...] = jnp.zeros_like(acc)

        turned = [[here[zz, c * 128 : (c + 1) * 128, :] for c in range(6)] for zz in range(2)]
        minus = [[-turned[zz][a] for a in range(3)] for zz in range(2)]

        def build(m):
            mode = 2 * (first + m)
            for zz in range(2):
                cosine = phase[zz, mode : mode + 1, :]
                sine = phase[zz, mode + 1 : mode + 2, :]
                for a in range(3):
                    real, imag = turned[zz][a], turned[zz][3 + a]
                    spot = zz * 1152 + a * 128
                    pair = (real * cosine - imag * sine, minus[zz][a] * sine - imag * cosine)
                    for part in range(2):
                        hi, lo = halves(pair[part])
                        rows = slice(m * 256 + part * 128, m * 256 + part * 128 + 128)
                        left[rows, spot : spot + 128] = hi
                        left[rows, spot + 384 : spot + 512] = hi
                        left[rows, spot + 768 : spot + 896] = lo

        def multiply(low, high):
            done = slice(low * 256, high * 256)
            found = jnp.dot(left[done, :], rx[...].reshape(2304, 256), preferred_element_type=F32)
            acc[done, 0:256] = acc[done, 0:256] + found
            found = jnp.dot(left[done, :], ryz[...].reshape(2304, 512), preferred_element_type=F32)
            acc[done, 256:768] = acc[done, 256:768] + found

        for m in range(2):
            build(m)
        for m in range(2, count):
            build(m)
        for low in range(0, count, 2):
            multiply(low, min(low + 2, count))

        @pl.when(step == 3)
        def _():
            def share(lanes, value):
                for chip in range(16):
                    low, high = value[chip * 8 : chip * 8 + 4], value[chip * 8 + 4 : chip * 8 + 8]
                    kept[chip, :, lanes] = jnp.where(own, low, high)
                    given[chip, :, lanes] = jnp.where(own, high, low)

            width = spare * 128
            lanes = slice(count * 768, count * 768 + width)
            share(lanes, jnp.zeros((128, width), F32) if extra is None else refs[0][...])
            turn = halves(jnp.concatenate([z_ref[0].T, z_ref[1].T], axis=0))
            for m in range(count):
                real, imag = slice(m * 256, m * 256 + 128), slice(m * 256 + 128, m * 256 + 256)
                for k in range(3):
                    one, two = slice(256 * k, 256 * k + 128), slice(256 * k + 128, 256 * k + 256)
                    raw = [acc[real, one] - acc[imag, two], acc[real, two] + acc[imag, one]]
                    found = dot3(turn, halves(jnp.concatenate(raw, axis=1)))
                    place = (m * 3 + k) * 256
                    share(slice(place, place + 128), found[0:128, 0:128] + found[128:256, 128:256])
                    share(slice(place + 128, place + 256), found[0:128, 128:256] - found[128:256, 0:128])

    shape = (16, 4, count * 768 + spare * 128)
    return pl.pallas_call(
        kernel,
        grid=(4,),
        in_specs=[
            pl.BlockSpec(memory_space=pltpu.SMEM),
            pl.BlockSpec((2, 128, 128), lambda z: (0, 0, 0)),
            pl.BlockSpec((2, 768, 128), lambda z: (z, 0, 0)),
            pl.BlockSpec((2, 1152, 256), lambda z: (z, 0, 0)),
            pl.BlockSpec((2, 1152, 512), lambda z: (z, 0, 0)),
            pl.BlockSpec((2, 14, 128), lambda z: (z, 0, 0)),
        ]
        + [pl.BlockSpec((128, 128), lambda z: (0, 0))] * (extra is not None),
        out_specs=[pl.BlockSpec(shape, lambda z: (0, 0, 0))] * 2,
        out_shape=[jax.ShapeDtypeStruct(shape, F32)] * 2,
        scratch_shapes=[
            pltpu.VMEM((count * 256, 2304), BF16),
            pltpu.VMEM((count * 256, 768), F32),
        ],
        compiler_params=params(56),
        cost_estimate=pl.CostEstimate(flops=5_500_000_000 * count, bytes_accessed=16_000_000, transcendentals=0),
        name=name,
    )(core, z, turned_u, right_x, right_yz, phases, *([] if extra is None else [extra]))


def hermitian(packed):
    row = lax.broadcasted_iota(jnp.int32, (128, 128), 0)
    column = lax.broadcasted_iota(jnp.int32, (128, 128), 1)
    diagonal = jnp.where(column == row, packed, 0.0)
    upper = jnp.where(column > row, packed, 0.0)
    lower = jnp.where(column < row, packed, 0.0)
    return upper + upper.T + diagonal, lower - lower.T


def complex_dot(left, right):
    top = jnp.concatenate([left[0], -left[1]], axis=1)
    bottom = jnp.concatenate([left[1], left[0]], axis=1)
    both = dot3(halves(jnp.concatenate([top, bottom], axis=0)), halves(jnp.concatenate([right[0], right[1]], axis=0)))
    return both[0:128], both[128:256]


def newton(total):
    def kernel(ref, z_out):
        row = lax.broadcasted_iota(jnp.int32, (128, 128), 0)
        column = lax.broadcasted_iota(jnp.int32, (128, 128), 1)
        identity = jnp.where(row == column, 1.0, 0.0).astype(F32)
        g_real, g_imag = hermitian(ref[0:128, :])
        shrink = 1.0 / (RANGE * RANGE)
        n1 = jnp.sum(ref[128:136, :], axis=0, keepdims=True) * shrink / COUNT
        n2 = jnp.sum(ref[136:144, :], axis=0, keepdims=True) * shrink / COUNT
        n3 = jnp.sum(jnp.where(row == column, g_real, 0.0), axis=0, keepdims=True) * shrink / COUNT
        scale = lax.rsqrt(n1 + EPS)
        scale = scale * lax.rsqrt(scale * scale * n2 + EPS)
        scale = scale * lax.rsqrt(scale * scale * n3 + EPS)
        scale = jnp.broadcast_to(scale * (1.0 / RANGE), (128, 128))
        side = scale.T
        y = (side * g_real * scale / COUNT, side * g_imag * scale / COUNT)
        inverse = None
        for step in range(3):
            middle = y if inverse is None else complex_dot(inverse, y)
            factor = (1.5 * identity - 0.5 * middle[0], -0.5 * middle[1])
            if step < 2:
                y = complex_dot(y, factor)
            inverse = factor if inverse is None else complex_dot(factor, inverse)
        z_out[0] = side * inverse[0]
        z_out[1] = side * inverse[1]

    return pl.pallas_call(
        kernel,
        out_shape=jax.ShapeDtypeStruct((2, 128, 128), F32),
        compiler_params=params(12),
        cost_estimate=pl.CostEstimate(flops=5_000_000_000, bytes_accessed=300_000, transcendentals=0),
        name="newton",
    )(total)


def rayleigh(total, z):
    def kernel(ref, z_ref, out):
        h = hermitian(ref[...])
        inverse = (z_ref[0], z_ref[1])
        half = complex_dot(h, inverse)
        full = complex_dot((inverse[0].T, -inverse[1].T), half)
        out[0] = full[0] / COUNT
        out[1] = full[1] / COUNT

    return pl.pallas_call(
        kernel,
        out_shape=jax.ShapeDtypeStruct((2, 128, 128), F32),
        compiler_params=params(12),
        cost_estimate=pl.CostEstimate(flops=3_000_000_000, bytes_accessed=300_000, transcendentals=0),
        name="rayleigh",
    )(total, z)


def rotate(z, blocks):
    def kernel(z_ref, ref, out):
        top = jnp.concatenate([z_ref[0], z_ref[1]], axis=1)
        bottom = jnp.concatenate([-z_ref[1], z_ref[0]], axis=1)
        right = halves(jnp.concatenate([top, bottom], axis=0))
        for a in range(3):
            real, imag = slice(a * 128, a * 128 + 128), slice(384 + a * 128, 512 + a * 128)
            left = jnp.concatenate(
                [jnp.concatenate([ref[q, real, :], ref[q, imag, :]], axis=1) for q in range(TURN)], axis=0
            )
            found = dot3(halves(left), right)
            out[a] = found[:, 0:128]
            out[3 + a] = found[:, 128:256]

    return pl.pallas_call(
        kernel,
        grid=(8 // TURN,),
        in_specs=[
            pl.BlockSpec((2, 128, 128), lambda i: (0, 0, 0)),
            pl.BlockSpec((TURN, 768, 128), lambda i: (i, 0, 0)),
        ],
        out_specs=pl.BlockSpec((6, 128 * TURN, 128), lambda i: (0, i, 0)),
        out_shape=jax.ShapeDtypeStruct((6, 1024, 128), F32),
        compiler_params=params(24),
        cost_estimate=pl.CostEstimate(flops=5_000_000_000, bytes_accessed=7_000_000, transcendentals=0),
        name="rotate",
    )(z, blocks)


def ring_pairs(step):
    return [(z * 8 + r, z * 8 + (r + step) % 8) for z in range(4) for r in range(8)]


def z_pairs(step):
    return [(i, (i + 8 * step) % 32) for i in range(32)]


def y_pairs(step):
    return ring_pairs(2 * step)


RINGS = [[z * 8 + r for r in range(8)] for z in range(4)]
CORES = [[2 * chip + core for chip in range(16)] for core in range(2)]
CORE_PAIRS = [(i, i ^ 1) for i in range(32)]


def move(value, pairs):
    return lax.ppermute(value, "sa", pairs)


def trade(value, groups=None):
    return lax.all_to_all(value, "sa", 0, 0, axis_index_groups=groups, tiled=True)


def spread(value, pairs):
    return [move(value, pairs(step)) for step in (2, 1, -1)]


def gathered(value, parts):
    return (value + parts[0]) + (parts[1] + parts[2])


def local(start, links, momenta, displace):
    device = lax.axis_index("sa")
    ring = device % 8

    u = trade(lay_out(start.reshape(6, 1024, 128), links.reshape(54, 32, 32)), RINGS)

    zs = (device // 8) * 8 + jnp.arange(8, dtype=jnp.int32)[None, :, None, None]
    ys = ring * 4 + jnp.arange(4, dtype=jnp.int32)[None, None, :, None]
    xs = jnp.arange(32, dtype=jnp.int32)[None, None, None, :]
    along_x = momenta[:, 0][:, None, None, None]
    along_y = momenta[:, 1][:, None, None, None]
    along_z = momenta[:, 2][:, None, None, None]
    angles = TWO_PI * (
        (along_x * xs % 32).astype(F32) / 32
        + (along_y * ys % 32).astype(F32) / 32
        + (along_z * zs % 32).astype(F32) / 32
    )
    angles = angles.reshape(NMOM, 8, 128)
    phases = jnp.stack([jnp.cos(angles), jnp.sin(angles)], axis=1).reshape(2 * NMOM, 8, 128)
    phases = jnp.transpose(phases, (1, 0, 2))

    cells = u[:, 0:768].reshape(8, 6, 128, 128)
    z_low, z_high = u[0, 0:768], u[7]
    y_low, y_high = cells[:, :, 0:32], cells[:, :, 96:128]
    before = mesh_links = z_links = None
    norms = []
    for step in range(3):
        weight = (1.0 if step else RANGE) * (2.0 if step else 1.0)
        z_down = move(z_high, z_pairs(1))
        z_up = move(z_low, z_pairs(-1))
        y_down = move(y_high, ring_pairs(1))
        y_up = move(y_low, ring_pairs(-1))
        if step == 0:
            z_links = z_down[768:840]
        found = interior(
            u,
            mesh_links,
            before,
            weight * (6.0 * ALPHA - BETA),
            weight * ALPHA,
            RANGE if step == 1 else 1.0,
            f"interior_{step}",
        )
        if step == 0:
            mesh_links = found[2]
        norms.append(found[1])
        fresh, y_low, y_high, z_low, z_high = boundary(
            found[0], mesh_links, (z_up, z_down, y_up, y_down), z_links, weight * ALPHA, f"boundary_{step}"
        )
        before, u = u, fresh

    z_up = move(z_low, z_pairs(-1))
    y_up = move(y_low, ring_pairs(-1))
    packed_gram, turned = gram(u, norms[1], norms[2])
    shared = packed_gram + move(packed_gram, CORE_PAIRS)
    ring_parts = spread(shared, y_pairs)
    right_x, x_hops = carry_x(u, turned, mesh_links)
    ring_parts, x_hops, z_up, y_up, u = lax.optimization_barrier((ring_parts, x_hops, z_up, y_up, u))
    back = trade(u, RINGS)
    shared = gathered(shared, ring_parts)
    z_parts = spread(shared, z_pairs)
    right_yz, packed_h = carry_yz(u, turned, mesh_links, z_up, y_up, x_hops, packed_gram)
    z_parts, packed_h = lax.optimization_barrier((z_parts, packed_h))
    total_gram = gathered(shared, z_parts)
    z = newton(total_gram)
    core = device % 2
    where = core.reshape(1).astype(jnp.int32)
    kept, given = elementals(where, z, turned, right_x, right_yz, phases, 0, 4, packed_h, 1, "elementals_0")
    first = kept + move(given, CORE_PAIRS)
    first, back, turned = lax.optimization_barrier((first, back, turned))
    first = jnp.sum(trade(first, CORES), axis=0)
    kept, given = elementals(where, z, turned, right_x, right_yz, phases, 4, 3, None, 2, "elementals_1")
    first, kept, given = lax.optimization_barrier((first, kept, given))
    share = jnp.broadcast_to(first[:, 3072:], (16, 4, 128))
    given = lax.dynamic_update_slice(given, share, (0, 0, 2432))
    second = lax.dynamic_update_slice(kept, share, (0, 0, 2304)) + move(given, CORE_PAIRS)
    second, back = lax.optimization_barrier((second, back))
    second = trade(second, CORES)
    mine, others = second[:, :, 2304:2432], second[:, :, 2432:]
    low, high = jnp.where(core == 0, mine, others), jnp.where(core == 0, others, mine)
    total = jnp.stack([low, high], axis=1).reshape(128, 128)
    sums = [first[:, :3072], jnp.sum(second[:, :, :2304], axis=0)]
    ritz = rayleigh(total, z)
    basis = rotate(z, back).reshape(start.shape)

    rows = jnp.concatenate([part.reshape(4, -1, 2, 128) for part in sums], axis=1)
    real, imag = rows[:, :, 0].reshape(-1, 128), rows[:, :, 1].reshape(-1, 128)
    left = jnp.concatenate([real, imag], axis=1)
    top = jnp.concatenate([z[0], z[1]], axis=1)
    bottom = jnp.concatenate([-z[1], z[0]], axis=1)
    phi = jnp.dot(left, jnp.concatenate([top, bottom], axis=0), precision=HIGHEST)
    phi = (phi * (1.0 / math.sqrt(32768.0))).reshape(4, NMOM, 3, 2, 128)
    slots = displace[:, None] == jnp.arange(3, dtype=displace.dtype)[None, :]
    phi = jnp.sum(jnp.where(slots[None, None, :, :, None, None], phi[:, :, None], 0.0), axis=3)
    return (basis, ritz, phi)


def solution(mesh):
    in_specs = (
        P("ta", None, "sa", None, None, None),
        P("ta", None, None, None, "sa", None, None),
        P(),
        P(),
    )
    out_specs = (
        P("ta", None, "sa", None, None, None),
        P("ta", None, None),
        P("sa", "ta", None, None, None),
    )
    return jax.shard_map(local, mesh=mesh, in_specs=in_specs, out_specs=out_specs, check_vma=False)
```
